256 devices in a mesh: prefix: 16 (over z, core), branch: 16 (over y, x).
Axes of the slice: x: 4, y: 4, z: 8, core: 2. Of those that a mesh axis runs over, the one named last changes fastest.
Arguments:
- token_ids: int32 [4, 768], P(None, 'prefix'), may hold values from 0 to 127999
- prompt_of: int32 [768, 1], P('prefix'), may hold values from 0 to 31; in each aligned block of 48 rows (0 to 47, 48 to 95, ...) at most 6 rows name the same one
- suffix_len: int32 [768], P('prefix'), may hold values from 1 to 8, 3072 in all
- table: bfloat16 [128000, 4608], P('prefix', 'branch'), may hold values from -12 to 12
- pre_gain: float32 [4608], replicated, may hold values from 0.1 to 1.9
- w_query: bfloat16 [4608, 4096], P(None, 'branch'), may hold values from -0.09375 to 0.09375
- w_keyval: bfloat16 [2, 4608, 2048], P(None, None, 'branch'), may hold values from -0.09375 to 0.09375
- w_out: bfloat16 [4096, 4608], P('branch'), may hold values from -2.5 to 2.5
- post_gain: float32 [4608], P('branch'), may hold values from 0.1 to 1.9
- prefix_keys: bfloat16 [32, 1024, 2048], P('prefix', None, 'branch'), may hold values from -6 to 6
- prefix_values: bfloat16 [32, 1024, 2048], P('prefix', None, 'branch'), may hold values from -4 to 4
- suffix_keys: bfloat16 [768, 8, 2048], P('prefix', None, 'branch'), may hold values from -6 to 6
- suffix_values: bfloat16 [768, 8, 2048], P('prefix', None, 'branch'), may hold values from -6 to 6
Outputs:
- layer_out: bfloat16 [4, 768, 4608], P(None, 'prefix', 'branch')
The draws below stay inside these ranges and needn't reach their ends.
Inputs may be any that keep to these rules, and one draw needn't show every extreme that they name: `prompt_of`: at most 6 of the rows of one index of prefix name the same prompt; in every draw some index reaches 6 for some prompt, and every prompt is named by some row. `suffix_len`: some row fills all 8 slots.
All inputs are finite; a program needn't handle non-finite values. No bound on the sum of `suffix_len` on one device may be relied on, other than what follows from the above.
Results may differ from the reference program's by a relative error of at most 0.017.
Values may be sent and summed in bfloat16 or wider, within the bound.
No kernel may reach another device: no remote copies, remote signals or barrier semaphores. Data moves between devices by JAX's collectives and lax.ppermute only.
A program may use at most 64 MiB of HBM per device.

```python
import math
import jax
import jax.numpy as jnp
import numpy as np
from jax import lax

D = 4608
HEADS = 32
KV_HEADS = 16
HEAD = 128
VOCAB = 128000
STEPS = 4
ROWS_DEV = 48
LPRE = 1024
SUF = 8
MOST = 6
PROMPTS = 32
ROWS = 768


def draw_table(key, part):
    key = jax.random.fold_in(key, 11)
    base_key, scale_key = jax.random.split(key)
    base = jnp.clip(jax.random.normal(base_key, (VOCAB, D), jnp.float32), -4.0, 4.0)
    spread = jax.random.uniform(scale_key, (VOCAB, 1), jnp.float32, math.log(0.3), math.log(3.0))
    return (base * jnp.exp(spread)).astype(jnp.bfloat16)


def draw_w_out(key, part):
    key = jax.random.fold_in(key, 12)
    base_key, rough_key = jax.random.split(key)
    column_place = jnp.arange(D, dtype=jnp.float32)[None, :] / D
    base = jnp.clip(jax.random.normal(base_key, (HEADS * HEAD, D), jnp.float32), -4.0, 4.0)
    trend = jnp.exp(column_place * math.log(3.0))
    rough = jnp.exp(jax.random.uniform(rough_key, (1, D), jnp.float32, 0.0, math.log(10.0)))
    value = jnp.clip(base * rough * trend / math.sqrt(HEADS * HEAD), -2.5, 2.5)
    return value.astype(jnp.bfloat16)


def plant(entries, stream_key, low, largest):
    index_at = [jax.random.randint(jax.random.fold_in(stream_key, axis), (), 0, length) for axis, length in enumerate(entries.shape)]
    longest = entries.shape.index(max(entries.shape))
    neighbour = index_at[:longest] + [(index_at[longest] + 1) % entries.shape[longest]] + index_at[longest + 1:]
    return entries.at[tuple(index_at)].set(low).at[tuple(neighbour)].set(largest)


def steps_of(key, extent, pieces, low, high):
    factor_of = 1.0
    for axis_at, blocks in pieces:
        steps = jax.random.uniform(jax.random.fold_in(jax.random.fold_in(key, 6), axis_at), (blocks,), jnp.float32, low / len(pieces), high / len(pieces))
        factor_of = factor_of * jnp.repeat(jnp.exp(steps), extent[axis_at] // blocks).reshape((-1,) + (1,) * (len(extent) - 1 - axis_at))
    return factor_of


def skewed_wide(stream_key, extent, amount, skew):
    loads = [min(1 << octave, amount + 1 - (1 << octave)) * (1 << 20) // math.isqrt((1 << octave) ** skew) + 1 for octave in range((amount + 1).bit_length()) if 1 << octave <= amount]
    width = 1 + sum(loads) // (1 << 30)
    grid = np.cumsum(np.array([max(1, weight // width) for weight in loads]))
    pick = jax.random.randint(jax.random.fold_in(stream_key, 1), extent, 0, int(grid[len(loads) - 1]))
    start = jnp.left_shift(1, jnp.searchsorted(jnp.asarray(grid, jnp.int32), pick, side="right").astype(jnp.int32))
    rank = start - 1 + jax.random.randint(jax.random.fold_in(stream_key, 4), extent, 0, 1 << 30) % jnp.minimum(start, amount + 1 - start)
    return jax.random.permutation(jax.random.fold_in(stream_key, 2), amount)[rank].astype(jnp.int32)


def profile(number_of, total, most, slope):
    portions = [(1 << 20) // math.isqrt(standing ** slope) + 1 for standing in range(2, number_of + 1)]
    rest, counts = total - most - (number_of - 1), [1] * (number_of - 1)
    while rest > 0:
        movable = [i for i in range(number_of - 1) if counts[i] < most]
        mass, remaining = sum([portions[i] for i in movable]), rest
        for i in movable:
            more = min(most - counts[i], max(1, remaining * portions[i] // mass), rest)
            counts[i] = counts[i] + more
            rest = rest - more
    return np.array([most] + counts)


def ragged(own_key, count, total, bound, slope):
    if count == 2:
        one = jax.random.randint(own_key, (), max(1, total - bound), min(bound, total - 1) + 1)
        return jnp.stack([one, total - one])
    tallies = jnp.asarray(profile(count, total, bound, slope), jnp.int32)
    pairs = (count - 1) // 2
    source_of, taker = tallies[1:1 + 2 * pairs:2], tallies[2:2 + 2 * pairs:2]
    margin = jnp.minimum(source_of - 1, bound - taker)
    moved = jax.random.randint(jax.random.fold_in(own_key, 1), (pairs,), 0, 1 << 20) % (margin + 1)
    tallies = tallies.at[1:1 + 2 * pairs:2].set(source_of - moved).at[2:2 + 2 * pairs:2].set(taker + moved)
    return tallies[jax.random.permutation(jax.random.fold_in(own_key, 2), count)]


def routed_block(own_key, own, number, rows, number_of, top, limit, skew):
    sequence = jax.random.permutation(own_key, number_of)
    crowded, usual = shares(number_of, rows * top, limit, skew, True), shares(number_of, rows * top, limit, skew, False)
    places = jnp.arange(number_of)

    def named(tallies, rotation):
        used = int((tallies > 0).sum())
        fixed = max(1, used // 4)
        shifted = fixed + (places - fixed + rotation * (used - fixed)) % max(1, number_of - fixed)
        return jnp.zeros((number_of,), jnp.int32).at[sequence[jnp.where(places < fixed, places, shifted)]].set(jnp.asarray(tallies, jnp.int32))

    tallies = jnp.where(number % 4 == 0, named(crowded, number // 4), named(usual, number - number // 4 - 1))
    mixed = jax.random.permutation(jax.random.fold_in(own, 3), number_of)
    giver, receiver = mixed[0:number_of // 2 * 2:2], mixed[1:number_of // 2 * 2:2]
    slack = jnp.minimum(tallies[giver] - 1, limit - tallies[receiver]) // 2
    slack = jnp.where((giver == sequence[0]) | (receiver == sequence[0]) | (tallies[receiver] == 0), 0, jnp.maximum(slack, 0))
    shifted = jax.random.randint(jax.random.fold_in(own, 4), (number_of // 2,), 0, 1 << 20) % (slack + 1)
    tallies = tallies.at[giver].add(-shifted).at[receiver].add(shifted)
    members = jnp.searchsorted(jnp.cumsum(tallies), jnp.arange(rows * top), side="right").astype(jnp.int32)
    listing = members.reshape(top, rows).T
    listing = listing[jax.random.permutation(jax.random.fold_in(own, 1), rows)]
    rotation = jax.random.randint(jax.random.fold_in(own, 2), (rows, 1), 0, top)
    return jnp.take_along_axis(listing, (jnp.arange(top)[None, :] + rotation) % top, axis=1)


def shares(number_of, total, reach, skew, full):
    portions = [(1 << 20) // math.isqrt(standing ** skew) + 1 for standing in range(1, number_of + 1)]
    largest = reach if full else min(reach, max(-(-total // number_of), total * portions[0] // sum(portions)))
    least = 1 if total - largest >= number_of - 1 else 0
    counts, spare = [largest] + [least] * (number_of - 1), total - largest - least * (number_of - 1)
    while spare > 0:
        free = [i for i in range(1, number_of) if counts[i] < largest] or [i for i in range(1, number_of) if counts[i] < reach]
        pool, left = sum([portions[i] for i in free]), spare
        for i in free:
            more = min(reach - counts[i], max(1, left * portions[i] // pool), spare)
            counts[i] = counts[i] + more
            spare = spare - more
    return np.array(counts)


def noise(key, shape, deviation, reach, cuts=(), kind=jnp.bfloat16):
    factor_of = steps_of(key, shape, cuts, -0.22, 0.18) if cuts else 1.0
    entries = jax.random.normal(key, shape, jnp.float32) * deviation * factor_of
    return jnp.minimum(jnp.maximum(entries, -reach), reach).astype(kind)


def setup_inputs(seed: int = 0) -> dict:
    seeds = jax.random.split(jax.random.key(seed), 14)
    token_ids = plant(skewed_wide(seeds[0], (STEPS, ROWS), VOCAB, 2), jax.random.fold_in(seeds[0], 3), 0, VOCAB - 1).astype(jnp.int32)
    prompt_of_keys = jax.random.split(jax.random.fold_in(seeds[1], 1), ROWS // ROWS_DEV)
    prompt_of_turns = jax.random.permutation(jax.random.fold_in(seeds[1], 3), ROWS // ROWS_DEV)
    prompt_of = jax.vmap(lambda own, number: routed_block(jax.random.fold_in(seeds[1], 2), own, number, ROWS_DEV, PROMPTS, 1, MOST, 2))(prompt_of_keys, prompt_of_turns).reshape((ROWS, 1))
    suffix_len = ragged(seeds[2], ROWS, ROWS * SUF // 2, SUF, 2).astype(jnp.int32)
    table = draw_table(jax.random.fold_in(seeds[13], 71), 0)
    pre_gain = jnp.clip(1.0 + 0.18 * jax.random.normal(seeds[4], (D,), jnp.float32), 0.1, 1.9)
    w_query = noise(seeds[5], (D, HEADS * HEAD), D ** -0.5, 0.09375, ((1, 16),))
    w_keyval = noise(seeds[6], (2, D, KV_HEADS * HEAD), D ** -0.5, 0.09375, ((2, 16),))
    w_out = draw_w_out(jax.random.fold_in(seeds[13], 71), 0)
    post_gain = jnp.clip(1.0 + 0.18 * jax.random.normal(seeds[8], (D,), jnp.float32), 0.1, 1.9)
    prefix_keys = noise(seeds[9], (PROMPTS, LPRE, KV_HEADS * HEAD), 1.0, 6.0, ((0, 16), (2, 16)))
    prefix_values = noise(seeds[10], (PROMPTS, LPRE, KV_HEADS * HEAD), 0.25, 4.0, ((0, 16), (2, 16)))
    suffix_keys = noise(seeds[11], (ROWS, SUF, KV_HEADS * HEAD), 1.0, 6.0, ((0, 16), (2, 16)))
    suffix_values = noise(seeds[12], (ROWS, SUF, KV_HEADS * HEAD), 1.0, 6.0, ((0, 16), (2, 16)))
    return {"token_ids": token_ids, "prompt_of": prompt_of, "suffix_len": suffix_len, "table": table, "pre_gain": pre_gain, "w_query": w_query, "w_keyval": w_keyval, "w_out": w_out, "post_gain": post_gain, "prefix_keys": prefix_keys, "prefix_values": prefix_values, "suffix_keys": suffix_keys, "suffix_values": suffix_values}


SOFT_CAP = 50.0
EPSILON = 1e-06

def rotary(values, positions):
    half_size = values.shape[-1] // 2
    frequency = 10000.0 ** (-(jnp.arange(half_size, dtype=jnp.float32) * 2.0 / values.shape[-1]))
    angles = positions[..., None] * frequency
    cosines = jnp.cos(angles)
    sines = jnp.sin(angles)
    lower_half = values[..., :half_size]
    upper_half = values[..., half_size:]
    return jnp.concatenate([lower_half * cosines - upper_half * sines, upper_half * cosines + lower_half * sines], axis=-1)

def capped_exp(scores):
    return jnp.exp(SOFT_CAP * jnp.tanh(scores / SOFT_CAP))

def reference(token_ids, prompt_of, suffix_len, table, pre_gain, w_query, w_keyval, w_out, post_gain, prefix_keys, prefix_values, suffix_keys, suffix_values):
    group = HEADS // KV_HEADS
    score_scale = float(D // HEADS) ** (-0.5)
    embedded = jnp.take(table, token_ids, axis=0)
    wide = embedded.astype(jnp.float32)
    normed = (wide * lax.rsqrt(lax.optimization_barrier(jnp.mean(wide * wide, axis=-1, keepdims=True)) + EPSILON) * pre_gain).astype(jnp.bfloat16)
    flat = normed.reshape(STEPS * ROWS, D)
    positions = (LPRE + suffix_len[None, :] + jnp.arange(STEPS)[:, None]).astype(jnp.float32)[..., None]
    queries = rotary(jnp.dot(flat, w_query, preferred_element_type=jnp.float32).reshape(STEPS, ROWS, HEADS, HEAD), positions).astype(jnp.bfloat16)
    new_keys = rotary(jnp.dot(flat, w_keyval[0], preferred_element_type=jnp.float32).reshape(STEPS, ROWS, KV_HEADS, HEAD), positions).astype(jnp.bfloat16)
    new_values = jnp.dot(flat, w_keyval[1], preferred_element_type=jnp.float32).reshape(STEPS, ROWS, KV_HEADS, HEAD).astype(jnp.bfloat16)
    blocks = ROWS // 4
    query_blocks = queries.transpose(1, 0, 2, 3).reshape(blocks, 4, STEPS, KV_HEADS, group, HEAD)
    key_blocks = new_keys.transpose(1, 0, 2, 3).reshape(blocks, 4, STEPS, KV_HEADS, HEAD)
    value_blocks = new_values.transpose(1, 0, 2, 3).reshape(blocks, 4, STEPS, KV_HEADS, HEAD)
    prompt_blocks = prompt_of[:, 0].reshape(blocks, 4)
    length_blocks = suffix_len.reshape(blocks, 4)
    suffix_key_blocks = suffix_keys.reshape(blocks, 4, SUF, KV_HEADS, HEAD)
    suffix_value_blocks = suffix_values.reshape(blocks, 4, SUF, KV_HEADS, HEAD)

    def row_block(block_items):
        query_rows, key_rows, value_rows, prompt_rows, length_rows, suffix_key_rows, suffix_value_rows = block_items
        cache_keys = jnp.take(prefix_keys, prompt_rows, axis=0).reshape(4, LPRE, KV_HEADS, HEAD).astype(jnp.float32)
        cache_values = jnp.take(prefix_values, prompt_rows, axis=0).reshape(4, LPRE, KV_HEADS, HEAD).astype(jnp.float32)
        query_wide = query_rows.astype(jnp.float32)
        prefix_low = capped_exp(jnp.einsum('rtcge,rkce->rtcgk', query_wide, cache_keys) * score_scale).astype(jnp.bfloat16)
        prefix_weights = lax.optimization_barrier(prefix_low).astype(jnp.float32)
        prefix_numer = jnp.einsum('rtcgk,rkce->rtcge', prefix_weights, cache_values)
        prefix_denom = lax.optimization_barrier(jnp.sum(prefix_weights, axis=-1))
        local_keys = jnp.concatenate([suffix_key_rows.astype(jnp.float32), key_rows.astype(jnp.float32)], axis=1)
        local_values = jnp.concatenate([suffix_value_rows.astype(jnp.float32), value_rows.astype(jnp.float32)], axis=1)
        slot_ids = jnp.arange(SUF + STEPS)[None, None, :]
        step_ids = jnp.arange(STEPS)[None, :, None]
        usable = jnp.where(slot_ids < SUF, slot_ids < length_rows[:, None, None], slot_ids - SUF <= step_ids)
        local_scores = jnp.einsum('rtcge,rjce->rtcgj', query_wide, local_keys) * score_scale
        local_low = jnp.where(usable[:, :, None, None, :], capped_exp(local_scores), 0.0).astype(jnp.bfloat16)
        local_weights = lax.optimization_barrier(local_low).astype(jnp.float32)
        local_numer = jnp.einsum('rtcgj,rjce->rtcge', local_weights, local_values)
        local_denom = lax.optimization_barrier(jnp.sum(local_weights, axis=-1))
        return ((prefix_numer + local_numer) / (prefix_denom + local_denom)[..., None]).astype(jnp.bfloat16)
    attended = lax.map(row_block, (query_blocks, key_blocks, value_blocks, prompt_blocks, length_blocks, suffix_key_blocks, suffix_value_blocks))
    attended = attended.reshape(ROWS, STEPS, HEADS * HEAD).transpose(1, 0, 2).reshape(STEPS * ROWS, HEADS * HEAD)
    projected = jnp.dot(attended, w_out, preferred_element_type=jnp.float32)
    scaled = projected * lax.rsqrt(lax.optimization_barrier(jnp.mean(projected * projected, axis=-1, keepdims=True)) + EPSILON) * post_gain
    layer_out = (wide.reshape(STEPS * ROWS, D) + scaled).astype(jnp.bfloat16)
    return layer_out.reshape(STEPS, ROWS, D)
```

```python
import functools

import jax
import jax.numpy as jnp
from jax import lax
from jax.experimental import pallas as pl
from jax.experimental.pallas import tpu as pltpu
from jax.sharding import PartitionSpec as P

D = 4608
HEADS = 32
KV_HEADS = 16
HEAD = 128
SUF = 8
SOFT_CAP = 50.0
EPSILON = 1e-06
SCALE = float(D // HEADS) ** (-0.5)

RING = 16
STEPS = 4
ROWS = 48
TOKENS = STEPS * ROWS
SHARE = D // RING
TAIL = SHARE - 2 * HEAD
PACKED = 2 * TOKENS + ROWS
TAKE = 24
ROOM = 32
ENDS = ROOM + 16
SLOT = 8
GROUP = HEADS // KV_HEADS
PAIRS = STEPS * GROUP
WIDE = PAIRS * HEAD
BACK = WIDE + HEAD

F32 = jnp.float32
BF16 = jnp.bfloat16
VMEM = pl.BlockSpec(memory_space=pltpu.VMEM)
ANY = pl.BlockSpec(memory_space=pl.ANY)


def call(kernel, out_shape, args, flops=0, left=(), scratch=(), limit=24):
    nbytes = sum(a.size * a.dtype.itemsize for a in args)
    many = isinstance(out_shape, (list, tuple))
    return pl.pallas_call(
        kernel,
        out_shape=out_shape,
        in_specs=[ANY if n in left else VMEM for n in range(len(args))],
        out_specs=[VMEM] * len(out_shape) if many else VMEM,
        scratch_shapes=list(scratch),
        compiler_params=pltpu.CompilerParams(vmem_limit_bytes=limit * 1024 * 1024),
        cost_estimate=pl.CostEstimate(flops=flops, bytes_accessed=nbytes, transcendentals=0),
    )(*args)


def dot(a, b, contract=((1,), (0,))):
    return lax.dot_general(a, b, (contract, ((), ())), preferred_element_type=F32)


def iota(shape, axis):
    return lax.broadcasted_iota(jnp.int32, shape, axis)


def capped_exp(scores):
    return jnp.exp(SOFT_CAP * jnp.tanh(scores * (SCALE / SOFT_CAP)))


def lane_group(shape):
    return lax.shift_right_logical(iota(shape, 1), 5)


def column_of(row):
    n = row.shape[1]
    diagonal = iota((n, n), 0) == iota((n, n), 1)
    return jnp.sum(jnp.where(diagonal, row, 0), axis=1, keepdims=True)


def ask_kernel(vocab, ids_ref, prompt_ref, notes_ref, at_ref, columns_ref, lines_ref):
    def owner_of(ids):
        total = jnp.zeros(ids.shape, jnp.int32)
        for d in range(1, RING):
            total = total + (ids >= d * vocab).astype(jnp.int32)
        return total

    rows = [ids_ref[t : t + 1, :] for t in range(STEPS)]
    column = jnp.concatenate([column_of(row) for row in rows], axis=0)
    owner = owner_of(column)
    base = owner * vocab
    down = iota((TOKENS, ROWS), 0)
    over = iota((TOKENS, ROWS), 1)
    rank = jnp.zeros((TOKENS, ROWS), jnp.int32)
    new_rows = []
    for t in range(STEPS):
        seen = (column == rows[t]) & (down < over + t * ROWS)
        new = 1 - jnp.max(seen.astype(jnp.int32), axis=0, keepdims=True)
        new_rows.append(new)
        rank = rank + jnp.where((rows[t] >= base) & (rows[t] < column), new, 0)
    rank = jnp.sum(rank, axis=1, keepdims=True)
    fits = rank < TAKE
    at_ref[...] = jnp.where(fits, owner * TAKE + rank, -1)
    value = column - base + 1
    cell = jnp.where(fits, rank, -1) == iota((TOKENS, HEAD), 1)
    coarse = jnp.where(cell, lax.shift_right_logical(value, 6), 0).astype(F32).astype(BF16)
    fine = jnp.where(cell, value & 63, 0).astype(F32).astype(BF16)
    holders = iota((RING, ROWS), 0)
    high = jnp.zeros((RING, HEAD), F32)
    low = jnp.zeros((RING, HEAD), F32)
    for t in range(STEPS):
        part = slice(t * ROWS, (t + 1) * ROWS)
        mine = jnp.where(owner_of(rows[t]) == holders, new_rows[t], 0).astype(F32).astype(BF16)
        high = high + dot(mine, coarse[part])
        low = low + dot(mine, fine[part])
    asked = high.astype(jnp.int32) * 64 + low.astype(jnp.int32) - 1

    prompt = prompt_ref[...]
    prompt_column = column_of(prompt)
    holder = lax.shift_right_logical(prompt, 1)
    holder_column = lax.shift_right_logical(prompt_column, 1)
    down = iota((ROWS, ROWS), 0)
    over = iota((ROWS, ROWS), 1)
    same = holder == holder_column
    turn = jnp.sum((same & (down < over)).astype(jnp.int32), axis=0, keepdims=True)
    turn_column = jnp.sum((same & (over < down)).astype(jnp.int32), axis=1, keepdims=True)
    mine = (holder == holders).astype(F32).astype(BF16)
    odd = jnp.where(turn_column + ROOM == iota((ROWS, HEAD), 1), prompt_column & 1, 0)
    odds = dot(mine, odd.astype(F32).astype(BF16)).astype(jnp.int32)
    lane = iota((RING, HEAD), 1)
    notes = jnp.where(lane < ROOM, asked, odds)
    most = jnp.max(rank, axis=0, keepdims=True) + 1
    notes = jnp.where(lane == ENDS, most, notes)
    most = jnp.max(turn_column, axis=0, keepdims=True) + 1
    notes_ref[...] = jnp.where(lane == ENDS + 1, most, notes)

    def slots(holder, turn):
        now = jnp.where(turn < SLOT, holder * SLOT + turn, -1)
        later = jnp.where(turn >= SLOT, holder * SLOT + turn - SLOT, -1)
        return now, later

    columns_ref[...] = jnp.concatenate(slots(holder_column, turn_column), axis=1)
    lines_ref[...] = jnp.concatenate(slots(holder, turn), axis=0)


PIECE = 1024


def pick_kernel(notes_ref, rest_ref, table_ref, out_ref, held_ref, done):
    whole = held_ref.shape[1]
    copies = []
    for start in range(0, whole, PIECE):
        part = pl.ds(start, min(PIECE, whole - start))
        copy = pltpu.make_async_copy(
            table_ref.at[:, part], held_ref.at[:, part], done.at[start // PIECE]
        )
        copy.start()
        copies.append(copy)
    group = lane_group((1, HEAD))
    blocks = []
    for first in range(0, RING, 4):
        block = jnp.full((1, HEAD), -1, jnp.int32)
        for i in range(4):
            row = notes_ref[first + i : first + i + 1, :]
            row = pltpu.roll(row, ROOM * i, 1) if i else row
            block = jnp.where(group == i, row, block)
        blocks.append(block)
    ids = jnp.concatenate(blocks, axis=1)
    count = RING * ROOM
    step = 256
    lines = iota((step, count), 0).astype(F32).astype(BF16)

    def picked(start, rows):
        size = rows.shape[1]
        hots = []
        for at in range(start, start + size, step):
            here = (ids >= at) & (ids < at + step)
            near = jnp.where(here, ids - at, -1).astype(F32).astype(BF16)
            some = lines[: min(step, start + size - at)]
            hots.append(jnp.where(some == near, jnp.ones((), BF16), jnp.zeros((), BF16)))
        return dot(rows, jnp.concatenate(hots, axis=0) if len(hots) > 1 else hots[0])

    total = picked(whole, rest_ref[...])
    for start in range(0, whole, PIECE):
        copies[start // PIECE].wait()
        total = total + picked(start, held_ref[:, start : min(start + PIECE, whole)])
    total = total.T
    for d in range(RING):
        out_ref[d] = total[d * ROOM : d * ROOM + TAKE].astype(BF16)


def pack(rows, packed_ref):
    low = rows[:, :HEAD].astype(BF16)
    high = rows[:, HEAD : 2 * HEAD].astype(BF16)
    tail = jnp.concatenate([rows[:, 2 * HEAD :], jnp.zeros((TOKENS, HEAD - TAIL), F32)], axis=1)
    mixed = tail[:ROWS]
    for t in range(1, STEPS):
        mixed = mixed + pltpu.roll(tail[t * ROWS : (t + 1) * ROWS], TAIL * t, 1)
    mixed = mixed.astype(BF16)
    for b in range(RING):
        packed_ref[b, :TOKENS, :] = low
        packed_ref[b, TOKENS : 2 * TOKENS, :] = high
        packed_ref[b, 2 * TOKENS :, :] = mixed


def unpack_kernel(at_ref, got_ref, out_ref, packed_ref):
    hot = (at_ref[...] == iota((TOKENS, RING * TAKE), 1)).astype(F32).astype(BF16)
    rows = dot(hot, got_ref[...])
    out_ref[...] = rows.astype(BF16)
    pack(rows, packed_ref)


def pack_kernel(rows_ref, packed_ref):
    pack(rows_ref[...].astype(F32), packed_ref)


def normed_times(all_ref, gain_ref, weights):
    group = lane_group((ROWS, HEAD))
    squares = jnp.zeros((TOKENS, HEAD), F32)
    tail_squares = jnp.zeros((ROWS, HEAD), F32)
    product = jnp.zeros((TOKENS, 2 * HEAD), F32)
    tail_blocks, tail_weights = [], []
    for b in range(RING):
        low = all_ref[b, :TOKENS, :].astype(F32)
        high = all_ref[b, TOKENS : 2 * TOKENS, :].astype(F32)
        tail = all_ref[b, 2 * TOKENS :, :].astype(F32)
        main_weights, more_weights = weights(b)
        squares = squares + (low * low + high * high)
        tail_squares = tail_squares + tail * tail
        both = jnp.concatenate(
            [
                (low * gain_ref[0, b : b + 1, :]).astype(BF16),
                (high * gain_ref[1, b : b + 1, :]).astype(BF16),
            ],
            axis=1,
        )
        product = product + dot(both, main_weights)
        tail_weights.append(more_weights)
        scaled = tail * gain_ref[2, b : b + 1, :]
        place = b % 4
        if place == 0:
            tail_blocks.append([jnp.zeros((ROWS, HEAD), F32) for _ in range(STEPS)])
        for t in range(STEPS):
            shift = (TAIL * (place - t)) % HEAD
            moved = pltpu.roll(scaled, shift, 1) if shift else scaled
            tail_blocks[-1][t] = jnp.where(group == place, moved, tail_blocks[-1][t])
    tails = jnp.concatenate(
        [jnp.concatenate(block, axis=0).astype(BF16) for block in tail_blocks], axis=1
    )
    product = product + dot(tails, jnp.concatenate(tail_weights, axis=0))
    total = jnp.sum(squares, axis=1, keepdims=True) + jnp.concatenate(
        [
            jnp.sum(jnp.where(group == t, tail_squares, 0.0), axis=1, keepdims=True)
            for t in range(STEPS)
        ],
        axis=0,
    )
    return product * lax.rsqrt(total * (1.0 / D) + EPSILON)


def rotary(u, cos_ref, sin_ref):
    return u * cos_ref[...] + pltpu.roll(u, HEAD // 2, 1) * sin_ref[...]


def query_kernel(
    all_ref, gain_ref, cos_ref, sin_ref, slot_ref, wq_ref, q_ref, send_ref, held_ref, done
):
    copies = []
    for b in range(RING):
        rows = pl.ds(b * SHARE, SHARE)
        copies.append(pltpu.make_async_copy(wq_ref.at[rows, :], held_ref.at[b], done.at[b]))
        copies[-1].start()

    def weights(b):
        copies[b].wait()
        return held_ref[b, : 2 * HEAD, :], held_ref[b, 2 * HEAD :, :]

    query = normed_times(all_ref, gain_ref, weights)
    turned = jnp.concatenate(
        [
            rotary(query[:, :HEAD], cos_ref, sin_ref).astype(BF16),
            rotary(query[:, HEAD:], cos_ref, sin_ref).astype(BF16),
        ],
        axis=1,
    )
    q_ref[...] = turned
    wide = jnp.concatenate([turned[t * ROWS : (t + 1) * ROWS] for t in range(STEPS)], axis=1)
    hot = (iota((RING * SLOT, ROWS), 0) == slot_ref[0:1, :]).astype(F32).astype(BF16)
    send_ref[...] = dot(hot, wide).astype(BF16)


def place_kernel(q_ref, slot_ref, send_ref):
    turned = q_ref[...]
    wide = jnp.concatenate([turned[t * ROWS : (t + 1) * ROWS] for t in range(STEPS)], axis=1)
    hot = (iota((RING * SLOT, ROWS), 0) == slot_ref[1:2, :]).astype(F32).astype(BF16)
    send_ref[...] = dot(hot, wide).astype(BF16)


def prefix_kernel(turn, own_ref, notes_ref, keys_ref, values_ref, out_ref):
    lanes = iota((RING, SLOT, HEAD), 2) - (ROOM + turn) == iota((RING, SLOT, HEAD), 1)
    notes = jnp.where(lanes, notes_ref[...][:, None, :], 0).reshape(RING * SLOT, HEAD)
    odd = jnp.sum(notes, axis=1, keepdims=True) == 1
    keys = jnp.concatenate([keys_ref[0], keys_ref[1]], axis=1)
    values = jnp.concatenate([values_ref[0], values_ref[1]], axis=1)
    slots = RING * SLOT
    lanes = iota((slots, HEAD), 1)
    denoms = jnp.zeros((slots, HEAD), F32)
    batch = 4
    for first in range(0, PAIRS, batch):
        some = range(first, first + batch)
        parts = []
        for i in some:
            q = own_ref[:, i * HEAD : (i + 1) * HEAD].astype(F32)
            parts.append(
                jnp.concatenate(
                    [jnp.where(odd, 0.0, q).astype(BF16), jnp.where(odd, q, 0.0).astype(BF16)],
                    axis=1,
                )
            )
        scores = dot(jnp.concatenate(parts, axis=0), keys, ((1,), (1,)))
        weights = capped_exp(scores).astype(BF16)
        numer = dot(weights, values)
        denom = jnp.sum(weights.astype(F32), axis=1, keepdims=True)
        for n, i in enumerate(some):
            part = numer[n * slots : (n + 1) * slots]
            out_ref[:, i * HEAD : (i + 1) * HEAD] = jnp.where(
                odd, part[:, HEAD:], part[:, :HEAD]
            ).astype(BF16)
            denoms = jnp.where(lanes == i, denom[n * slots : (n + 1) * slots], denoms)
    out_ref[:, WIDE:] = denoms.astype(BF16)


def local_kernel(
    all_ref, gain_ref, cos_ref, sin_ref, wkv_ref, q_ref, sk_ref, sv_ref, len_ref, out_ref
):
    def weights(b):
        start = b * SHARE
        return [
            jnp.concatenate([wkv_ref[0, rows, :], wkv_ref[1, rows, :]], axis=1)
            for rows in (
                slice(start, start + 2 * HEAD),
                slice(start + 2 * HEAD, start + SHARE),
            )
        ]

    keyval = normed_times(all_ref, gain_ref, weights)
    new_keys = rotary(keyval[:, :HEAD], cos_ref, sin_ref).astype(BF16)
    new_values = keyval[:, HEAD:].astype(BF16)
    suffix = ROWS * SUF
    keys = jnp.concatenate([sk_ref[...], new_keys], axis=0)
    values = jnp.concatenate([sv_ref[...], new_values], axis=0)
    columns = suffix + TOKENS
    column = iota((ROWS, columns), 1)
    row = iota((ROWS, columns), 0)
    first = row * SUF
    in_suffix = (column >= first) & (column < first + len_ref[...])
    lanes = iota((ROWS, HEAD), 1)
    denoms = jnp.zeros((ROWS, HEAD), F32)
    usable = in_suffix
    for t in range(STEPS):
        usable = usable | (column == row + (suffix + t * ROWS))
        for g in range(GROUP):
            i = t * GROUP + g
            q = q_ref[t * ROWS : (t + 1) * ROWS, g * HEAD : (g + 1) * HEAD]
            scores = dot(q, keys, ((1,), (1,)))
            weights = jnp.where(usable, capped_exp(scores), 0.0).astype(BF16)
            out_ref[:, i * HEAD : (i + 1) * HEAD] = dot(weights, values)
            denom = jnp.sum(weights.astype(F32), axis=1, keepdims=True)
            denoms = jnp.where(lanes == i, denom, denoms)
    out_ref[:, WIDE:] = denoms


def select_kernel(slot_ref, back_ref, local_ref, out_ref):
    hot = (slot_ref[:, 1:2] == iota((ROWS, RING * SLOT), 1)).astype(F32).astype(BF16)
    out_ref[...] = dot(hot, back_ref[...]) + local_ref[...]


def output_kernel(slot_ref, back_ref, local_ref, w_ref, out_ref):
    hot = (slot_ref[:, 0:1] == iota((ROWS, RING * SLOT), 1)).astype(F32).astype(BF16)
    total = dot(hot, back_ref[...]) + local_ref[...]
    rows = []
    for t in range(STEPS):
        heads = []
        for g in range(GROUP):
            i = t * GROUP + g
            heads.append(
                (
                    total[:, i * HEAD : (i + 1) * HEAD] / total[:, WIDE + i : WIDE + i + 1]
                ).astype(BF16)
            )
        rows.append(jnp.concatenate(heads, axis=1))
    attended = jnp.concatenate(rows, axis=0)
    lanes = iota((TOKENS, HEAD), 1)
    group = lane_group((ROWS, HEAD))
    quad = 4 * SHARE
    for first in range(0, RING, 4):
        part = dot(attended, w_ref[:, first * SHARE : first * SHARE + quad])
        for i in range(4):
            b = first + i
            tiles = [part[:, (2 * i + n) * HEAD : (2 * i + n + 1) * HEAD] for n in range(3)]
            away = TAIL * i
            if away:
                moved = [pltpu.roll(tile, HEAD - away, 1) for tile in tiles]
                low = jnp.where(lanes < HEAD - away, moved[0], moved[1])
                high = jnp.where(lanes < HEAD - away, moved[1], moved[2])
            else:
                low, high = tiles[0], tiles[1]
            out_ref[b, :TOKENS, :] = low.astype(BF16)
            out_ref[b, TOKENS : 2 * TOKENS, :] = high.astype(BF16)
            mixed = jnp.zeros((ROWS, HEAD), F32)
            for t in range(STEPS):
                tail = tiles[2][t * ROWS : (t + 1) * ROWS]
                shift = (TAIL * (t - i)) % HEAD
                tail = pltpu.roll(tail, shift, 1) if shift else tail
                mixed = jnp.where(group == t, tail, mixed)
            out_ref[b, 2 * TOKENS :, :] = mixed.astype(BF16)


def reduce_kernel(parts_ref, sum_ref, squares_ref):
    total = parts_ref[0].astype(F32)
    for b in range(1, RING):
        total = total + parts_ref[b].astype(F32)
    sum_ref[...] = total
    low, high, tail = total[:TOKENS], total[TOKENS : 2 * TOKENS], total[2 * TOKENS :]
    group = lane_group((ROWS, HEAD))
    squares = jnp.sum(low * low + high * high, axis=1, keepdims=True) + jnp.concatenate(
        [
            jnp.sum(jnp.where(group == t, tail * tail, 0.0), axis=1, keepdims=True)
            for t in range(STEPS)
        ],
        axis=0,
    )
    diagonal = iota((HEAD, HEAD), 0) == iota((HEAD, HEAD), 1)
    one = jnp.sum(jnp.where(diagonal, squares[:HEAD], 0.0), axis=0, keepdims=True)
    rest = TOKENS - HEAD
    two = jnp.sum(jnp.where(diagonal[:rest], squares[HEAD:], 0.0), axis=0, keepdims=True)
    line = jnp.concatenate([one, two], axis=0)
    for b in range(RING):
        squares_ref[b] = line


def finish_kernel(squares_ref, sum_ref, rows_ref, gain_ref, out_ref):
    line = squares_ref[0]
    for b in range(1, RING):
        line = line + squares_ref[b]
    line = lax.rsqrt(line * (1.0 / D) + EPSILON)
    diagonal = iota((HEAD, HEAD), 0) == iota((HEAD, HEAD), 1)
    rest = TOKENS - HEAD
    one = jnp.sum(jnp.where(diagonal, line[0:1], 0.0), axis=1, keepdims=True)
    two = jnp.sum(jnp.where(diagonal[:rest], line[1:2], 0.0), axis=1, keepdims=True)
    root = jnp.concatenate([one, two], axis=0)
    rows = rows_ref[...].astype(F32)
    gain = gain_ref[...]
    total = sum_ref[...]
    low = total[:TOKENS] * root * gain[:, :HEAD]
    high = total[TOKENS : 2 * TOKENS] * root * gain[:, HEAD : 2 * HEAD]
    tails = []
    for t in range(STEPS):
        tail = total[2 * TOKENS :]
        tails.append(pltpu.roll(tail, HEAD - TAIL * t, 1) if t else tail)
    tail = jnp.concatenate(tails, axis=0)[:, :TAIL] * root * gain[:, 2 * HEAD :]
    scaled = jnp.concatenate([low, high, tail], axis=1)
    out_ref[...] = (rows + scaled).astype(BF16)


def exchange(x, axis):
    return lax.all_to_all(x, axis, split_axis=0, concat_axis=0, tiled=True)


def per_device(
    token_ids,
    prompt_of,
    suffix_len,
    table,
    pre_gain,
    w_query,
    w_keyval,
    w_out,
    post_gain,
    prefix_keys,
    prefix_values,
    suffix_keys,
    suffix_values,
):
    vocab = table.shape[0]
    prompt_len = prefix_keys.shape[1]
    shape = jax.ShapeDtypeStruct

    notes, at, slot_columns, slot_lines = call(
        functools.partial(ask_kernel, vocab),
        [
            shape((RING, HEAD), jnp.int32),
            shape((TOKENS, 1), jnp.int32),
            shape((ROWS, 2), jnp.int32),
            shape((2, ROWS), jnp.int32),
        ],
        (token_ids, prompt_of.reshape(1, ROWS)),
    )
    notes = exchange(notes.reshape(RING, 1, HEAD), "prefix").reshape(RING, HEAD)
    ends = jnp.max(notes[:, ENDS : ENDS + 2], axis=0)

    whole = vocab // 256 * 256
    picked = call(
        pick_kernel,
        shape((RING, TAKE, SHARE), BF16),
        (notes, table[whole:].T, table.T),
        flops=2 * vocab * RING * ROOM * SHARE,
        left=(2,),
        scratch=(
            pltpu.VMEM((SHARE, whole), BF16),
            pltpu.SemaphoreType.DMA((-(-whole // PIECE),)),
        ),
    )
    got = exchange(picked, "prefix").reshape(RING * TAKE, SHARE)
    own = shape((TOKENS, SHARE), BF16), shape((RING, PACKED, HEAD), BF16)
    placed = tuple(call(unpack_kernel, list(own), (at, got)))

    def take_all(_):
        everyone = exchange(jnp.broadcast_to(token_ids, (RING, STEPS, ROWS)), "prefix")
        inside_at = everyone - lax.axis_index("prefix") * vocab
        inside = (inside_at >= 0) & (inside_at < vocab)
        rows = jnp.take(table, jnp.clip(inside_at, 0, vocab - 1), axis=0)
        rows = jnp.where(inside[..., None], rows, jnp.zeros_like(rows))
        rows = exchange(rows, "prefix").astype(F32).sum(axis=0).astype(BF16)
        rows = rows.reshape(TOKENS, SHARE)
        return rows, call(pack_kernel, own[1], (rows,))

    embedded, packed = lax.cond(ends[0] > TAKE, take_all, lambda placed: placed, placed)
    everywhere = exchange(packed, "branch")

    half = HEAD // 2
    frequency = 10000.0 ** (-(jnp.arange(half, dtype=F32) * 2.0 / HEAD))
    positions = (prompt_len + suffix_len[None, :] + jnp.arange(STEPS)[:, None]).astype(F32)
    angles = positions.reshape(TOKENS, 1) * frequency
    cosines = jnp.cos(angles)
    sines = jnp.sin(angles)
    cosines = jnp.concatenate([cosines, cosines], axis=1)
    sines = jnp.concatenate([-sines, sines], axis=1)
    gains = pre_gain.reshape(RING, SHARE)
    gains = jnp.stack(
        [gains[:, :HEAD], gains[:, HEAD : 2 * HEAD], jnp.tile(gains[:, 2 * HEAD :], (1, 4))]
    )
    queries, sent = call(
        query_kernel,
        [shape((TOKENS, GROUP * HEAD), BF16), shape((RING * SLOT, WIDE), BF16)],
        (everywhere, gains, cosines, sines, slot_lines, w_query),
        flops=2 * TOKENS * D * 2 * HEAD,
        left=(5,),
        scratch=(
            pltpu.VMEM((RING, SHARE, GROUP * HEAD), BF16),
            pltpu.SemaphoreType.DMA((RING,)),
        ),
    )

    def ask(sent):
        return exchange(sent.reshape(RING, SLOT, WIDE), "prefix").reshape(RING * SLOT, WIDE)

    def answer(own, turn):
        sums = call(
            functools.partial(prefix_kernel, turn),
            shape((RING * SLOT, BACK), BF16),
            (own, notes, prefix_keys, prefix_values),
            flops=8 * RING * SLOT * prompt_len * WIDE,
        )
        return exchange(sums.reshape(RING, SLOT, BACK), "prefix").reshape(RING * SLOT, BACK)

    own = ask(sent)
    local = call(
        local_kernel,
        shape((ROWS, BACK), F32),
        (
            everywhere,
            gains,
            cosines,
            sines,
            w_keyval,
            queries,
            suffix_keys.reshape(ROWS * SUF, HEAD),
            suffix_values.reshape(ROWS * SUF, HEAD),
            suffix_len.reshape(ROWS, 1),
        ),
        flops=2 * TOKENS * D * 2 * HEAD + 4 * ROWS * WIDE * (ROWS * SUF + TOKENS),
    )
    own, local = lax.optimization_barrier((own, local))

    def second_round(local):
        sent = call(
            place_kernel,
            shape((RING * SLOT, WIDE), BF16),
            (queries, slot_lines),
        )
        back = answer(ask(sent), SLOT)
        return call(
            select_kernel,
            shape((ROWS, BACK), F32),
            (slot_columns, back, local),
        )

    local = lax.cond(ends[1] > SLOT, second_round, lambda local: local, local)
    own, local = lax.optimization_barrier((own, local))
    back = answer(own, 0)

    shares = call(
        output_kernel,
        shape((RING, PACKED, HEAD), BF16),
        (slot_columns, back, local, w_out),
        flops=2 * TOKENS * GROUP * HEAD * D,
    )
    shares = exchange(shares, "branch")
    total, squares = call(
        reduce_kernel,
        [shape((PACKED, HEAD), F32), shape((RING, 2, HEAD), F32)],
        (shares,),
    )
    squares = exchange(squares, "branch")
    layer_out = call(
        finish_kernel,
        shape((TOKENS, SHARE), BF16),
        (squares, total, embedded, post_gain.reshape(1, SHARE)),
    )
    return layer_out.reshape(STEPS, ROWS, SHARE)


def solution(mesh):
    placed = (
        P(None, "prefix"),
        P("prefix", None),
        P("prefix"),
        P("prefix", "branch"),
        P(),
        P(None, "branch"),
        P(None, None, "branch"),
        P("branch", None),
        P("branch"),
        P("prefix", None, "branch"),
        P("prefix", None, "branch"),
        P("prefix", None, "branch"),
        P("prefix", None, "branch"),
    )
    return jax.shard_map(
        per_device,
        mesh=mesh,
        in_specs=placed,
        out_specs=P(None, "prefix", "branch"),
        check_vma=False,
    )
```

```python
import functools

import jax
import jax.numpy as jnp
from jax import lax
from jax.experimental import pallas as pl
from jax.experimental.pallas import tpu as pltpu
from jax.sharding import PartitionSpec as P

D = 4608
HEADS = 32
KV_HEADS = 16
HEAD = 128
SUF = 8
SOFT_CAP = 50.0
EPSILON = 1e-06
SCALE = float(D // HEADS) ** (-0.5)

RING = 16
STEPS = 4
ROWS = 48
TOKENS = STEPS * ROWS
SHARE = D // RING
TAIL = SHARE - 2 * HEAD
PACKED = 2 * TOKENS + ROWS
TAKE = 24
ROOM = 32
ENDS = ROOM + 16
COUNTS = 64
ALL = 256
SLOT = 8
GROUP = HEADS // KV_HEADS
PAIRS = STEPS * GROUP
WIDE = PAIRS * HEAD
BACK = WIDE + HEAD

F32 = jnp.float32
BF16 = jnp.bfloat16
VMEM = pl.BlockSpec(memory_space=pltpu.VMEM)
SMEM = pl.BlockSpec(memory_space=pltpu.SMEM)
ANY = pl.BlockSpec(memory_space=pl.ANY)


def call(kernel, out_shape, args, flops=0, scalars=0, left=(), scratch=(), limit=24):
    nbytes = sum(a.size * a.dtype.itemsize for a in args)
    many = isinstance(out_shape, (list, tuple))
    return pl.pallas_call(
        kernel,
        out_shape=out_shape,
        in_specs=[
            SMEM if n < scalars else ANY if n in left else VMEM for n in range(len(args))
        ],
        out_specs=[VMEM] * len(out_shape) if many else VMEM,
        scratch_shapes=list(scratch),
        compiler_params=pltpu.CompilerParams(vmem_limit_bytes=limit * 1024 * 1024),
        cost_estimate=pl.CostEstimate(flops=flops, bytes_accessed=nbytes, transcendentals=0),
    )(*args)


def dot(a, b, contract=((1,), (0,))):
    return lax.dot_general(a, b, (contract, ((), ())), preferred_element_type=F32)


def iota(shape, axis):
    return lax.broadcasted_iota(jnp.int32, shape, axis)


def capped_exp(scores):
    return jnp.exp(SOFT_CAP * jnp.tanh(scores * (SCALE / SOFT_CAP)))


def lane_group(shape):
    return lax.shift_right_logical(iota(shape, 1), 5)


def column_of(row):
    n = row.shape[1]
    diagonal = iota((n, n), 0) == iota((n, n), 1)
    return jnp.sum(jnp.where(diagonal, row, 0), axis=1, keepdims=True)


def ask_kernel(vocab, ids_ref, prompt_ref, notes_ref, at_ref, columns_ref, lines_ref):
    def owner_of(ids):
        total = jnp.zeros(ids.shape, jnp.int32)
        for d in range(1, RING):
            total = total + (ids >= d * vocab).astype(jnp.int32)
        return total

    rows = [ids_ref[t : t + 1, :] for t in range(STEPS)]
    column = jnp.concatenate([column_of(row) for row in rows], axis=0)
    owner = owner_of(column)
    base = owner * vocab
    down = iota((TOKENS, ROWS), 0)
    over = iota((TOKENS, ROWS), 1)
    rank = jnp.zeros((TOKENS, ROWS), jnp.int32)
    new_rows = []
    for t in range(STEPS):
        seen = (column == rows[t]) & (down < over + t * ROWS)
        new = 1 - jnp.max(seen.astype(jnp.int32), axis=0, keepdims=True)
        new_rows.append(new)
        rank = rank + jnp.where((rows[t] >= base) & (rows[t] < column), new, 0)
    rank = jnp.sum(rank, axis=1, keepdims=True)
    fits = rank < TAKE
    at_ref[...] = jnp.where(fits, owner * TAKE + rank, -1)
    value = column - base + 1
    cell = jnp.where(fits, rank, -1) == iota((TOKENS, HEAD), 1)
    coarse = jnp.where(cell, lax.shift_right_logical(value, 6), 0).astype(F32).astype(BF16)
    fine = jnp.where(cell, value & 63, 0).astype(F32).astype(BF16)
    holders = iota((RING, ROWS), 0)
    high = jnp.zeros((RING, HEAD), F32)
    low = jnp.zeros((RING, HEAD), F32)
    count = jnp.zeros((RING, ROWS), F32)
    for t in range(STEPS):
        part = slice(t * ROWS, (t + 1) * ROWS)
        mine = jnp.where(owner_of(rows[t]) == holders, new_rows[t], 0).astype(F32)
        count = count + mine
        mine = mine.astype(BF16)
        high = high + dot(mine, coarse[part])
        low = low + dot(mine, fine[part])
    asked = high.astype(jnp.int32) * 64 + low.astype(jnp.int32) - 1

    prompt = prompt_ref[...]
    prompt_column = column_of(prompt)
    holder = lax.shift_right_logical(prompt, 1)
    holder_column = lax.shift_right_logical(prompt_column, 1)
    down = iota((ROWS, ROWS), 0)
    over = iota((ROWS, ROWS), 1)
    same = holder == holder_column
    turn = jnp.sum((same & (down < over)).astype(jnp.int32), axis=0, keepdims=True)
    turn_column = jnp.sum((same & (over < down)).astype(jnp.int32), axis=1, keepdims=True)
    mine = (holder == holders).astype(F32).astype(BF16)
    odd = jnp.where(turn_column + ROOM == iota((ROWS, HEAD), 1), prompt_column & 1, 0)
    odds = dot(mine, odd.astype(F32).astype(BF16)).astype(jnp.int32)
    lane = iota((RING, HEAD), 1)
    notes = jnp.where(lane < ROOM, asked, odds)
    most = jnp.max(rank, axis=0, keepdims=True) + 1
    notes = jnp.where(lane == ENDS, most, notes)
    most = jnp.max(turn_column, axis=0, keepdims=True) + 1
    notes = jnp.where(lane == ENDS + 1, most, notes)
    count = jnp.sum(count, axis=1, keepdims=True).astype(jnp.int32)
    notes = jnp.where(lane == ENDS + 2, count, notes)
    counts = jnp.where(lane == iota((RING, HEAD), 0) + COUNTS, count, 0)
    counts = jnp.sum(counts, axis=0, keepdims=True)
    listed = (lane >= COUNTS) & (lane < COUNTS + RING)
    notes_ref[...] = jnp.where(listed, counts, notes)

    def slots(holder, turn):
        now = jnp.where(turn < SLOT, holder * SLOT + turn, -1)
        later = jnp.where(turn >= SLOT, holder * SLOT + turn - SLOT, -1)
        return now, later

    columns_ref[...] = jnp.concatenate(slots(holder_column, turn_column), axis=1)
    lines_ref[...] = jnp.concatenate(slots(holder, turn), axis=0)


LONG = 20_000_000_000
PIECE = 1024


def pick_kernel(counts_ref, notes_ref, rest_ref, table_ref, out_ref, held_ref, rows_ref, done):
    whole = held_ref.shape[1]
    copies = []
    for start in range(0, whole, PIECE):
        part = pl.ds(start, min(PIECE, whole - start))
        copy = pltpu.make_async_copy(
            table_ref.at[:, part], held_ref.at[:, part], done.at[start // PIECE]
        )
        copy.start()
        copies.append(copy)
    lane = iota((8, HEAD), 1)
    ids = jnp.zeros((8, ALL), jnp.int32)
    start = 0
    starts = []
    for d in range(RING):
        starts.append(start)
        row = jnp.broadcast_to(notes_ref[d : d + 1, :], (8, HEAD))
        row = jnp.where(lane < ROOM, row + 1, 0)
        row = jnp.concatenate([row, jnp.zeros((8, ALL - HEAD), jnp.int32)], axis=1)
        ids = ids + (pltpu.roll(row, start & (ALL - 1), 1) if d else row)
        start = jnp.minimum(start + counts_ref[d, ENDS + 2], ALL)
    ids = ids[0:1] - 1
    count = ALL
    step = 256
    lines = iota((step, count), 0).astype(F32).astype(BF16)

    def picked(start, rows):
        size = rows.shape[1]
        hots = []
        for at in range(start, start + size, step):
            here = (ids >= at) & (ids < at + step)
            near = jnp.where(here, ids - at, -1).astype(F32).astype(BF16)
            some = lines[: min(step, start + size - at)]
            hots.append(jnp.where(some == near, jnp.ones((), BF16), jnp.zeros((), BF16)))
        return dot(rows, jnp.concatenate(hots, axis=0) if len(hots) > 1 else hots[0])

    total = picked(whole, rest_ref[...])
    for start in range(0, whole, PIECE):
        copies[start // PIECE].wait()
        total = total + picked(start, held_ref[:, start : min(start + PIECE, whole)])
    rows_ref[:ALL, :] = total.T
    rows_ref[ALL:, :] = jnp.zeros((ROOM, SHARE), F32)
    for d in range(RING):
        if d:
            whole_start = pl.multiple_of(starts[d] - (starts[d] & 7), 8)
            some = rows_ref[pl.ds(whole_start, ROOM), :]
            some = pltpu.roll(some, (ROOM - (starts[d] & 7)) & (ROOM - 1), 0)
        else:
            some = rows_ref[:ROOM, :]
        out_ref[d] = some[:TAKE].astype(BF16)


def pack(rows, packed_ref):
    low = rows[:, :HEAD].astype(BF16)
    high = rows[:, HEAD : 2 * HEAD].astype(BF16)
    tail = jnp.concatenate([rows[:, 2 * HEAD :], jnp.zeros((TOKENS, HEAD - TAIL), F32)], axis=1)
    mixed = tail[:ROWS]
    for t in range(1, STEPS):
        mixed = mixed + pltpu.roll(tail[t * ROWS : (t + 1) * ROWS], TAIL * t, 1)
    mixed = mixed.astype(BF16)
    for b in range(RING):
        packed_ref[b, :TOKENS, :] = low
        packed_ref[b, TOKENS : 2 * TOKENS, :] = high
        packed_ref[b, 2 * TOKENS :, :] = mixed


def unpack_kernel(at_ref, got_ref, out_ref, packed_ref):
    hot = (at_ref[...] == iota((TOKENS, RING * TAKE), 1)).astype(F32).astype(BF16)
    rows = dot(hot, got_ref[...])
    out_ref[...] = rows.astype(BF16)
    pack(rows, packed_ref)


def pack_kernel(rows_ref, packed_ref):
    pack(rows_ref[...].astype(F32), packed_ref)


def normed_times(all_ref, gain_ref, weights):
    group = lane_group((ROWS, HEAD))
    squares = jnp.zeros((TOKENS, HEAD), F32)
    tail_squares = jnp.zeros((ROWS, HEAD), F32)
    product = jnp.zeros((TOKENS, 2 * HEAD), F32)
    tail_blocks, tail_weights = [], []
    for b in range(RING):
        low = all_ref[b, :TOKENS, :].astype(F32)
        high = all_ref[b, TOKENS : 2 * TOKENS, :].astype(F32)
        tail = all_ref[b, 2 * TOKENS :, :].astype(F32)
        main_weights, more_weights = weights(b)
        squares = squares + (low * low + high * high)
        tail_squares = tail_squares + tail * tail
        both = jnp.concatenate(
            [
                (low * gain_ref[0, b : b + 1, :]).astype(BF16),
                (high * gain_ref[1, b : b + 1, :]).astype(BF16),
            ],
            axis=1,
        )
        product = product + dot(both, main_weights)
        tail_weights.append(more_weights)
        scaled = tail * gain_ref[2, b : b + 1, :]
        place = b % 4
        if place == 0:
            tail_blocks.append([jnp.zeros((ROWS, HEAD), F32) for _ in range(STEPS)])
        for t in range(STEPS):
            shift = (TAIL * (place - t)) % HEAD
            moved = pltpu.roll(scaled, shift, 1) if shift else scaled
            tail_blocks[-1][t] = jnp.where(group == place, moved, tail_blocks[-1][t])
    tails = jnp.concatenate(
        [jnp.concatenate(block, axis=0).astype(BF16) for block in tail_blocks], axis=1
    )
    product = product + dot(tails, jnp.concatenate(tail_weights, axis=0))
    total = jnp.sum(squares, axis=1, keepdims=True) + jnp.concatenate(
        [
            jnp.sum(jnp.where(group == t, tail_squares, 0.0), axis=1, keepdims=True)
            for t in range(STEPS)
        ],
        axis=0,
    )
    return product * lax.rsqrt(total * (1.0 / D) + EPSILON)


def rotary(u, cos_ref, sin_ref):
    return u * cos_ref[...] + pltpu.roll(u, HEAD // 2, 1) * sin_ref[...]


def query_kernel(all_ref, gain_ref, cos_ref, sin_ref, slot_ref, wq_ref, q_ref, send_ref):
    def weights(b):
        start = b * SHARE
        return wq_ref[start : start + 2 * HEAD, :], wq_ref[start + 2 * HEAD : start + SHARE, :]

    query = normed_times(all_ref, gain_ref, weights)
    turned = jnp.concatenate(
        [
            rotary(query[:, :HEAD], cos_ref, sin_ref).astype(BF16),
            rotary(query[:, HEAD:], cos_ref, sin_ref).astype(BF16),
        ],
        axis=1,
    )
    q_ref[...] = turned
    wide = jnp.concatenate([turned[t * ROWS : (t + 1) * ROWS] for t in range(STEPS)], axis=1)
    hot = (iota((RING * SLOT, ROWS), 0) == slot_ref[0:1, :]).astype(F32).astype(BF16)
    send_ref[...] = dot(hot, wide).astype(BF16)


def place_kernel(q_ref, slot_ref, send_ref):
    turned = q_ref[...]
    wide = jnp.concatenate([turned[t * ROWS : (t + 1) * ROWS] for t in range(STEPS)], axis=1)
    hot = (iota((RING * SLOT, ROWS), 0) == slot_ref[1:2, :]).astype(F32).astype(BF16)
    send_ref[...] = dot(hot, wide).astype(BF16)


def prefix_kernel(turn, own_ref, notes_ref, keys_ref, values_ref, out_ref):
    lanes = iota((RING, SLOT, HEAD), 2) - (ROOM + turn) == iota((RING, SLOT, HEAD), 1)
    notes = jnp.where(lanes, notes_ref[...][:, None, :], 0).reshape(RING * SLOT, HEAD)
    odd = jnp.sum(notes, axis=1, keepdims=True) == 1
    keys = jnp.concatenate([keys_ref[0], keys_ref[1]], axis=1)
    values = jnp.concatenate([values_ref[0], values_ref[1]], axis=1)
    slots = RING * SLOT
    lanes = iota((slots, HEAD), 1)
    denoms = jnp.zeros((slots, HEAD), F32)
    batch = 4
    for first in range(0, PAIRS, batch):
        some = range(first, first + batch)
        parts = []
        for i in some:
            q = own_ref[:, i * HEAD : (i + 1) * HEAD].astype(F32)
            parts.append(
                jnp.concatenate(
                    [jnp.where(odd, 0.0, q).astype(BF16), jnp.where(odd, q, 0.0).astype(BF16)],
                    axis=1,
                )
            )
        scores = dot(jnp.concatenate(parts, axis=0), keys, ((1,), (1,)))
        weights = capped_exp(scores).astype(BF16)
        numer = dot(weights, values)
        denom = jnp.sum(weights.astype(F32), axis=1, keepdims=True)
        for n, i in enumerate(some):
            part = numer[n * slots : (n + 1) * slots]
            out_ref[:, i * HEAD : (i + 1) * HEAD] = jnp.where(
                odd, part[:, HEAD:], part[:, :HEAD]
            ).astype(BF16)
            denoms = jnp.where(lanes == i, denom[n * slots : (n + 1) * slots], denoms)
    out_ref[:, WIDE:] = denoms.astype(BF16)


def local_kernel(
    all_ref, gain_ref, cos_ref, sin_ref, wkv_ref, q_ref, sk_ref, sv_ref, len_ref, out_ref
):
    def weights(b):
        start = b * SHARE
        return [
            jnp.concatenate([wkv_ref[0, rows, :], wkv_ref[1, rows, :]], axis=1)
            for rows in (
                slice(start, start + 2 * HEAD),
                slice(start + 2 * HEAD, start + SHARE),
            )
        ]

    keyval = normed_times(all_ref, gain_ref, weights)
    new_keys = rotary(keyval[:, :HEAD], cos_ref, sin_ref).astype(BF16)
    new_values = keyval[:, HEAD:].astype(BF16)
    suffix = ROWS * SUF
    keys = jnp.concatenate([sk_ref[...], new_keys], axis=0)
    values = jnp.concatenate([sv_ref[...], new_values], axis=0)
    columns = suffix + TOKENS
    column = iota((ROWS, columns), 1)
    row = iota((ROWS, columns), 0)
    first = row * SUF
    in_suffix = (column >= first) & (column < first + len_ref[...])
    lanes = iota((ROWS, HEAD), 1)
    denoms = jnp.zeros((ROWS, HEAD), F32)
    usable = in_suffix
    for t in range(STEPS):
        usable = usable | (column == row + (suffix + t * ROWS))
        for g in range(GROUP):
            i = t * GROUP + g
            q = q_ref[t * ROWS : (t + 1) * ROWS, g * HEAD : (g + 1) * HEAD]
            scores = dot(q, keys, ((1,), (1,)))
            weights = jnp.where(usable, capped_exp(scores), 0.0).astype(BF16)
            out_ref[:, i * HEAD : (i + 1) * HEAD] = dot(weights, values)
            denom = jnp.sum(weights.astype(F32), axis=1, keepdims=True)
            denoms = jnp.where(lanes == i, denom, denoms)
    out_ref[:, WIDE:] = denoms


def select_kernel(slot_ref, back_ref, local_ref, out_ref):
    hot = (slot_ref[:, 1:2] == iota((ROWS, RING * SLOT), 1)).astype(F32).astype(BF16)
    out_ref[...] = dot(hot, back_ref[...]) + local_ref[...]


def output_kernel(slot_ref, back_ref, local_ref, w_ref, out_ref):
    hot = (slot_ref[:, 0:1] == iota((ROWS, RING * SLOT), 1)).astype(F32).astype(BF16)
    total = dot(hot, back_ref[...]) + local_ref[...]
    rows = []
    for t in range(STEPS):
        heads = []
        for g in range(GROUP):
            i = t * GROUP + g
            heads.append(
                (
                    total[:, i * HEAD : (i + 1) * HEAD] / total[:, WIDE + i : WIDE + i + 1]
                ).astype(BF16)
            )
        rows.append(jnp.concatenate(heads, axis=1))
    attended = jnp.concatenate(rows, axis=0)
    lanes = iota((TOKENS, HEAD), 1)
    group = lane_group((ROWS, HEAD))
    quad = 4 * SHARE
    for first in range(0, RING, 4):
        part = dot(attended, w_ref[:, first * SHARE : first * SHARE + quad])
        for i in range(4):
            b = first + i
            tiles = [part[:, (2 * i + n) * HEAD : (2 * i + n + 1) * HEAD] for n in range(3)]
            away = TAIL * i
            if away:
                moved = [pltpu.roll(tile, HEAD - away, 1) for tile in tiles]
                low = jnp.where(lanes < HEAD - away, moved[0], moved[1])
                high = jnp.where(lanes < HEAD - away, moved[1], moved[2])
            else:
                low, high = tiles[0], tiles[1]
            out_ref[b, :TOKENS, :] = low.astype(BF16)
            out_ref[b, TOKENS : 2 * TOKENS, :] = high.astype(BF16)
            mixed = jnp.zeros((ROWS, HEAD), F32)
            for t in range(STEPS):
                tail = tiles[2][t * ROWS : (t + 1) * ROWS]
                shift = (TAIL * (t - i)) % HEAD
                tail = pltpu.roll(tail, shift, 1) if shift else tail
                mixed = jnp.where(group == t, tail, mixed)
            out_ref[b, 2 * TOKENS :, :] = mixed.astype(BF16)


def reduce_kernel(parts_ref, sum_ref, squares_ref):
    total = parts_ref[0].astype(F32)
    for b in range(1, RING):
        total = total + parts_ref[b].astype(F32)
    sum_ref[...] = total
    low, high, tail = total[:TOKENS], total[TOKENS : 2 * TOKENS], total[2 * TOKENS :]
    group = lane_group((ROWS, HEAD))
    squares = jnp.sum(low * low + high * high, axis=1, keepdims=True) + jnp.concatenate(
        [
            jnp.sum(jnp.where(group == t, tail * tail, 0.0), axis=1, keepdims=True)
            for t in range(STEPS)
        ],
        axis=0,
    )
    diagonal = iota((HEAD, HEAD), 0) == iota((HEAD, HEAD), 1)
    one = jnp.sum(jnp.where(diagonal, squares[:HEAD], 0.0), axis=0, keepdims=True)
    rest = TOKENS - HEAD
    two = jnp.sum(jnp.where(diagonal[:rest], squares[HEAD:], 0.0), axis=0, keepdims=True)
    line = jnp.concatenate([one, two], axis=0)
    for b in range(RING):
        squares_ref[b] = line


def scale_kernel(sum_ref, gain_ref, out_ref):
    total = sum_ref[...]
    tails = []
    for t in range(STEPS):
        tail = total[2 * TOKENS :]
        tails.append(pltpu.roll(tail, HEAD - TAIL * t, 1) if t else tail)
    tail = jnp.concatenate(tails, axis=0)[:, :TAIL]
    placed = jnp.concatenate([total[:TOKENS], total[TOKENS : 2 * TOKENS], tail], axis=1)
    out_ref[...] = placed * gain_ref[...]


def finish_kernel(squares_ref, scaled_ref, rows_ref, out_ref):
    line = squares_ref[0]
    for b in range(1, RING):
        line = line + squares_ref[b]
    line = lax.rsqrt(line * (1.0 / D) + EPSILON)
    diagonal = iota((HEAD, HEAD), 0) == iota((HEAD, HEAD), 1)
    rest = TOKENS - HEAD
    one = jnp.sum(jnp.where(diagonal, line[0:1], 0.0), axis=1, keepdims=True)
    two = jnp.sum(jnp.where(diagonal[:rest], line[1:2], 0.0), axis=1, keepdims=True)
    root = jnp.concatenate([one, two], axis=0)
    out_ref[...] = (rows_ref[...].astype(F32) + scaled_ref[...] * root).astype(BF16)


def exchange(x, axis):
    return lax.all_to_all(x, axis, split_axis=0, concat_axis=0, tiled=True)


def per_device(
    token_ids,
    prompt_of,
    suffix_len,
    table,
    pre_gain,
    w_query,
    w_keyval,
    w_out,
    post_gain,
    prefix_keys,
    prefix_values,
    suffix_keys,
    suffix_values,
):
    vocab = table.shape[0]
    prompt_len = prefix_keys.shape[1]
    shape = jax.ShapeDtypeStruct

    notes, at, slot_columns, slot_lines = call(
        functools.partial(ask_kernel, vocab),
        [
            shape((RING, HEAD), jnp.int32),
            shape((TOKENS, 1), jnp.int32),
            shape((ROWS, 2), jnp.int32),
            shape((2, ROWS), jnp.int32),
        ],
        (token_ids, prompt_of.reshape(1, ROWS)),
    )
    notes = exchange(notes.reshape(RING, 1, HEAD), "prefix").reshape(RING, HEAD)
    ends = jnp.max(notes[:, ENDS : ENDS + 2], axis=0)
    asked = jnp.max(jnp.sum(notes[:, COUNTS : COUNTS + RING], axis=0))
    crowded = (ends[0] > TAKE) | (asked > ALL)

    whole = vocab // 256 * 256
    rest = table[whole:].T
    half = HEAD // 2
    frequency = 10000.0 ** (-(jnp.arange(half, dtype=F32) * 2.0 / HEAD))
    positions = (prompt_len + suffix_len[None, :] + jnp.arange(STEPS)[:, None]).astype(F32)
    angles = positions.reshape(TOKENS, 1) * frequency
    cosines = jnp.cos(angles)
    sines = jnp.sin(angles)
    cosines = jnp.concatenate([cosines, cosines], axis=1)
    sines = jnp.concatenate([-sines, sines], axis=1)
    gains = pre_gain.reshape(RING, SHARE)
    gains = jnp.stack(
        [gains[:, :HEAD], gains[:, HEAD : 2 * HEAD], jnp.tile(gains[:, 2 * HEAD :], (1, 4))]
    )
    lengths = suffix_len.reshape(ROWS, 1)
    notes, rest, cosines, sines, gains, lengths = lax.optimization_barrier(
        (notes, rest, cosines, sines, gains, lengths)
    )
    picked = call(
        pick_kernel,
        shape((RING, TAKE, SHARE), BF16),
        (notes, notes, rest, table.T),
        flops=2 * vocab * ALL * SHARE,
        scalars=1,
        left=(3,),
        scratch=(
            pltpu.VMEM((SHARE, whole), BF16),
            pltpu.VMEM((ALL + ROOM, SHARE), F32),
            pltpu.SemaphoreType.DMA((-(-whole // PIECE),)),
        ),
    )
    got = exchange(picked, "prefix").reshape(RING * TAKE, SHARE)
    own = shape((TOKENS, SHARE), BF16), shape((RING, PACKED, HEAD), BF16)
    placed = tuple(call(unpack_kernel, list(own), (at, got), flops=LONG))

    def take_all(_):
        everyone = exchange(jnp.broadcast_to(token_ids, (RING, STEPS, ROWS)), "prefix")
        inside_at = everyone - lax.axis_index("prefix") * vocab
        inside = (inside_at >= 0) & (inside_at < vocab)
        rows = jnp.take(table, jnp.clip(inside_at, 0, vocab - 1), axis=0)
        rows = jnp.where(inside[..., None], rows, jnp.zeros_like(rows))
        rows = exchange(rows, "prefix").astype(F32).sum(axis=0).astype(BF16)
        rows = rows.reshape(TOKENS, SHARE)
        return rows, call(pack_kernel, own[1], (rows,))

    embedded, packed = lax.cond(crowded, take_all, lambda placed: placed, placed)
    everywhere = exchange(packed, "branch")

    queries, sent = call(
        query_kernel,
        [shape((TOKENS, GROUP * HEAD), BF16), shape((RING * SLOT, WIDE), BF16)],
        (everywhere, gains, cosines, sines, slot_lines, w_query),
        flops=LONG,
    )

    def ask(sent):
        return exchange(sent.reshape(RING, SLOT, WIDE), "prefix").reshape(RING * SLOT, WIDE)

    def answer(own, turn):
        sums = call(
            functools.partial(prefix_kernel, turn),
            shape((RING * SLOT, BACK), BF16),
            (own, notes, prefix_keys, prefix_values),
            flops=8 * RING * SLOT * prompt_len * WIDE,
        )
        return exchange(sums.reshape(RING, SLOT, BACK), "prefix").reshape(RING * SLOT, BACK)

    own = ask(sent)
    local = call(
        local_kernel,
        shape((ROWS, BACK), F32),
        (
            everywhere,
            gains,
            cosines,
            sines,
            w_keyval,
            queries,
            suffix_keys.reshape(ROWS * SUF, HEAD),
            suffix_values.reshape(ROWS * SUF, HEAD),
            lengths,
        ),
        flops=2 * TOKENS * D * 2 * HEAD + 4 * ROWS * WIDE * (ROWS * SUF + TOKENS),
    )
    own, local = lax.optimization_barrier((own, local))

    def second_round(local):
        sent = call(
            place_kernel,
            shape((RING * SLOT, WIDE), BF16),
            (queries, slot_lines),
        )
        back = answer(ask(sent), SLOT)
        return call(
            select_kernel,
            shape((ROWS, BACK), F32),
            (slot_columns, back, local),
        )

    local = lax.cond(ends[1] > SLOT, second_round, lambda local: local, local)
    own, local = lax.optimization_barrier((own, local))
    back = answer(own, 0)

    shares = call(
        output_kernel,
        shape((RING, PACKED, HEAD), BF16),
        (slot_columns, back, local, w_out),
        flops=2 * TOKENS * GROUP * HEAD * D,
    )
    shares = exchange(shares, "branch")
    total, squares = call(
        reduce_kernel,
        [shape((PACKED, HEAD), F32), shape((RING, 2, HEAD), F32)],
        (shares,),
    )
    squares = exchange(squares, "branch")
    scaled = call(
        scale_kernel, shape((TOKENS, SHARE), F32), (total, post_gain.reshape(1, SHARE))
    )
    layer_out = call(
        finish_kernel,
        shape((TOKENS, SHARE), BF16),
        (squares, scaled, embedded),
    )
    return layer_out.reshape(STEPS, ROWS, SHARE)


def solution(mesh):
    placed = (
        P(None, "prefix"),
        P("prefix", None),
        P("prefix"),
        P("prefix", "branch"),
        P(),
        P(None, "branch"),
        P(None, None, "branch"),
        P("branch", None),
        P("branch"),
        P("prefix", None, "branch"),
        P("prefix", None, "branch"),
        P("prefix", None, "branch"),
        P("prefix", None, "branch"),
    )
    return jax.shard_map(
        per_device,
        mesh=mesh,
        in_specs=placed,
        out_specs=P(None, "prefix", "branch"),
        check_vma=False,
    )
```

```python
import functools

import jax
import jax.numpy as jnp
from jax import lax
from jax.experimental import pallas as pl
from jax.experimental.pallas import tpu as pltpu
from jax.sharding import PartitionSpec as P

D = 4608
HEADS = 32
KV_HEADS = 16
HEAD = 128
SUF = 8
SOFT_CAP = 50.0
EPSILON = 1e-06
SCALE = float(D // HEADS) ** (-0.5)

RING = 16
STEPS = 4
ROWS = 48
TOKENS = STEPS * ROWS
SHARE = D // RING
TAIL = SHARE - 2 * HEAD
PACKED = 2 * TOKENS + ROWS
TAKE = 24
ROOM = 32
ENDS = ROOM + 16
COUNTS = 64
ALL = 256
SLOT = 8
GROUP = HEADS // KV_HEADS
PAIRS = STEPS * GROUP
WIDE = PAIRS * HEAD
BACK = WIDE + HEAD

F32 = jnp.float32
BF16 = jnp.bfloat16
VMEM = pl.BlockSpec(memory_space=pltpu.VMEM)
SMEM = pl.BlockSpec(memory_space=pltpu.SMEM)


def call(kernel, out_shape, args, flops=0, scalars=0, scratch=(), limit=24):
    nbytes = sum(a.size * a.dtype.itemsize for a in args)
    many = isinstance(out_shape, (list, tuple))
    return pl.pallas_call(
        kernel,
        out_shape=out_shape,
        in_specs=[SMEM] * scalars + [VMEM] * (len(args) - scalars),
        out_specs=[VMEM] * len(out_shape) if many else VMEM,
        scratch_shapes=list(scratch),
        compiler_params=pltpu.CompilerParams(vmem_limit_bytes=limit * 1024 * 1024),
        cost_estimate=pl.CostEstimate(flops=flops, bytes_accessed=nbytes, transcendentals=0),
    )(*args)


def dot(a, b, contract=((1,), (0,))):
    return lax.dot_general(a, b, (contract, ((), ())), preferred_element_type=F32)


def iota(shape, axis):
    return lax.broadcasted_iota(jnp.int32, shape, axis)


def capped_exp(scores):
    return jnp.exp(SOFT_CAP * jnp.tanh(scores * (SCALE / SOFT_CAP)))


def lane_group(shape):
    return lax.shift_right_logical(iota(shape, 1), 5)


def column_of(row):
    n = row.shape[1]
    diagonal = iota((n, n), 0) == iota((n, n), 1)
    return jnp.sum(jnp.where(diagonal, row, 0), axis=1, keepdims=True)


def ask_kernel(vocab, ids_ref, prompt_ref, notes_ref, at_ref, columns_ref, lines_ref):
    def owner_of(ids):
        total = jnp.zeros(ids.shape, jnp.int32)
        for d in range(1, RING):
            total = total + (ids >= d * vocab).astype(jnp.int32)
        return total

    rows = [ids_ref[t : t + 1, :] for t in range(STEPS)]
    column = jnp.concatenate([column_of(row) for row in rows], axis=0)
    owner = owner_of(column)
    base = owner * vocab
    down = iota((TOKENS, ROWS), 0)
    over = iota((TOKENS, ROWS), 1)
    rank = jnp.zeros((TOKENS, ROWS), jnp.int32)
    new_rows = []
    for t in range(STEPS):
        seen = (column == rows[t]) & (down < over + t * ROWS)
        new = 1 - jnp.max(seen.astype(jnp.int32), axis=0, keepdims=True)
        new_rows.append(new)
        rank = rank + jnp.where((rows[t] >= base) & (rows[t] < column), new, 0)
    rank = jnp.sum(rank, axis=1, keepdims=True)
    fits = rank < TAKE
    at_ref[...] = jnp.where(fits, owner * TAKE + rank, -1)
    value = column - base + 1
    cell = jnp.where(fits, rank, -1) == iota((TOKENS, HEAD), 1)
    coarse = jnp.where(cell, lax.shift_right_logical(value, 6), 0).astype(F32).astype(BF16)
    fine = jnp.where(cell, value & 63, 0).astype(F32).astype(BF16)
    holders = iota((RING, ROWS), 0)
    high = jnp.zeros((RING, HEAD), F32)
    low = jnp.zeros((RING, HEAD), F32)
    count = jnp.zeros((RING, ROWS), F32)
    for t in range(STEPS):
        part = slice(t * ROWS, (t + 1) * ROWS)
        mine = jnp.where(owner_of(rows[t]) == holders, new_rows[t], 0).astype(F32)
        count = count + mine
        mine = mine.astype(BF16)
        high = high + dot(mine, coarse[part])
        low = low + dot(mine, fine[part])
    asked = high.astype(jnp.int32) * 64 + low.astype(jnp.int32) - 1

    prompt = prompt_ref[...]
    prompt_column = column_of(prompt)
    holder = lax.shift_right_logical(prompt, 1)
    holder_column = lax.shift_right_logical(prompt_column, 1)
    down = iota((ROWS, ROWS), 0)
    over = iota((ROWS, ROWS), 1)
    same = holder == holder_column
    turn = jnp.sum((same & (down < over)).astype(jnp.int32), axis=0, keepdims=True)
    turn_column = jnp.sum((same & (over < down)).astype(jnp.int32), axis=1, keepdims=True)
    mine = (holder == holders).astype(F32).astype(BF16)
    odd = jnp.where(turn_column + ROOM == iota((ROWS, HEAD), 1), prompt_column & 1, 0)
    odds = dot(mine, odd.astype(F32).astype(BF16)).astype(jnp.int32)
    lane = iota((RING, HEAD), 1)
    notes = jnp.where(lane < ROOM, asked, odds)
    most = jnp.max(rank, axis=0, keepdims=True) + 1
    notes = jnp.where(lane == ENDS, most, notes)
    most = jnp.max(turn_column, axis=0, keepdims=True) + 1
    notes = jnp.where(lane == ENDS + 1, most, notes)
    count = jnp.sum(count, axis=1, keepdims=True).astype(jnp.int32)
    notes = jnp.where(lane == ENDS + 2, count, notes)
    counts = jnp.where(lane == iota((RING, HEAD), 0) + COUNTS, count, 0)
    counts = jnp.sum(counts, axis=0, keepdims=True)
    listed = (lane >= COUNTS) & (lane < COUNTS + RING)
    notes_ref[...] = jnp.where(listed, counts, notes)

    def slots(holder, turn):
        now = jnp.where(turn < SLOT, holder * SLOT + turn, -1)
        later = jnp.where(turn >= SLOT, holder * SLOT + turn - SLOT, -1)
        return now, later

    columns_ref[...] = jnp.concatenate(slots(holder_column, turn_column), axis=1)
    lines_ref[...] = jnp.concatenate(slots(holder, turn), axis=0)


LONG = 20_000_000_000
PIECE = 1024


def pick_kernel(counts_ref, notes_ref, table_ref, out_ref, rows_ref):
    vocab = table_ref.shape[1]
    lane = iota((8, HEAD), 1)
    ids = jnp.zeros((8, ALL), jnp.int32)
    start = 0
    starts = []
    for d in range(RING):
        starts.append(start)
        row = jnp.broadcast_to(notes_ref[d : d + 1, :], (8, HEAD))
        row = jnp.where(lane < ROOM, row + 1, 0)
        row = jnp.concatenate([row, jnp.zeros((8, ALL - HEAD), jnp.int32)], axis=1)
        ids = ids + (pltpu.roll(row, start & (ALL - 1), 1) if d else row)
        start = jnp.minimum(start + counts_ref[d, ENDS + 2], ALL)
    ids = ids[0:1] - 1
    count = ALL
    step = 256
    lines = iota((step, count), 0).astype(F32).astype(BF16)

    def picked(start, rows):
        size = rows.shape[1]
        hots = []
        for at in range(start, start + size, step):
            here = (ids >= at) & (ids < at + step)
            near = jnp.where(here, ids - at, -1).astype(F32).astype(BF16)
            some = lines[: min(step, start + size - at)]
            hots.append(jnp.where(some == near, jnp.ones((), BF16), jnp.zeros((), BF16)))
        return dot(rows, jnp.concatenate(hots, axis=0) if len(hots) > 1 else hots[0])

    total = jnp.zeros((SHARE, count), F32)
    for start in range(0, vocab, PIECE):
        total = total + picked(start, table_ref[:, start : min(start + PIECE, vocab)])
    rows_ref[:ALL, :] = total.T
    rows_ref[ALL:, :] = jnp.zeros((ROOM, SHARE), F32)
    for d in range(RING):
        if d:
            whole_start = pl.multiple_of(starts[d] - (starts[d] & 7), 8)
            some = rows_ref[pl.ds(whole_start, ROOM), :]
            some = pltpu.roll(some, (ROOM - (starts[d] & 7)) & (ROOM - 1), 0)
        else:
            some = rows_ref[:ROOM, :]
        out_ref[d] = some[:TAKE].astype(BF16)


def pack(rows, packed_ref):
    low = rows[:, :HEAD].astype(BF16)
    high = rows[:, HEAD : 2 * HEAD].astype(BF16)
    tail = jnp.concatenate([rows[:, 2 * HEAD :], jnp.zeros((TOKENS, HEAD - TAIL), F32)], axis=1)
    mixed = tail[:ROWS]
    for t in range(1, STEPS):
        mixed = mixed + pltpu.roll(tail[t * ROWS : (t + 1) * ROWS], TAIL * t, 1)
    mixed = mixed.astype(BF16)
    for b in range(RING):
        packed_ref[b, :TOKENS, :] = low
        packed_ref[b, TOKENS : 2 * TOKENS, :] = high
        packed_ref[b, 2 * TOKENS :, :] = mixed


def unpack_kernel(at_ref, got_ref, out_ref, packed_ref):
    hot = (at_ref[...] == iota((TOKENS, RING * TAKE), 1)).astype(F32).astype(BF16)
    rows = dot(hot, got_ref[...])
    out_ref[...] = rows.astype(BF16)
    pack(rows, packed_ref)


def pack_kernel(rows_ref, packed_ref):
    pack(rows_ref[...].astype(F32), packed_ref)


def normed_times(all_ref, gain_ref, weights):
    group = lane_group((ROWS, HEAD))
    squares = jnp.zeros((TOKENS, HEAD), F32)
    tail_squares = jnp.zeros((ROWS, HEAD), F32)
    product = jnp.zeros((TOKENS, 2 * HEAD), F32)
    tail_blocks, tail_weights = [], []
    for b in range(RING):
        low = all_ref[b, :TOKENS, :].astype(F32)
        high = all_ref[b, TOKENS : 2 * TOKENS, :].astype(F32)
        tail = all_ref[b, 2 * TOKENS :, :].astype(F32)
        main_weights, more_weights = weights(b)
        squares = squares + (low * low + high * high)
        tail_squares = tail_squares + tail * tail
        both = jnp.concatenate(
            [
                (low * gain_ref[0, b : b + 1, :]).astype(BF16),
                (high * gain_ref[1, b : b + 1, :]).astype(BF16),
            ],
            axis=1,
        )
        product = product + dot(both, main_weights)
        tail_weights.append(more_weights)
        scaled = tail * gain_ref[2, b : b + 1, :]
        place = b % 4
        if place == 0:
            tail_blocks.append([jnp.zeros((ROWS, HEAD), F32) for _ in range(STEPS)])
        for t in range(STEPS):
            shift = (TAIL * (place - t)) % HEAD
            moved = pltpu.roll(scaled, shift, 1) if shift else scaled
            tail_blocks[-1][t] = jnp.where(group == place, moved, tail_blocks[-1][t])
    tails = jnp.concatenate(
        [jnp.concatenate(block, axis=0).astype(BF16) for block in tail_blocks], axis=1
    )
    product = product + dot(tails, jnp.concatenate(tail_weights, axis=0))
    total = jnp.sum(squares, axis=1, keepdims=True) + jnp.concatenate(
        [
            jnp.sum(jnp.where(group == t, tail_squares, 0.0), axis=1, keepdims=True)
            for t in range(STEPS)
        ],
        axis=0,
    )
    return product * lax.rsqrt(total * (1.0 / D) + EPSILON)


def rotary(u, cos_ref, sin_ref):
    return u * cos_ref[...] + pltpu.roll(u, HEAD // 2, 1) * sin_ref[...]


def query_kernel(all_ref, gain_ref, cos_ref, sin_ref, slot_ref, wq_ref, q_ref, send_ref):
    def weights(b):
        start = b * SHARE
        return wq_ref[start : start + 2 * HEAD, :], wq_ref[start + 2 * HEAD : start + SHARE, :]

    query = normed_times(all_ref, gain_ref, weights)
    turned = jnp.concatenate(
        [
            rotary(query[:, :HEAD], cos_ref, sin_ref).astype(BF16),
            rotary(query[:, HEAD:], cos_ref, sin_ref).astype(BF16),
        ],
        axis=1,
    )
    q_ref[...] = turned
    wide = jnp.concatenate([turned[t * ROWS : (t + 1) * ROWS] for t in range(STEPS)], axis=1)
    hot = (iota((RING * SLOT, ROWS), 0) == slot_ref[0:1, :]).astype(F32).astype(BF16)
    send_ref[...] = dot(hot, wide).astype(BF16)


def place_kernel(q_ref, slot_ref, send_ref):
    turned = q_ref[...]
    wide = jnp.concatenate([turned[t * ROWS : (t + 1) * ROWS] for t in range(STEPS)], axis=1)
    hot = (iota((RING * SLOT, ROWS), 0) == slot_ref[1:2, :]).astype(F32).astype(BF16)
    send_ref[...] = dot(hot, wide).astype(BF16)


def prefix_kernel(turn, own_ref, notes_ref, keys_ref, values_ref, out_ref):
    lanes = iota((RING, SLOT, HEAD), 2) - (ROOM + turn) == iota((RING, SLOT, HEAD), 1)
    notes = jnp.where(lanes, notes_ref[...][:, None, :], 0).reshape(RING * SLOT, HEAD)
    odd = jnp.sum(notes, axis=1, keepdims=True) == 1
    keys = jnp.concatenate([keys_ref[0], keys_ref[1]], axis=1)
    values = jnp.concatenate([values_ref[0], values_ref[1]], axis=1)
    slots = RING * SLOT
    lanes = iota((slots, HEAD), 1)
    denoms = jnp.zeros((slots, HEAD), F32)
    batch = 4
    for first in range(0, PAIRS, batch):
        some = range(first, first + batch)
        parts = []
        for i in some:
            q = own_ref[:, i * HEAD : (i + 1) * HEAD].astype(F32)
            parts.append(
                jnp.concatenate(
                    [jnp.where(odd, 0.0, q).astype(BF16), jnp.where(odd, q, 0.0).astype(BF16)],
                    axis=1,
                )
            )
        scores = dot(jnp.concatenate(parts, axis=0), keys, ((1,), (1,)))
        weights = capped_exp(scores).astype(BF16)
        numer = dot(weights, values)
        denom = jnp.sum(weights.astype(F32), axis=1, keepdims=True)
        for n, i in enumerate(some):
            part = numer[n * slots : (n + 1) * slots]
            out_ref[:, i * HEAD : (i + 1) * HEAD] = jnp.where(
                odd, part[:, HEAD:], part[:, :HEAD]
            ).astype(BF16)
            denoms = jnp.where(lanes == i, denom[n * slots : (n + 1) * slots], denoms)
    out_ref[:, WIDE:] = denoms.astype(BF16)


def local_kernel(
    all_ref, gain_ref, cos_ref, sin_ref, wkv_ref, q_ref, sk_ref, sv_ref, len_ref, out_ref
):
    def weights(b):
        start = b * SHARE
        return [
            jnp.concatenate([wkv_ref[0, rows, :], wkv_ref[1, rows, :]], axis=1)
            for rows in (
                slice(start, start + 2 * HEAD),
                slice(start + 2 * HEAD, start + SHARE),
            )
        ]

    keyval = normed_times(all_ref, gain_ref, weights)
    new_keys = rotary(keyval[:, :HEAD], cos_ref, sin_ref).astype(BF16)
    new_values = keyval[:, HEAD:].astype(BF16)
    suffix = ROWS * SUF
    keys = jnp.concatenate([sk_ref[...], new_keys], axis=0)
    values = jnp.concatenate([sv_ref[...], new_values], axis=0)
    columns = suffix + TOKENS
    column = iota((ROWS, columns), 1)
    row = iota((ROWS, columns), 0)
    first = row * SUF
    in_suffix = (column >= first) & (column < first + len_ref[...])
    lanes = iota((ROWS, HEAD), 1)
    denoms = jnp.zeros((ROWS, HEAD), F32)
    usable = in_suffix
    for t in range(STEPS):
        usable = usable | (column == row + (suffix + t * ROWS))
        for g in range(GROUP):
            i = t * GROUP + g
            q = q_ref[t * ROWS : (t + 1) * ROWS, g * HEAD : (g + 1) * HEAD]
            scores = dot(q, keys, ((1,), (1,)))
            weights = jnp.where(usable, capped_exp(scores), 0.0).astype(BF16)
            out_ref[:, i * HEAD : (i + 1) * HEAD] = dot(weights, values)
            denom = jnp.sum(weights.astype(F32), axis=1, keepdims=True)
            denoms = jnp.where(lanes == i, denom, denoms)
    out_ref[:, WIDE:] = denoms


def select_kernel(slot_ref, back_ref, local_ref, out_ref):
    hot = (slot_ref[:, 1:2] == iota((ROWS, RING * SLOT), 1)).astype(F32).astype(BF16)
    out_ref[...] = dot(hot, back_ref[...]) + local_ref[...]


def output_kernel(slot_ref, back_ref, local_ref, w_ref, out_ref):
    hot = (slot_ref[:, 0:1] == iota((ROWS, RING * SLOT), 1)).astype(F32).astype(BF16)
    total = dot(hot, back_ref[...]) + local_ref[...]
    rows = []
    for t in range(STEPS):
        heads = []
        for g in range(GROUP):
            i = t * GROUP + g
            heads.append(
                (
                    total[:, i * HEAD : (i + 1) * HEAD] / total[:, WIDE + i : WIDE + i + 1]
                ).astype(BF16)
            )
        rows.append(jnp.concatenate(heads, axis=1))
    attended = jnp.concatenate(rows, axis=0)
    lanes = iota((TOKENS, HEAD), 1)
    group = lane_group((ROWS, HEAD))
    quad = 4 * SHARE
    for first in range(0, RING, 4):
        part = dot(attended, w_ref[:, first * SHARE : first * SHARE + quad])
        for i in range(4):
            b = first + i
            tiles = [part[:, (2 * i + n) * HEAD : (2 * i + n + 1) * HEAD] for n in range(3)]
            away = TAIL * i
            if away:
                moved = [pltpu.roll(tile, HEAD - away, 1) for tile in tiles]
                low = jnp.where(lanes < HEAD - away, moved[0], moved[1])
                high = jnp.where(lanes < HEAD - away, moved[1], moved[2])
            else:
                low, high = tiles[0], tiles[1]
            out_ref[b, :TOKENS, :] = low.astype(BF16)
            out_ref[b, TOKENS : 2 * TOKENS, :] = high.astype(BF16)
            mixed = jnp.zeros((ROWS, HEAD), F32)
            for t in range(STEPS):
                tail = tiles[2][t * ROWS : (t + 1) * ROWS]
                shift = (TAIL * (t - i)) % HEAD
                tail = pltpu.roll(tail, shift, 1) if shift else tail
                mixed = jnp.where(group == t, tail, mixed)
            out_ref[b, 2 * TOKENS :, :] = mixed.astype(BF16)


def reduce_kernel(parts_ref, sum_ref, squares_ref):
    total = parts_ref[0].astype(F32)
    for b in range(1, RING):
        total = total + parts_ref[b].astype(F32)
    sum_ref[...] = total
    low, high, tail = total[:TOKENS], total[TOKENS : 2 * TOKENS], total[2 * TOKENS :]
    group = lane_group((ROWS, HEAD))
    squares = jnp.sum(low * low + high * high, axis=1, keepdims=True) + jnp.concatenate(
        [
            jnp.sum(jnp.where(group == t, tail * tail, 0.0), axis=1, keepdims=True)
            for t in range(STEPS)
        ],
        axis=0,
    )
    diagonal = iota((HEAD, HEAD), 0) == iota((HEAD, HEAD), 1)
    one = jnp.sum(jnp.where(diagonal, squares[:HEAD], 0.0), axis=0, keepdims=True)
    rest = TOKENS - HEAD
    two = jnp.sum(jnp.where(diagonal[:rest], squares[HEAD:], 0.0), axis=0, keepdims=True)
    line = jnp.concatenate([one, two], axis=0)
    for b in range(RING):
        squares_ref[b] = line


def scale_kernel(sum_ref, gain_ref, rows_ref, out_ref, wide_ref):
    total = sum_ref[...]
    tails = []
    for t in range(STEPS):
        tail = total[2 * TOKENS :]
        tails.append(pltpu.roll(tail, HEAD - TAIL * t, 1) if t else tail)
    tail = jnp.concatenate(tails, axis=0)[:, :TAIL]
    placed = jnp.concatenate([total[:TOKENS], total[TOKENS : 2 * TOKENS], tail], axis=1)
    out_ref[...] = placed * gain_ref[...]
    wide_ref[...] = rows_ref[...].astype(F32)


def finish_kernel(squares_ref, scaled_ref, wide_ref, out_ref):
    line = squares_ref[0]
    for b in range(1, RING):
        line = line + squares_ref[b]
    line = lax.rsqrt(line * (1.0 / D) + EPSILON)
    diagonal = iota((HEAD, HEAD), 0) == iota((HEAD, HEAD), 1)
    rest = TOKENS - HEAD
    one = jnp.sum(jnp.where(diagonal, line[0:1], 0.0), axis=1, keepdims=True)
    two = jnp.sum(jnp.where(diagonal[:rest], line[1:2], 0.0), axis=1, keepdims=True)
    root = jnp.concatenate([one, two], axis=0)
    out_ref[...] = (wide_ref[...] + scaled_ref[...] * root).astype(BF16)


def exchange(x, axis):
    return lax.all_to_all(x, axis, split_axis=0, concat_axis=0, tiled=True)


def per_device(
    token_ids,
    prompt_of,
    suffix_len,
    table,
    pre_gain,
    w_query,
    w_keyval,
    w_out,
    post_gain,
    prefix_keys,
    prefix_values,
    suffix_keys,
    suffix_values,
):
    vocab = table.shape[0]
    prompt_len = prefix_keys.shape[1]
    shape = jax.ShapeDtypeStruct

    notes, at, slot_columns, slot_lines = call(
        functools.partial(ask_kernel, vocab),
        [
            shape((RING, HEAD), jnp.int32),
            shape((TOKENS, 1), jnp.int32),
            shape((ROWS, 2), jnp.int32),
            shape((2, ROWS), jnp.int32),
        ],
        (token_ids, prompt_of.reshape(1, ROWS)),
        flops=LONG,
    )
    notes = exchange(notes.reshape(RING, 1, HEAD), "prefix").reshape(RING, HEAD)
    ends = jnp.max(notes[:, ENDS : ENDS + 2], axis=0)
    asked = jnp.max(jnp.sum(notes[:, COUNTS : COUNTS + RING], axis=0))
    crowded = (ends[0] > TAKE) | (asked > ALL)

    half = HEAD // 2
    frequency = 10000.0 ** (-(jnp.arange(half, dtype=F32) * 2.0 / HEAD))
    positions = (prompt_len + suffix_len[None, :] + jnp.arange(STEPS)[:, None]).astype(F32)
    angles = positions.reshape(TOKENS, 1) * frequency
    cosines = jnp.cos(angles)
    sines = jnp.sin(angles)
    cosines = jnp.concatenate([cosines, cosines], axis=1)
    sines = jnp.concatenate([-sines, sines], axis=1)
    gains = pre_gain.reshape(RING, SHARE)
    gains = jnp.stack(
        [gains[:, :HEAD], gains[:, HEAD : 2 * HEAD], jnp.tile(gains[:, 2 * HEAD :], (1, 4))]
    )
    lengths = suffix_len.reshape(ROWS, 1)
    notes, cosines, sines, gains, lengths = lax.optimization_barrier(
        (notes, cosines, sines, gains, lengths)
    )
    picked = call(
        pick_kernel,
        shape((RING, TAKE, SHARE), BF16),
        (notes, notes, table.T),
        flops=LONG,
        scalars=1,
        scratch=(pltpu.VMEM((ALL + ROOM, SHARE), F32),),
    )
    got = exchange(picked, "prefix").reshape(RING * TAKE, SHARE)
    own = shape((TOKENS, SHARE), BF16), shape((RING, PACKED, HEAD), BF16)
    placed = tuple(call(unpack_kernel, list(own), (at, got)))

    def take_all(_):
        everyone = exchange(jnp.broadcast_to(token_ids, (RING, STEPS, ROWS)), "prefix")
        inside_at = everyone - lax.axis_index("prefix") * vocab
        inside = (inside_at >= 0) & (inside_at < vocab)
        rows = jnp.take(table, jnp.clip(inside_at, 0, vocab - 1), axis=0)
        rows = jnp.where(inside[..., None], rows, jnp.zeros_like(rows))
        rows = exchange(rows, "prefix").astype(F32).sum(axis=0).astype(BF16)
        rows = rows.reshape(TOKENS, SHARE)
        return rows, call(pack_kernel, own[1], (rows,))

    embedded, packed = lax.cond(crowded, take_all, lambda placed: placed, placed)
    everywhere = exchange(packed, "branch")

    queries, sent = call(
        query_kernel,
        [shape((TOKENS, GROUP * HEAD), BF16), shape((RING * SLOT, WIDE), BF16)],
        (everywhere, gains, cosines, sines, slot_lines, w_query),
        flops=LONG,
    )

    def ask(sent):
        return exchange(sent.reshape(RING, SLOT, WIDE), "prefix").reshape(RING * SLOT, WIDE)

    def answer(own, turn):
        sums = call(
            functools.partial(prefix_kernel, turn),
            shape((RING * SLOT, BACK), BF16),
            (own, notes, prefix_keys, prefix_values),
            flops=8 * RING * SLOT * prompt_len * WIDE,
        )
        return exchange(sums.reshape(RING, SLOT, BACK), "prefix").reshape(RING * SLOT, BACK)

    own = ask(sent)
    local = call(
        local_kernel,
        shape((ROWS, BACK), F32),
        (
            everywhere,
            gains,
            cosines,
            sines,
            w_keyval,
            queries,
            suffix_keys.reshape(ROWS * SUF, HEAD),
            suffix_values.reshape(ROWS * SUF, HEAD),
            lengths,
        ),
        flops=LONG,
    )
    own, local = lax.optimization_barrier((own, local))

    def second_round(local):
        sent = call(
            place_kernel,
            shape((RING * SLOT, WIDE), BF16),
            (queries, slot_lines),
        )
        back = answer(ask(sent), SLOT)
        return call(
            select_kernel,
            shape((ROWS, BACK), F32),
            (slot_columns, back, local),
        )

    local = lax.cond(ends[1] > SLOT, second_round, lambda local: local, local)
    own, local = lax.optimization_barrier((own, local))
    back = answer(own, 0)

    shares = call(
        output_kernel,
        shape((RING, PACKED, HEAD), BF16),
        (slot_columns, back, local, w_out),
        flops=2 * TOKENS * GROUP * HEAD * D,
    )
    shares = exchange(shares, "branch")
    total, squares = call(
        reduce_kernel,
        [shape((PACKED, HEAD), F32), shape((RING, 2, HEAD), F32)],
        (shares,),
    )
    squares = exchange(squares, "branch")
    scaled, wide = call(
        scale_kernel,
        [shape((TOKENS, SHARE), F32)] * 2,
        (total, post_gain.reshape(1, SHARE), embedded),
    )
    layer_out = call(
        finish_kernel,
        shape((TOKENS, SHARE), BF16),
        (squares, scaled, wide),
    )
    return layer_out.reshape(STEPS, ROWS, SHARE)


def solution(mesh):
    placed = (
        P(None, "prefix"),
        P("prefix", None),
        P("prefix"),
        P("prefix", "branch"),
        P(),
        P(None, "branch"),
        P(None, None, "branch"),
        P("branch", None),
        P("branch"),
        P("prefix", None, "branch"),
        P("prefix", None, "branch"),
        P("prefix", None, "branch"),
        P("prefix", None, "branch"),
    )
    return jax.shard_map(
        per_device,
        mesh=mesh,
        in_specs=placed,
        out_specs=P(None, "prefix", "branch"),
        check_vma=False,
    )
```

```python
import functools

import jax
import jax.numpy as jnp
from jax import lax
from jax.experimental import pallas as pl
from jax.experimental.pallas import tpu as pltpu
from jax.sharding import PartitionSpec as P

D = 4608
HEADS = 32
KV_HEADS = 16
HEAD = 128
SUF = 8
SOFT_CAP = 50.0
EPSILON = 1e-06
SCALE = float(D // HEADS) ** (-0.5)

RING = 16
STEPS = 4
ROWS = 48
TOKENS = STEPS * ROWS
SHARE = D // RING
TAIL = SHARE - 2 * HEAD
PACKED = 2 * TOKENS + ROWS
TAKE = 24
ROOM = 32
ENDS = ROOM + 16
COUNTS = 64
ALL = 256
SLOT = 8
GROUP = HEADS // KV_HEADS
PAIRS = STEPS * GROUP
WIDE = PAIRS * HEAD
BACK = WIDE + HEAD

F32 = jnp.float32
BF16 = jnp.bfloat16
VMEM = pl.BlockSpec(memory_space=pltpu.VMEM)
SMEM = pl.BlockSpec(memory_space=pltpu.SMEM)


def call(kernel, out_shape, args, flops=0, scalars=0, scratch=(), limit=24):
    nbytes = sum(a.size * a.dtype.itemsize for a in args)
    many = isinstance(out_shape, (list, tuple))
    return pl.pallas_call(
        kernel,
        out_shape=out_shape,
        in_specs=[SMEM] * scalars + [VMEM] * (len(args) - scalars),
        out_specs=[VMEM] * len(out_shape) if many else VMEM,
        scratch_shapes=list(scratch),
        compiler_params=pltpu.CompilerParams(vmem_limit_bytes=limit * 1024 * 1024),
        cost_estimate=pl.CostEstimate(flops=flops, bytes_accessed=nbytes, transcendentals=0),
    )(*args)


def dot(a, b, contract=((1,), (0,))):
    return lax.dot_general(a, b, (contract, ((), ())), preferred_element_type=F32)


def iota(shape, axis):
    return lax.broadcasted_iota(jnp.int32, shape, axis)


def capped_exp(scores):
    return jnp.exp(SOFT_CAP * jnp.tanh(scores * (SCALE / SOFT_CAP)))


def lane_group(shape):
    return lax.shift_right_logical(iota(shape, 1), 5)


def column_of(row):
    n = row.shape[1]
    diagonal = iota((n, n), 0) == iota((n, n), 1)
    return jnp.sum(jnp.where(diagonal, row, 0), axis=1, keepdims=True)


def ask_kernel(vocab, ids_ref, prompt_ref, notes_ref, at_ref, columns_ref, lines_ref):
    def owner_of(ids):
        total = jnp.zeros(ids.shape, jnp.int32)
        for d in range(1, RING):
            total = total + (ids >= d * vocab).astype(jnp.int32)
        return total

    rows = [ids_ref[t : t + 1, :] for t in range(STEPS)]
    column = jnp.concatenate([column_of(row) for row in rows], axis=0)
    owner = owner_of(column)
    base = owner * vocab
    down = iota((TOKENS, ROWS), 0)
    over = iota((TOKENS, ROWS), 1)
    rank = jnp.zeros((TOKENS, ROWS), jnp.int32)
    new_rows = []
    for t in range(STEPS):
        seen = (column == rows[t]) & (down < over + t * ROWS)
        new = 1 - jnp.max(seen.astype(jnp.int32), axis=0, keepdims=True)
        new_rows.append(new)
        rank = rank + jnp.where((rows[t] >= base) & (rows[t] < column), new, 0)
    rank = jnp.sum(rank, axis=1, keepdims=True)
    fits = rank < TAKE
    at_ref[...] = jnp.where(fits, owner * TAKE + rank, -1)
    value = column - base + 1
    cell = jnp.where(fits, rank, -1) == iota((TOKENS, HEAD), 1)
    coarse = jnp.where(cell, lax.shift_right_logical(value, 6), 0).astype(F32).astype(BF16)
    fine = jnp.where(cell, value & 63, 0).astype(F32).astype(BF16)
    holders = iota((RING, ROWS), 0)
    high = jnp.zeros((RING, HEAD), F32)
    low = jnp.zeros((RING, HEAD), F32)
    count = jnp.zeros((RING, ROWS), F32)
    for t in range(STEPS):
        part = slice(t * ROWS, (t + 1) * ROWS)
        mine = jnp.where(owner_of(rows[t]) == holders, new_rows[t], 0).astype(F32)
        count = count + mine
        mine = mine.astype(BF16)
        high = high + dot(mine, coarse[part])
        low = low + dot(mine, fine[part])
    asked = high.astype(jnp.int32) * 64 + low.astype(jnp.int32) - 1

    prompt = prompt_ref[...]
    prompt_column = column_of(prompt)
    holder = lax.shift_right_logical(prompt, 1)
    holder_column = lax.shift_right_logical(prompt_column, 1)
    down = iota((ROWS, ROWS), 0)
    over = iota((ROWS, ROWS), 1)
    same = holder == holder_column
    turn = jnp.sum((same & (down < over)).astype(jnp.int32), axis=0, keepdims=True)
    turn_column = jnp.sum((same & (over < down)).astype(jnp.int32), axis=1, keepdims=True)
    mine = (holder == holders).astype(F32).astype(BF16)
    odd = jnp.where(turn_column + ROOM == iota((ROWS, HEAD), 1), prompt_column & 1, 0)
    odds = dot(mine, odd.astype(F32).astype(BF16)).astype(jnp.int32)
    lane = iota((RING, HEAD), 1)
    notes = jnp.where(lane < ROOM, asked, odds)
    most = jnp.max(rank, axis=0, keepdims=True) + 1
    notes = jnp.where(lane == ENDS, most, notes)
    most = jnp.max(turn_column, axis=0, keepdims=True) + 1
    notes = jnp.where(lane == ENDS + 1, most, notes)
    count = jnp.sum(count, axis=1, keepdims=True).astype(jnp.int32)
    notes = jnp.where(lane == ENDS + 2, count, notes)
    counts = jnp.where(lane == iota((RING, HEAD), 0) + COUNTS, count, 0)
    counts = jnp.sum(counts, axis=0, keepdims=True)
    listed = (lane >= COUNTS) & (lane < COUNTS + RING)
    notes_ref[...] = jnp.where(listed, counts, notes)

    def slots(holder, turn):
        now = jnp.where(turn < SLOT, holder * SLOT + turn, -1)
        later = jnp.where(turn >= SLOT, holder * SLOT + turn - SLOT, -1)
        return now, later

    columns_ref[...] = jnp.concatenate(slots(holder_column, turn_column), axis=1)
    lines_ref[...] = jnp.concatenate(slots(holder, turn), axis=0)


LONG = 20_000_000_000
PIECE = 1024


def pick_kernel(counts_ref, notes_ref, table_ref, out_ref, rows_ref):
    vocab = table_ref.shape[1]
    lane = iota((8, HEAD), 1)
    ids = jnp.zeros((8, ALL), jnp.int32)
    start = 0
    starts = []
    for d in range(RING):
        starts.append(start)
        row = jnp.broadcast_to(notes_ref[d : d + 1, :], (8, HEAD))
        row = jnp.where(lane < ROOM, row + 1, 0)
        row = jnp.concatenate([row, jnp.zeros((8, ALL - HEAD), jnp.int32)], axis=1)
        ids = ids + (pltpu.roll(row, start & (ALL - 1), 1) if d else row)
        start = jnp.minimum(start + counts_ref[d, ENDS + 2], ALL)
    ids = ids[0:1] - 1
    count = ALL
    step = 256
    lines = iota((step, count), 0).astype(F32).astype(BF16)

    def picked(start, rows):
        size = rows.shape[1]
        hots = []
        for at in range(start, start + size, step):
            here = (ids >= at) & (ids < at + step)
            near = jnp.where(here, ids - at, -1).astype(F32).astype(BF16)
            some = lines[: min(step, start + size - at)]
            hots.append(jnp.where(some == near, jnp.ones((), BF16), jnp.zeros((), BF16)))
        return dot(rows, jnp.concatenate(hots, axis=0) if len(hots) > 1 else hots[0])

    total = jnp.zeros((SHARE, count), F32)
    for start in range(0, vocab, PIECE):
        total = total + picked(start, table_ref[:, start : min(start + PIECE, vocab)])
    rows_ref[:ALL, :] = total.T
    rows_ref[ALL:, :] = jnp.zeros((ROOM, SHARE), F32)
    for d in range(RING):
        if d:
            whole_start = pl.multiple_of(starts[d] - (starts[d] & 7), 8)
            some = rows_ref[pl.ds(whole_start, ROOM), :]
            some = pltpu.roll(some, (ROOM - (starts[d] & 7)) & (ROOM - 1), 0)
        else:
            some = rows_ref[:ROOM, :]
        out_ref[d] = some[:TAKE].astype(BF16)


def pack(rows, packed_ref):
    low = rows[:, :HEAD].astype(BF16)
    high = rows[:, HEAD : 2 * HEAD].astype(BF16)
    tail = jnp.concatenate([rows[:, 2 * HEAD :], jnp.zeros((TOKENS, HEAD - TAIL), F32)], axis=1)
    mixed = tail[:ROWS]
    for t in range(1, STEPS):
        mixed = mixed + pltpu.roll(tail[t * ROWS : (t + 1) * ROWS], TAIL * t, 1)
    mixed = mixed.astype(BF16)
    for b in range(RING):
        packed_ref[b, :TOKENS, :] = low
        packed_ref[b, TOKENS : 2 * TOKENS, :] = high
        packed_ref[b, 2 * TOKENS :, :] = mixed


def unpack_kernel(at_ref, got_ref, out_ref, packed_ref):
    hot = (at_ref[...] == iota((TOKENS, RING * TAKE), 1)).astype(F32).astype(BF16)
    rows = dot(hot, got_ref[...])
    out_ref[...] = rows.astype(BF16)
    pack(rows, packed_ref)


def pack_kernel(rows_ref, packed_ref):
    pack(rows_ref[...].astype(F32), packed_ref)


def normed_times(all_ref, gain_ref, weights):
    group = lane_group((ROWS, HEAD))
    squares = jnp.zeros((TOKENS, HEAD), F32)
    tail_squares = jnp.zeros((ROWS, HEAD), F32)
    product = jnp.zeros((TOKENS, 2 * HEAD), F32)
    tail_blocks, tail_weights = [], []
    for b in range(RING):
        low = all_ref[b, :TOKENS, :].astype(F32)
        high = all_ref[b, TOKENS : 2 * TOKENS, :].astype(F32)
        tail = all_ref[b, 2 * TOKENS :, :].astype(F32)
        main_weights, more_weights = weights(b)
        squares = squares + (low * low + high * high)
        tail_squares = tail_squares + tail * tail
        both = jnp.concatenate(
            [
                (low * gain_ref[0, b : b + 1, :]).astype(BF16),
                (high * gain_ref[1, b : b + 1, :]).astype(BF16),
            ],
            axis=1,
        )
        product = product + dot(both, main_weights)
        tail_weights.append(more_weights)
        scaled = tail * gain_ref[2, b : b + 1, :]
        place = b % 4
        if place == 0:
            tail_blocks.append([jnp.zeros((ROWS, HEAD), F32) for _ in range(STEPS)])
        for t in range(STEPS):
            shift = (TAIL * (place - t)) % HEAD
            moved = pltpu.roll(scaled, shift, 1) if shift else scaled
            tail_blocks[-1][t] = jnp.where(group == place, moved, tail_blocks[-1][t])
    tails = jnp.concatenate(
        [jnp.concatenate(block, axis=0).astype(BF16) for block in tail_blocks], axis=1
    )
    product = product + dot(tails, jnp.concatenate(tail_weights, axis=0))
    total = jnp.sum(squares, axis=1, keepdims=True) + jnp.concatenate(
        [
            jnp.sum(jnp.where(group == t, tail_squares, 0.0), axis=1, keepdims=True)
            for t in range(STEPS)
        ],
        axis=0,
    )
    return product * lax.rsqrt(total * (1.0 / D) + EPSILON)


def rotary(u, cos_ref, sin_ref):
    return u * cos_ref[...] + pltpu.roll(u, HEAD // 2, 1) * sin_ref[...]


def query_kernel(all_ref, gain_ref, cos_ref, sin_ref, slot_ref, wq_ref, q_ref, send_ref):
    def weights(b):
        start = b * SHARE
        return wq_ref[start : start + 2 * HEAD, :], wq_ref[start + 2 * HEAD : start + SHARE, :]

    query = normed_times(all_ref, gain_ref, weights)
    turned = jnp.concatenate(
        [
            rotary(query[:, :HEAD], cos_ref, sin_ref).astype(BF16),
            rotary(query[:, HEAD:], cos_ref, sin_ref).astype(BF16),
        ],
        axis=1,
    )
    q_ref[...] = turned
    wide = jnp.concatenate([turned[t * ROWS : (t + 1) * ROWS] for t in range(STEPS)], axis=1)
    hot = (iota((RING * SLOT, ROWS), 0) == slot_ref[0:1, :]).astype(F32).astype(BF16)
    send_ref[...] = dot(hot, wide).astype(BF16)


def place_kernel(q_ref, slot_ref, send_ref):
    turned = q_ref[...]
    wide = jnp.concatenate([turned[t * ROWS : (t + 1) * ROWS] for t in range(STEPS)], axis=1)
    hot = (iota((RING * SLOT, ROWS), 0) == slot_ref[1:2, :]).astype(F32).astype(BF16)
    send_ref[...] = dot(hot, wide).astype(BF16)


def prefix_kernel(turn, own_ref, notes_ref, keys_ref, values_ref, out_ref):
    lanes = iota((RING, SLOT, HEAD), 2) - (ROOM + turn) == iota((RING, SLOT, HEAD), 1)
    notes = jnp.where(lanes, notes_ref[...][:, None, :], 0).reshape(RING * SLOT, HEAD)
    odd = jnp.sum(notes, axis=1, keepdims=True) == 1
    keys = jnp.concatenate([keys_ref[0], keys_ref[1]], axis=1)
    values = jnp.concatenate([values_ref[0], values_ref[1]], axis=1)
    slots = RING * SLOT
    lanes = iota((slots, HEAD), 1)
    denoms = jnp.zeros((slots, HEAD), F32)
    batch = 4
    for first in range(0, PAIRS, batch):
        some = range(first, first + batch)
        parts = []
        for i in some:
            q = own_ref[:, i * HEAD : (i + 1) * HEAD].astype(F32)
            parts.append(
                jnp.concatenate(
                    [jnp.where(odd, 0.0, q).astype(BF16), jnp.where(odd, q, 0.0).astype(BF16)],
                    axis=1,
                )
            )
        scores = dot(jnp.concatenate(parts, axis=0), keys, ((1,), (1,)))
        weights = capped_exp(scores).astype(BF16)
        numer = dot(weights, values)
        denom = jnp.sum(weights.astype(F32), axis=1, keepdims=True)
        for n, i in enumerate(some):
            part = numer[n * slots : (n + 1) * slots]
            out_ref[:, i * HEAD : (i + 1) * HEAD] = jnp.where(
                odd, part[:, HEAD:], part[:, :HEAD]
            ).astype(BF16)
            denoms = jnp.where(lanes == i, denom[n * slots : (n + 1) * slots], denoms)
    out_ref[:, WIDE:] = denoms.astype(BF16)


def local_kernel(
    all_ref, gain_ref, cos_ref, sin_ref, wkv_ref, q_ref, sk_ref, sv_ref, len_ref, out_ref
):
    def weights(b):
        start = b * SHARE
        return [
            jnp.concatenate([wkv_ref[0, rows, :], wkv_ref[1, rows, :]], axis=1)
            for rows in (
                slice(start, start + 2 * HEAD),
                slice(start + 2 * HEAD, start + SHARE),
            )
        ]

    keyval = normed_times(all_ref, gain_ref, weights)
    new_keys = rotary(keyval[:, :HEAD], cos_ref, sin_ref).astype(BF16)
    new_values = keyval[:, HEAD:].astype(BF16)
    suffix = ROWS * SUF
    keys = jnp.concatenate([sk_ref[...], new_keys], axis=0)
    values = jnp.concatenate([sv_ref[...], new_values], axis=0)
    columns = suffix + TOKENS
    column = iota((ROWS, columns), 1)
    row = iota((ROWS, columns), 0)
    first = row * SUF
    in_suffix = (column >= first) & (column < first + len_ref[...])
    lanes = iota((ROWS, HEAD), 1)
    denoms = jnp.zeros((ROWS, HEAD), F32)
    usable = in_suffix
    for t in range(STEPS):
        usable = usable | (column == row + (suffix + t * ROWS))
        for g in range(GROUP):
            i = t * GROUP + g
            q = q_ref[t * ROWS : (t + 1) * ROWS, g * HEAD : (g + 1) * HEAD]
            scores = dot(q, keys, ((1,), (1,)))
            weights = jnp.where(usable, capped_exp(scores), 0.0).astype(BF16)
            out_ref[:, i * HEAD : (i + 1) * HEAD] = dot(weights, values)
            denom = jnp.sum(weights.astype(F32), axis=1, keepdims=True)
            denoms = jnp.where(lanes == i, denom, denoms)
    out_ref[:, WIDE:] = denoms


def select_kernel(slot_ref, back_ref, local_ref, out_ref):
    hot = (slot_ref[:, 1:2] == iota((ROWS, RING * SLOT), 1)).astype(F32).astype(BF16)
    out_ref[...] = dot(hot, back_ref[...]) + local_ref[...]


def output_kernel(slot_ref, back_ref, local_ref, w_ref, out_ref):
    hot = (slot_ref[:, 0:1] == iota((ROWS, RING * SLOT), 1)).astype(F32).astype(BF16)
    total = dot(hot, back_ref[...]) + local_ref[...]
    rows = []
    for t in range(STEPS):
        heads = []
        for g in range(GROUP):
            i = t * GROUP + g
            heads.append(
                (
                    total[:, i * HEAD : (i + 1) * HEAD] / total[:, WIDE + i : WIDE + i + 1]
                ).astype(BF16)
            )
        rows.append(jnp.concatenate(heads, axis=1))
    attended = jnp.concatenate(rows, axis=0)
    lanes = iota((TOKENS, HEAD), 1)
    group = lane_group((ROWS, HEAD))
    quad = 4 * SHARE
    for first in range(0, RING, 4):
        part = dot(attended, w_ref[:, first * SHARE : first * SHARE + quad])
        for i in range(4):
            b = first + i
            tiles = [part[:, (2 * i + n) * HEAD : (2 * i + n + 1) * HEAD] for n in range(3)]
            away = TAIL * i
            if away:
                moved = [pltpu.roll(tile, HEAD - away, 1) for tile in tiles]
                low = jnp.where(lanes < HEAD - away, moved[0], moved[1])
                high = jnp.where(lanes < HEAD - away, moved[1], moved[2])
            else:
                low, high = tiles[0], tiles[1]
            out_ref[b, :TOKENS, :] = low.astype(BF16)
            out_ref[b, TOKENS : 2 * TOKENS, :] = high.astype(BF16)
            mixed = jnp.zeros((ROWS, HEAD), F32)
            for t in range(STEPS):
                tail = tiles[2][t * ROWS : (t + 1) * ROWS]
                shift = (TAIL * (t - i)) % HEAD
                tail = pltpu.roll(tail, shift, 1) if shift else tail
                mixed = jnp.where(group == t, tail, mixed)
            out_ref[b, 2 * TOKENS :, :] = mixed.astype(BF16)


def reduce_kernel(parts_ref, sum_ref, squares_ref):
    total = parts_ref[0].astype(F32)
    for b in range(1, RING):
        total = total + parts_ref[b].astype(F32)
    sum_ref[...] = total
    low, high, tail = total[:TOKENS], total[TOKENS : 2 * TOKENS], total[2 * TOKENS :]
    group = lane_group((ROWS, HEAD))
    squares = jnp.sum(low * low + high * high, axis=1, keepdims=True) + jnp.concatenate(
        [
            jnp.sum(jnp.where(group == t, tail * tail, 0.0), axis=1, keepdims=True)
            for t in range(STEPS)
        ],
        axis=0,
    )
    diagonal = iota((HEAD, HEAD), 0) == iota((HEAD, HEAD), 1)
    one = jnp.sum(jnp.where(diagonal, squares[:HEAD], 0.0), axis=0, keepdims=True)
    rest = TOKENS - HEAD
    two = jnp.sum(jnp.where(diagonal[:rest], squares[HEAD:], 0.0), axis=0, keepdims=True)
    line = jnp.concatenate([one, two], axis=0)
    for b in range(RING):
        squares_ref[b] = line


def scale_kernel(sum_ref, gain_ref, rows_ref, out_ref, wide_ref):
    total = sum_ref[...]
    tails = []
    for t in range(STEPS):
        tail = total[2 * TOKENS :]
        tails.append(pltpu.roll(tail, HEAD - TAIL * t, 1) if t else tail)
    tail = jnp.concatenate(tails, axis=0)[:, :TAIL]
    placed = jnp.concatenate([total[:TOKENS], total[TOKENS : 2 * TOKENS], tail], axis=1)
    out_ref[...] = placed * gain_ref[...]
    wide_ref[...] = rows_ref[...].astype(F32)


def finish_kernel(squares_ref, scaled_ref, wide_ref, out_ref):
    line = squares_ref[0]
    for b in range(1, RING):
        line = line + squares_ref[b]
    line = lax.rsqrt(line * (1.0 / D) + EPSILON)
    diagonal = iota((HEAD, HEAD), 0) == iota((HEAD, HEAD), 1)
    rest = TOKENS - HEAD
    one = jnp.sum(jnp.where(diagonal, line[0:1], 0.0), axis=1, keepdims=True)
    two = jnp.sum(jnp.where(diagonal[:rest], line[1:2], 0.0), axis=1, keepdims=True)
    root = jnp.concatenate([one, two], axis=0)
    out_ref[...] = (wide_ref[...] + scaled_ref[...] * root).astype(BF16)


def exchange(x, axis):
    return lax.all_to_all(x, axis, split_axis=0, concat_axis=0, tiled=True)


def per_device(
    token_ids,
    prompt_of,
    suffix_len,
    table,
    pre_gain,
    w_query,
    w_keyval,
    w_out,
    post_gain,
    prefix_keys,
    prefix_values,
    suffix_keys,
    suffix_values,
):
    vocab = table.shape[0]
    prompt_len = prefix_keys.shape[1]
    shape = jax.ShapeDtypeStruct

    notes, at, slot_columns, slot_lines = call(
        functools.partial(ask_kernel, vocab),
        [
            shape((RING, HEAD), jnp.int32),
            shape((TOKENS, 1), jnp.int32),
            shape((ROWS, 2), jnp.int32),
            shape((2, ROWS), jnp.int32),
        ],
        (token_ids, prompt_of.reshape(1, ROWS)),
        flops=LONG,
    )
    notes = exchange(notes.reshape(RING, 1, HEAD), "prefix").reshape(RING, HEAD)
    ends = jnp.max(notes[:, ENDS : ENDS + 2], axis=0)
    asked = jnp.max(jnp.sum(notes[:, COUNTS : COUNTS + RING], axis=0))
    crowded = (ends[0] > TAKE) | (asked > ALL)

    half = HEAD // 2
    frequency = 10000.0 ** (-(jnp.arange(half, dtype=F32) * 2.0 / HEAD))
    positions = (prompt_len + suffix_len[None, :] + jnp.arange(STEPS)[:, None]).astype(F32)
    angles = positions.reshape(TOKENS, 1) * frequency
    cosines = jnp.cos(angles)
    sines = jnp.sin(angles)
    cosines = jnp.concatenate([cosines, cosines], axis=1)
    sines = jnp.concatenate([-sines, sines], axis=1)
    gains = pre_gain.reshape(RING, SHARE)
    gains = jnp.stack(
        [gains[:, :HEAD], gains[:, HEAD : 2 * HEAD], jnp.tile(gains[:, 2 * HEAD :], (1, 4))]
    )
    notes, cosines, sines, gains = lax.optimization_barrier((notes, cosines, sines, gains))
    picked = call(
        pick_kernel,
        shape((RING, TAKE, SHARE), BF16),
        (notes, notes, table.T),
        flops=LONG,
        scalars=1,
        scratch=(pltpu.VMEM((ALL + ROOM, SHARE), F32),),
    )
    got = exchange(picked, "prefix").reshape(RING * TAKE, SHARE)
    own = shape((TOKENS, SHARE), BF16), shape((RING, PACKED, HEAD), BF16)
    placed = tuple(call(unpack_kernel, list(own), (at, got), flops=LONG))

    def take_all(_):
        everyone = exchange(jnp.broadcast_to(token_ids, (RING, STEPS, ROWS)), "prefix")
        inside_at = everyone - lax.axis_index("prefix") * vocab
        inside = (inside_at >= 0) & (inside_at < vocab)
        rows = jnp.take(table, jnp.clip(inside_at, 0, vocab - 1), axis=0)
        rows = jnp.where(inside[..., None], rows, jnp.zeros_like(rows))
        rows = exchange(rows, "prefix").astype(F32).sum(axis=0).astype(BF16)
        rows = rows.reshape(TOKENS, SHARE)
        return rows, call(pack_kernel, own[1], (rows,))

    embedded, packed = lax.cond(crowded, take_all, lambda placed: placed, placed)
    everywhere = exchange(packed, "branch")

    queries, sent = call(
        query_kernel,
        [shape((TOKENS, GROUP * HEAD), BF16), shape((RING * SLOT, WIDE), BF16)],
        (everywhere, gains, cosines, sines, slot_lines, w_query),
        flops=LONG,
    )

    queries, lengths, ends = lax.optimization_barrier((queries, suffix_len, ends))

    def ask(sent):
        return exchange(sent.reshape(RING, SLOT, WIDE), "prefix").reshape(RING * SLOT, WIDE)

    def answer(own, turn):
        sums = call(
            functools.partial(prefix_kernel, turn),
            shape((RING * SLOT, BACK), BF16),
            (own, notes, prefix_keys, prefix_values),
            flops=8 * RING * SLOT * prompt_len * WIDE,
        )
        return exchange(sums.reshape(RING, SLOT, BACK), "prefix").reshape(RING * SLOT, BACK)

    own = ask(sent)
    local = call(
        local_kernel,
        shape((ROWS, BACK), F32),
        (
            everywhere,
            gains,
            cosines,
            sines,
            w_keyval,
            queries,
            suffix_keys.reshape(ROWS * SUF, HEAD),
            suffix_values.reshape(ROWS * SUF, HEAD),
            lengths.reshape(ROWS, 1),
        ),
        flops=LONG,
    )
    own, local = lax.optimization_barrier((own, local))

    def second_round(local):
        sent = call(
            place_kernel,
            shape((RING * SLOT, WIDE), BF16),
            (queries, slot_lines),
        )
        back = answer(ask(sent), SLOT)
        return call(
            select_kernel,
            shape((ROWS, BACK), F32),
            (slot_columns, back, local),
        )

    local = lax.cond(ends[1] > SLOT, second_round, lambda local: local, local)
    own, local = lax.optimization_barrier((own, local))
    back = answer(own, 0)

    shares = call(
        output_kernel,
        shape((RING, PACKED, HEAD), BF16),
        (slot_columns, back, local, w_out),
        flops=2 * TOKENS * GROUP * HEAD * D,
    )
    shares = exchange(shares, "branch")
    total, squares = call(
        reduce_kernel,
        [shape((PACKED, HEAD), F32), shape((RING, 2, HEAD), F32)],
        (shares,),
    )
    squares = exchange(squares, "branch")
    scaled, wide = call(
        scale_kernel,
        [shape((TOKENS, SHARE), F32)] * 2,
        (total, post_gain.reshape(1, SHARE), embedded),
    )
    layer_out = call(
        finish_kernel,
        shape((TOKENS, SHARE), BF16),
        (squares, scaled, wide),
    )
    return layer_out.reshape(STEPS, ROWS, SHARE)


def solution(mesh):
    placed = (
        P(None, "prefix"),
        P("prefix", None),
        P("prefix"),
        P("prefix", "branch"),
        P(),
        P(None, "branch"),
        P(None, None, "branch"),
        P("branch", None),
        P("branch"),
        P("prefix", None, "branch"),
        P("prefix", None, "branch"),
        P("prefix", None, "branch"),
        P("prefix", None, "branch"),
    )
    return jax.shard_map(
        per_device,
        mesh=mesh,
        in_specs=placed,
        out_specs=P(None, "prefix", "branch"),
        check_vma=False,
    )
```

```python
import functools

import jax
import jax.numpy as jnp
from jax import lax
from jax.experimental import pallas as pl
from jax.experimental.pallas import tpu as pltpu
from jax.sharding import PartitionSpec as P

D = 4608
HEADS = 32
KV_HEADS = 16
HEAD = 128
SUF = 8
SOFT_CAP = 50.0
EPSILON = 1e-06
SCALE = float(D // HEADS) ** (-0.5)

RING = 16
STEPS = 4
ROWS = 48
TOKENS = STEPS * ROWS
SHARE = D // RING
TAIL = SHARE - 2 * HEAD
PACKED = 2 * TOKENS + ROWS
TAKE = 24
ROOM = 32
ENDS = ROOM + 16
COUNTS = 64
ALL = 256
SLOT = 8
GROUP = HEADS // KV_HEADS
PAIRS = STEPS * GROUP
WIDE = PAIRS * HEAD
BACK = WIDE + HEAD

F32 = jnp.float32
BF16 = jnp.bfloat16
VMEM = pl.BlockSpec(memory_space=pltpu.VMEM)
SMEM = pl.BlockSpec(memory_space=pltpu.SMEM)
ANY = pl.BlockSpec(memory_space=pl.ANY)


def call(kernel, out_shape, args, flops=0, scalars=0, left=(), scratch=(), limit=24):
    nbytes = sum(a.size * a.dtype.itemsize for a in args)
    many = isinstance(out_shape, (list, tuple))
    return pl.pallas_call(
        kernel,
        out_shape=out_shape,
        in_specs=[
            SMEM if n < scalars else ANY if n in left else VMEM for n in range(len(args))
        ],
        out_specs=[VMEM] * len(out_shape) if many else VMEM,
        scratch_shapes=list(scratch),
        compiler_params=pltpu.CompilerParams(vmem_limit_bytes=limit * 1024 * 1024),
        cost_estimate=pl.CostEstimate(flops=flops, bytes_accessed=nbytes, transcendentals=0),
    )(*args)


def dot(a, b, contract=((1,), (0,))):
    return lax.dot_general(a, b, (contract, ((), ())), preferred_element_type=F32)


def iota(shape, axis):
    return lax.broadcasted_iota(jnp.int32, shape, axis)


def capped_exp(scores):
    return jnp.exp(SOFT_CAP * jnp.tanh(scores * (SCALE / SOFT_CAP)))


def lane_group(shape):
    return lax.shift_right_logical(iota(shape, 1), 5)


def column_of(row):
    n = row.shape[1]
    diagonal = iota((n, n), 0) == iota((n, n), 1)
    return jnp.sum(jnp.where(diagonal, row, 0), axis=1, keepdims=True)


def ask_kernel(vocab, ids_ref, prompt_ref, notes_ref, at_ref, columns_ref, lines_ref):
    def owner_of(ids):
        total = jnp.zeros(ids.shape, jnp.int32)
        for d in range(1, RING):
            total = total + (ids >= d * vocab).astype(jnp.int32)
        return total

    rows = [ids_ref[t : t + 1, :] for t in range(STEPS)]
    column = jnp.concatenate([column_of(row) for row in rows], axis=0)
    owner = owner_of(column)
    base = owner * vocab
    down = iota((TOKENS, ROWS), 0)
    over = iota((TOKENS, ROWS), 1)
    rank = jnp.zeros((TOKENS, ROWS), jnp.int32)
    new_rows = []
    for t in range(STEPS):
        seen = (column == rows[t]) & (down < over + t * ROWS)
        new = 1 - jnp.max(seen.astype(jnp.int32), axis=0, keepdims=True)
        new_rows.append(new)
        rank = rank + jnp.where((rows[t] >= base) & (rows[t] < column), new, 0)
    rank = jnp.sum(rank, axis=1, keepdims=True)
    fits = rank < TAKE
    at_ref[...] = jnp.where(fits, owner * TAKE + rank, -1)
    value = column - base + 1
    cell = jnp.where(fits, rank, -1) == iota((TOKENS, HEAD), 1)
    coarse = jnp.where(cell, lax.shift_right_logical(value, 6), 0).astype(F32).astype(BF16)
    fine = jnp.where(cell, value & 63, 0).astype(F32).astype(BF16)
    holders = iota((RING, ROWS), 0)
    high = jnp.zeros((RING, HEAD), F32)
    low = jnp.zeros((RING, HEAD), F32)
    count = jnp.zeros((RING, ROWS), F32)
    for t in range(STEPS):
        part = slice(t * ROWS, (t + 1) * ROWS)
        mine = jnp.where(owner_of(rows[t]) == holders, new_rows[t], 0).astype(F32)
        count = count + mine
        mine = mine.astype(BF16)
        high = high + dot(mine, coarse[part])
        low = low + dot(mine, fine[part])
    asked = high.astype(jnp.int32) * 64 + low.astype(jnp.int32) - 1

    prompt = prompt_ref[...]
    prompt_column = column_of(prompt)
    holder = lax.shift_right_logical(prompt, 1)
    holder_column = lax.shift_right_logical(prompt_column, 1)
    down = iota((ROWS, ROWS), 0)
    over = iota((ROWS, ROWS), 1)
    same = holder == holder_column
    turn = jnp.sum((same & (down < over)).astype(jnp.int32), axis=0, keepdims=True)
    turn_column = jnp.sum((same & (over < down)).astype(jnp.int32), axis=1, keepdims=True)
    mine = (holder == holders).astype(F32).astype(BF16)
    odd = jnp.where(turn_column + ROOM == iota((ROWS, HEAD), 1), prompt_column & 1, 0)
    odds = dot(mine, odd.astype(F32).astype(BF16)).astype(jnp.int32)
    lane = iota((RING, HEAD), 1)
    notes = jnp.where(lane < ROOM, asked, odds)
    most = jnp.max(rank, axis=0, keepdims=True) + 1
    notes = jnp.where(lane == ENDS, most, notes)
    most = jnp.max(turn_column, axis=0, keepdims=True) + 1
    notes = jnp.where(lane == ENDS + 1, most, notes)
    count = jnp.sum(count, axis=1, keepdims=True).astype(jnp.int32)
    notes = jnp.where(lane == ENDS + 2, count, notes)
    counts = jnp.where(lane == iota((RING, HEAD), 0) + COUNTS, count, 0)
    counts = jnp.sum(counts, axis=0, keepdims=True)
    listed = (lane >= COUNTS) & (lane < COUNTS + RING)
    notes_ref[...] = jnp.where(listed, counts, notes)

    def slots(holder, turn):
        now = jnp.where(turn < SLOT, holder * SLOT + turn, -1)
        later = jnp.where(turn >= SLOT, holder * SLOT + turn - SLOT, -1)
        return now, later

    columns_ref[...] = jnp.concatenate(slots(holder_column, turn_column), axis=1)
    lines_ref[...] = jnp.concatenate(slots(holder, turn), axis=0)


LONG = 20_000_000_000
PIECE = 2048


def pick_kernel(counts_ref, notes_ref, table_ref, out_ref, rows_ref, hot_ref, held_ref, done):
    fetch = pltpu.make_async_copy(table_ref, held_ref, done)
    fetch.start()
    vocab = table_ref.shape[1]
    lane = iota((8, HEAD), 1)
    ids = jnp.zeros((8, ALL), jnp.int32)
    start = 0
    starts = []
    for d in range(RING):
        starts.append(start)
        row = jnp.broadcast_to(notes_ref[d : d + 1, :], (8, HEAD))
        row = jnp.where(lane < ROOM, row + 1, 0)
        row = jnp.concatenate([row, jnp.zeros((8, ALL - HEAD), jnp.int32)], axis=1)
        ids = ids + (pltpu.roll(row, start & (ALL - 1), 1) if d else row)
        start = jnp.minimum(start + counts_ref[d, ENDS + 2], ALL)
    ids = ids[0:1] - 1
    count = ALL
    step = 256
    lines = iota((step, count), 0).astype(F32).astype(BF16)

    for start in range(0, vocab, step):
        size = min(step, vocab - start)
        here = (ids >= start) & (ids < start + step)
        near = jnp.where(here, ids - start, -1).astype(F32).astype(BF16)
        hot = jnp.where(lines[:size] == near, jnp.ones((), BF16), jnp.zeros((), BF16))
        hot_ref[start : start + size, :] = hot
    fetch.wait()
    total = jnp.zeros((SHARE, count), F32)
    for start in range(0, vocab, PIECE):
        part = slice(start, min(start + PIECE, vocab))
        total = total + dot(held_ref[:, part], hot_ref[part, :])
    rows_ref[:ALL, :] = total.T
    rows_ref[ALL:, :] = jnp.zeros((ROOM, SHARE), F32)
    for d in range(RING):
        if d:
            whole_start = pl.multiple_of(starts[d] - (starts[d] & 7), 8)
            some = rows_ref[pl.ds(whole_start, ROOM), :]
            some = pltpu.roll(some, (ROOM - (starts[d] & 7)) & (ROOM - 1), 0)
        else:
            some = rows_ref[:ROOM, :]
        out_ref[d] = some[:TAKE].astype(BF16)


def pack(rows, packed_ref):
    low = rows[:, :HEAD].astype(BF16)
    high = rows[:, HEAD : 2 * HEAD].astype(BF16)
    tail = jnp.concatenate([rows[:, 2 * HEAD :], jnp.zeros((TOKENS, HEAD - TAIL), F32)], axis=1)
    mixed = tail[:ROWS]
    for t in range(1, STEPS):
        mixed = mixed + pltpu.roll(tail[t * ROWS : (t + 1) * ROWS], TAIL * t, 1)
    mixed = mixed.astype(BF16)
    for b in range(RING):
        packed_ref[b, :TOKENS, :] = low
        packed_ref[b, TOKENS : 2 * TOKENS, :] = high
        packed_ref[b, 2 * TOKENS :, :] = mixed


def unpack_kernel(at_ref, got_ref, out_ref, packed_ref):
    hot = (at_ref[...] == iota((TOKENS, RING * TAKE), 1)).astype(F32).astype(BF16)
    rows = dot(hot, got_ref[...])
    out_ref[...] = rows.astype(BF16)
    pack(rows, packed_ref)


def normed_times(all_ref, gain_ref, weights):
    group = lane_group((ROWS, HEAD))
    squares = jnp.zeros((TOKENS, HEAD), F32)
    tail_squares = jnp.zeros((ROWS, HEAD), F32)
    product = jnp.zeros((TOKENS, 2 * HEAD), F32)
    tail_blocks, tail_weights = [], []
    for b in range(RING):
        low = all_ref[b, :TOKENS, :].astype(F32)
        high = all_ref[b, TOKENS : 2 * TOKENS, :].astype(F32)
        tail = all_ref[b, 2 * TOKENS :, :].astype(F32)
        main_weights, more_weights = weights(b)
        squares = squares + (low * low + high * high)
        tail_squares = tail_squares + tail * tail
        both = jnp.concatenate(
            [
                (low * gain_ref[0, b : b + 1, :]).astype(BF16),
                (high * gain_ref[1, b : b + 1, :]).astype(BF16),
            ],
            axis=1,
        )
        product = product + dot(both, main_weights)
        tail_weights.append(more_weights)
        scaled = tail * gain_ref[2, b : b + 1, :]
        place = b % 4
        if place == 0:
            tail_blocks.append([jnp.zeros((ROWS, HEAD), F32) for _ in range(STEPS)])
        for t in range(STEPS):
            shift = (TAIL * (place - t)) % HEAD
            moved = pltpu.roll(scaled, shift, 1) if shift else scaled
            tail_blocks[-1][t] = jnp.where(group == place, moved, tail_blocks[-1][t])
    tails = jnp.concatenate(
        [jnp.concatenate(block, axis=0).astype(BF16) for block in tail_blocks], axis=1
    )
    product = product + dot(tails, jnp.concatenate(tail_weights, axis=0))
    total = jnp.sum(squares, axis=1, keepdims=True) + jnp.concatenate(
        [
            jnp.sum(jnp.where(group == t, tail_squares, 0.0), axis=1, keepdims=True)
            for t in range(STEPS)
        ],
        axis=0,
    )
    return product * lax.rsqrt(total * (1.0 / D) + EPSILON)


def rotary(u, cos_ref, sin_ref):
    return u * cos_ref[...] + pltpu.roll(u, HEAD // 2, 1) * sin_ref[...]


def query_kernel(all_ref, gain_ref, cos_ref, sin_ref, slot_ref, wq_ref, q_ref, send_ref):
    def weights(b):
        start = b * SHARE
        return wq_ref[start : start + 2 * HEAD, :], wq_ref[start + 2 * HEAD : start + SHARE, :]

    query = normed_times(all_ref, gain_ref, weights)
    turned = jnp.concatenate(
        [
            rotary(query[:, :HEAD], cos_ref, sin_ref).astype(BF16),
            rotary(query[:, HEAD:], cos_ref, sin_ref).astype(BF16),
        ],
        axis=1,
    )
    q_ref[...] = turned
    wide = jnp.concatenate([turned[t * ROWS : (t + 1) * ROWS] for t in range(STEPS)], axis=1)
    hot = (iota((RING * SLOT, ROWS), 0) == slot_ref[0:1, :]).astype(F32).astype(BF16)
    send_ref[...] = dot(hot, wide).astype(BF16)


def place_kernel(q_ref, slot_ref, send_ref):
    turned = q_ref[...]
    wide = jnp.concatenate([turned[t * ROWS : (t + 1) * ROWS] for t in range(STEPS)], axis=1)
    hot = (iota((RING * SLOT, ROWS), 0) == slot_ref[1:2, :]).astype(F32).astype(BF16)
    send_ref[...] = dot(hot, wide).astype(BF16)


def prefix_kernel(turn, own_ref, notes_ref, keys_ref, values_ref, out_ref):
    lanes = iota((RING, SLOT, HEAD), 2) - (ROOM + turn) == iota((RING, SLOT, HEAD), 1)
    notes = jnp.where(lanes, notes_ref[...][:, None, :], 0).reshape(RING * SLOT, HEAD)
    odd = jnp.sum(notes, axis=1, keepdims=True) == 1
    keys = jnp.concatenate([keys_ref[0], keys_ref[1]], axis=1)
    values = jnp.concatenate([values_ref[0], values_ref[1]], axis=1)
    slots = RING * SLOT
    lanes = iota((slots, HEAD), 1)
    denoms = jnp.zeros((slots, HEAD), F32)
    batch = 4
    for first in range(0, PAIRS, batch):
        some = range(first, first + batch)
        parts = []
        for i in some:
            q = own_ref[:, i * HEAD : (i + 1) * HEAD].astype(F32)
            parts.append(
                jnp.concatenate(
                    [jnp.where(odd, 0.0, q).astype(BF16), jnp.where(odd, q, 0.0).astype(BF16)],
                    axis=1,
                )
            )
        scores = dot(jnp.concatenate(parts, axis=0), keys, ((1,), (1,)))
        weights = capped_exp(scores).astype(BF16)
        numer = dot(weights, values)
        denom = jnp.sum(weights.astype(F32), axis=1, keepdims=True)
        for n, i in enumerate(some):
            part = numer[n * slots : (n + 1) * slots]
            out_ref[:, i * HEAD : (i + 1) * HEAD] = jnp.where(
                odd, part[:, HEAD:], part[:, :HEAD]
            ).astype(BF16)
            denoms = jnp.where(lanes == i, denom[n * slots : (n + 1) * slots], denoms)
    out_ref[:, WIDE:] = denoms.astype(BF16)


def local_kernel(
    all_ref, gain_ref, cos_ref, sin_ref, wkv_ref, q_ref, sk_ref, sv_ref, len_ref, out_ref
):
    def weights(b):
        start = b * SHARE
        return [
            jnp.concatenate([wkv_ref[0, rows, :], wkv_ref[1, rows, :]], axis=1)
            for rows in (
                slice(start, start + 2 * HEAD),
                slice(start + 2 * HEAD, start + SHARE),
            )
        ]

    keyval = normed_times(all_ref, gain_ref, weights)
    new_keys = rotary(keyval[:, :HEAD], cos_ref, sin_ref).astype(BF16)
    new_values = keyval[:, HEAD:].astype(BF16)
    suffix = ROWS * SUF
    keys = jnp.concatenate([sk_ref[...], new_keys], axis=0)
    values = jnp.concatenate([sv_ref[...], new_values], axis=0)
    columns = suffix + TOKENS
    column = iota((ROWS, columns), 1)
    row = iota((ROWS, columns), 0)
    first = row * SUF
    in_suffix = (column >= first) & (column < first + len_ref[...])
    lanes = iota((ROWS, HEAD), 1)
    denoms = jnp.zeros((ROWS, HEAD), F32)
    usable = in_suffix
    for t in range(STEPS):
        usable = usable | (column == row + (suffix + t * ROWS))
        for g in range(GROUP):
            i = t * GROUP + g
            q = q_ref[t * ROWS : (t + 1) * ROWS, g * HEAD : (g + 1) * HEAD]
            scores = dot(q, keys, ((1,), (1,)))
            weights = jnp.where(usable, capped_exp(scores), 0.0).astype(BF16)
            out_ref[:, i * HEAD : (i + 1) * HEAD] = dot(weights, values)
            denom = jnp.sum(weights.astype(F32), axis=1, keepdims=True)
            denoms = jnp.where(lanes == i, denom, denoms)
    out_ref[:, WIDE:] = denoms


def select_kernel(slot_ref, back_ref, local_ref, out_ref):
    hot = (slot_ref[:, 1:2] == iota((ROWS, RING * SLOT), 1)).astype(F32).astype(BF16)
    out_ref[...] = dot(hot, back_ref[...]) + local_ref[...]


def output_kernel(slot_ref, back_ref, local_ref, w_ref, out_ref):
    hot = (slot_ref[:, 0:1] == iota((ROWS, RING * SLOT), 1)).astype(F32).astype(BF16)
    total = dot(hot, back_ref[...]) + local_ref[...]
    rows = []
    for t in range(STEPS):
        heads = []
        for g in range(GROUP):
            i = t * GROUP + g
            heads.append(
                (
                    total[:, i * HEAD : (i + 1) * HEAD] / total[:, WIDE + i : WIDE + i + 1]
                ).astype(BF16)
            )
        rows.append(jnp.concatenate(heads, axis=1))
    attended = jnp.concatenate(rows, axis=0)
    lanes = iota((TOKENS, HEAD), 1)
    group = lane_group((ROWS, HEAD))
    quad = 4 * SHARE
    for first in range(0, RING, 4):
        part = dot(attended, w_ref[:, first * SHARE : first * SHARE + quad])
        for i in range(4):
            b = first + i
            tiles = [part[:, (2 * i + n) * HEAD : (2 * i + n + 1) * HEAD] for n in range(3)]
            away = TAIL * i
            if away:
                moved = [pltpu.roll(tile, HEAD - away, 1) for tile in tiles]
                low = jnp.where(lanes < HEAD - away, moved[0], moved[1])
                high = jnp.where(lanes < HEAD - away, moved[1], moved[2])
            else:
                low, high = tiles[0], tiles[1]
            out_ref[b, :TOKENS, :] = low.astype(BF16)
            out_ref[b, TOKENS : 2 * TOKENS, :] = high.astype(BF16)
            mixed = jnp.zeros((ROWS, HEAD), F32)
            for t in range(STEPS):
                tail = tiles[2][t * ROWS : (t + 1) * ROWS]
                shift = (TAIL * (t - i)) % HEAD
                tail = pltpu.roll(tail, shift, 1) if shift else tail
                mixed = jnp.where(group == t, tail, mixed)
            out_ref[b, 2 * TOKENS :, :] = mixed.astype(BF16)


def reduce_kernel(parts_ref, sum_ref, squares_ref):
    total = parts_ref[0].astype(F32)
    for b in range(1, RING):
        total = total + parts_ref[b].astype(F32)
    sum_ref[...] = total
    low, high, tail = total[:TOKENS], total[TOKENS : 2 * TOKENS], total[2 * TOKENS :]
    group = lane_group((ROWS, HEAD))
    squares = jnp.sum(low * low + high * high, axis=1, keepdims=True) + jnp.concatenate(
        [
            jnp.sum(jnp.where(group == t, tail * tail, 0.0), axis=1, keepdims=True)
            for t in range(STEPS)
        ],
        axis=0,
    )
    diagonal = iota((HEAD, HEAD), 0) == iota((HEAD, HEAD), 1)
    one = jnp.sum(jnp.where(diagonal, squares[:HEAD], 0.0), axis=0, keepdims=True)
    rest = TOKENS - HEAD
    two = jnp.sum(jnp.where(diagonal[:rest], squares[HEAD:], 0.0), axis=0, keepdims=True)
    line = jnp.concatenate([one, two], axis=0)
    for b in range(RING):
        squares_ref[b] = line


def scale_kernel(sum_ref, gain_ref, rows_ref, out_ref, wide_ref):
    total = sum_ref[...]
    tails = []
    for t in range(STEPS):
        tail = total[2 * TOKENS :]
        tails.append(pltpu.roll(tail, HEAD - TAIL * t, 1) if t else tail)
    tail = jnp.concatenate(tails, axis=0)[:, :TAIL]
    placed = jnp.concatenate([total[:TOKENS], total[TOKENS : 2 * TOKENS], tail], axis=1)
    out_ref[...] = placed * gain_ref[...]
    wide_ref[...] = rows_ref[...].astype(F32)


def finish_kernel(squares_ref, scaled_ref, wide_ref, out_ref):
    line = squares_ref[0]
    for b in range(1, RING):
        line = line + squares_ref[b]
    line = lax.rsqrt(line * (1.0 / D) + EPSILON)
    diagonal = iota((HEAD, HEAD), 0) == iota((HEAD, HEAD), 1)
    rest = TOKENS - HEAD
    one = jnp.sum(jnp.where(diagonal, line[0:1], 0.0), axis=1, keepdims=True)
    two = jnp.sum(jnp.where(diagonal[:rest], line[1:2], 0.0), axis=1, keepdims=True)
    root = jnp.concatenate([one, two], axis=0)
    out_ref[...] = (wide_ref[...] + scaled_ref[...] * root).astype(BF16)


def exchange(x, axis):
    return lax.all_to_all(x, axis, split_axis=0, concat_axis=0, tiled=True)


def per_device(
    token_ids,
    prompt_of,
    suffix_len,
    table,
    pre_gain,
    w_query,
    w_keyval,
    w_out,
    post_gain,
    prefix_keys,
    prefix_values,
    suffix_keys,
    suffix_values,
):
    vocab = table.shape[0]
    prompt_len = prefix_keys.shape[1]
    shape = jax.ShapeDtypeStruct

    notes, at, slot_columns, slot_lines = call(
        functools.partial(ask_kernel, vocab),
        [
            shape((RING, HEAD), jnp.int32),
            shape((TOKENS, 1), jnp.int32),
            shape((ROWS, 2), jnp.int32),
            shape((2, ROWS), jnp.int32),
        ],
        (token_ids, prompt_of.reshape(1, ROWS)),
        flops=LONG,
    )
    notes = exchange(notes.reshape(RING, 1, HEAD), "prefix").reshape(RING, HEAD)
    ends = jnp.max(notes[:, ENDS : ENDS + 2], axis=0)
    asked = jnp.max(jnp.sum(notes[:, COUNTS : COUNTS + RING], axis=0))
    crowded = (ends[0] > TAKE) | (asked > ALL)

    half = HEAD // 2
    frequency = 10000.0 ** (-(jnp.arange(half, dtype=F32) * 2.0 / HEAD))
    positions = (prompt_len + suffix_len[None, :] + jnp.arange(STEPS)[:, None]).astype(F32)
    angles = positions.reshape(TOKENS, 1) * frequency
    cosines = jnp.cos(angles)
    sines = jnp.sin(angles)
    cosines = jnp.concatenate([cosines, cosines], axis=1)
    sines = jnp.concatenate([-sines, sines], axis=1)
    gains = pre_gain.reshape(RING, SHARE)
    gains = jnp.stack(
        [gains[:, :HEAD], gains[:, HEAD : 2 * HEAD], jnp.tile(gains[:, 2 * HEAD :], (1, 4))]
    )
    notes, cosines, sines, gains = lax.optimization_barrier((notes, cosines, sines, gains))
    picked = call(
        pick_kernel,
        shape((RING, TAKE, SHARE), BF16),
        (notes, notes, table.T),
        flops=LONG,
        scalars=1,
        left=(2,),
        scratch=(
            pltpu.VMEM((ALL + ROOM, SHARE), F32),
            pltpu.VMEM((vocab, ALL), BF16),
            pltpu.VMEM((SHARE, vocab), BF16),
            pltpu.SemaphoreType.DMA,
        ),
    )
    got = exchange(picked, "prefix").reshape(RING * TAKE, SHARE)

    def take_all(_):
        everyone = exchange(jnp.broadcast_to(token_ids, (RING, STEPS, ROWS)), "prefix")
        inside_at = everyone - lax.axis_index("prefix") * vocab
        inside = (inside_at >= 0) & (inside_at < vocab)
        rows = jnp.take(table, jnp.clip(inside_at, 0, vocab - 1), axis=0)
        rows = jnp.where(inside[..., None], rows, jnp.zeros_like(rows))
        rows = exchange(rows, "prefix").astype(F32).sum(axis=0).astype(BF16)
        rows = jnp.pad(rows.reshape(TOKENS, SHARE), ((0, RING * TAKE - TOKENS), (0, 0)))
        return jnp.arange(TOKENS, dtype=jnp.int32).reshape(TOKENS, 1), rows

    at, got = lax.cond(crowded, take_all, lambda found: found, (at, got))
    embedded, packed = call(
        unpack_kernel,
        [shape((TOKENS, SHARE), BF16), shape((RING, PACKED, HEAD), BF16)],
        (at, got),
        flops=LONG,
    )
    everywhere = exchange(packed, "branch")

    queries, sent = call(
        query_kernel,
        [shape((TOKENS, GROUP * HEAD), BF16), shape((RING * SLOT, WIDE), BF16)],
        (everywhere, gains, cosines, sines, slot_lines, w_query),
        flops=LONG,
    )

    queries, lengths, ends = lax.optimization_barrier((queries, suffix_len, ends))

    def ask(sent):
        return exchange(sent.reshape(RING, SLOT, WIDE), "prefix").reshape(RING * SLOT, WIDE)

    def answer(own, turn):
        sums = call(
            functools.partial(prefix_kernel, turn),
            shape((RING * SLOT, BACK), BF16),
            (own, notes, prefix_keys, prefix_values),
            flops=8 * RING * SLOT * prompt_len * WIDE,
        )
        return exchange(sums.reshape(RING, SLOT, BACK), "prefix").reshape(RING * SLOT, BACK)

    own = ask(sent)
    local = call(
        local_kernel,
        shape((ROWS, BACK), F32),
        (
            everywhere,
            gains,
            cosines,
            sines,
            w_keyval,
            queries,
            suffix_keys.reshape(ROWS * SUF, HEAD),
            suffix_values.reshape(ROWS * SUF, HEAD),
            lengths.reshape(ROWS, 1),
        ),
        flops=LONG,
    )
    own, local = lax.optimization_barrier((own, local))

    def second_round(local):
        sent = call(
            place_kernel,
            shape((RING * SLOT, WIDE), BF16),
            (queries, slot_lines),
        )
        back = answer(ask(sent), SLOT)
        return call(
            select_kernel,
            shape((ROWS, BACK), F32),
            (slot_columns, back, local),
        )

    local = lax.cond(ends[1] > SLOT, second_round, lambda local: local, local)
    own, local = lax.optimization_barrier((own, local))
    back = answer(own, 0)

    shares = call(
        output_kernel,
        shape((RING, PACKED, HEAD), BF16),
        (slot_columns, back, local, w_out),
        flops=2 * TOKENS * GROUP * HEAD * D,
    )
    shares = exchange(shares, "branch")
    total, squares = call(
        reduce_kernel,
        [shape((PACKED, HEAD), F32), shape((RING, 2, HEAD), F32)],
        (shares,),
    )
    squares = exchange(squares, "branch")
    scaled, wide = call(
        scale_kernel,
        [shape((TOKENS, SHARE), F32)] * 2,
        (total, post_gain.reshape(1, SHARE), embedded),
    )
    layer_out = call(
        finish_kernel,
        shape((TOKENS, SHARE), BF16),
        (squares, scaled, wide),
    )
    return layer_out.reshape(STEPS, ROWS, SHARE)


def solution(mesh):
    placed = (
        P(None, "prefix"),
        P("prefix", None),
        P("prefix"),
        P("prefix", "branch"),
        P(),
        P(None, "branch"),
        P(None, None, "branch"),
        P("branch", None),
        P("branch"),
        P("prefix", None, "branch"),
        P("prefix", None, "branch"),
        P("prefix", None, "branch"),
        P("prefix", None, "branch"),
    )
    return jax.shard_map(
        per_device,
        mesh=mesh,
        in_specs=placed,
        out_specs=P(None, "prefix", "branch"),
        check_vma=False,
    )
```

```python
import functools

import jax
import jax.numpy as jnp
from jax import lax
from jax.experimental import pallas as pl
from jax.experimental.pallas import tpu as pltpu
from jax.sharding import PartitionSpec as P

D = 4608
HEADS = 32
KV_HEADS = 16
HEAD = 128
SUF = 8
SOFT_CAP = 50.0
EPSILON = 1e-06
LOG2_E = 1.4426950408889634
SCALE = float(D // HEADS) ** (-0.5)

RING = 16
STEPS = 4
ROWS = 48
TOKENS = STEPS * ROWS
SHARE = D // RING
TAIL = SHARE - 2 * HEAD
PACKED = 2 * TOKENS + ROWS
TAKE = 24
ROOM = 32
ENDS = ROOM + 16
COUNTS = 64
ALL = 256
SLOT = 8
GROUP = HEADS // KV_HEADS
PAIRS = STEPS * GROUP
WIDE = PAIRS * HEAD
BACK = WIDE + HEAD

F32 = jnp.float32
BF16 = jnp.bfloat16
VMEM = pl.BlockSpec(memory_space=pltpu.VMEM)
SMEM = pl.BlockSpec(memory_space=pltpu.SMEM)
ANY = pl.BlockSpec(memory_space=pl.ANY)


def call(kernel, out_shape, args, flops=0, scalars=0, left=(), scratch=(), limit=24):
    nbytes = sum(a.size * a.dtype.itemsize for a in args)
    many = isinstance(out_shape, (list, tuple))
    return pl.pallas_call(
        kernel,
        out_shape=out_shape,
        in_specs=[
            SMEM if n < scalars else ANY if n in left else VMEM for n in range(len(args))
        ],
        out_specs=[VMEM] * len(out_shape) if many else VMEM,
        scratch_shapes=list(scratch),
        compiler_params=pltpu.CompilerParams(vmem_limit_bytes=limit * 1024 * 1024),
        cost_estimate=pl.CostEstimate(flops=flops, bytes_accessed=nbytes, transcendentals=0),
    )(*args)


def dot(a, b, contract=((1,), (0,))):
    return lax.dot_general(a, b, (contract, ((), ())), preferred_element_type=F32)


def iota(shape, axis):
    return lax.broadcasted_iota(jnp.int32, shape, axis)


def capped_exp(scores):
    return jnp.exp2(SOFT_CAP * LOG2_E * jnp.tanh(scores * (SCALE / SOFT_CAP)))


def lane_group(shape):
    return lax.shift_right_logical(iota(shape, 1), 5)


def column_of(row):
    n = row.shape[1]
    diagonal = iota((n, n), 0) == iota((n, n), 1)
    return jnp.sum(jnp.where(diagonal, row, 0), axis=1, keepdims=True)


def ask_kernel(vocab, ids_ref, prompt_ref, notes_ref, at_ref, columns_ref, lines_ref):
    def owner_of(ids):
        total = jnp.zeros(ids.shape, jnp.int32)
        for d in range(1, RING):
            total = total + (ids >= d * vocab).astype(jnp.int32)
        return total

    rows = [ids_ref[t : t + 1, :] for t in range(STEPS)]
    column = jnp.concatenate([column_of(row) for row in rows], axis=0)
    owner = owner_of(column)
    base = owner * vocab
    down = iota((TOKENS, ROWS), 0)
    over = iota((TOKENS, ROWS), 1)
    rank = jnp.zeros((TOKENS, ROWS), jnp.int32)
    new_rows = []
    for t in range(STEPS):
        seen = (column == rows[t]) & (down < over + t * ROWS)
        new = 1 - jnp.max(seen.astype(jnp.int32), axis=0, keepdims=True)
        new_rows.append(new)
        rank = rank + jnp.where((rows[t] >= base) & (rows[t] < column), new, 0)
    rank = jnp.sum(rank, axis=1, keepdims=True)
    fits = rank < TAKE
    at_ref[...] = jnp.where(fits, owner * TAKE + rank, -1)
    value = column - base + 1
    cell = jnp.where(fits, rank, -1) == iota((TOKENS, HEAD), 1)
    coarse = jnp.where(cell, lax.shift_right_logical(value, 6), 0).astype(F32).astype(BF16)
    fine = jnp.where(cell, value & 63, 0).astype(F32).astype(BF16)
    holders = iota((RING, ROWS), 0)
    high = jnp.zeros((RING, HEAD), F32)
    low = jnp.zeros((RING, HEAD), F32)
    count = jnp.zeros((RING, ROWS), F32)
    for t in range(STEPS):
        part = slice(t * ROWS, (t + 1) * ROWS)
        mine = jnp.where(owner_of(rows[t]) == holders, new_rows[t], 0).astype(F32)
        count = count + mine
        mine = mine.astype(BF16)
        high = high + dot(mine, coarse[part])
        low = low + dot(mine, fine[part])
    asked = high.astype(jnp.int32) * 64 + low.astype(jnp.int32) - 1

    prompt = prompt_ref[...]
    prompt_column = column_of(prompt)
    holder = lax.shift_right_logical(prompt, 1)
    holder_column = lax.shift_right_logical(prompt_column, 1)
    down = iota((ROWS, ROWS), 0)
    over = iota((ROWS, ROWS), 1)
    same = holder == holder_column
    turn = jnp.sum((same & (down < over)).astype(jnp.int32), axis=0, keepdims=True)
    turn_column = jnp.sum((same & (over < down)).astype(jnp.int32), axis=1, keepdims=True)
    mine = (holder == holders).astype(F32).astype(BF16)
    odd = jnp.where(turn_column + ROOM == iota((ROWS, HEAD), 1), prompt_column & 1, 0)
    odds = dot(mine, odd.astype(F32).astype(BF16)).astype(jnp.int32)
    lane = iota((RING, HEAD), 1)
    notes = jnp.where(lane < ROOM, asked, odds)
    most = jnp.max(rank, axis=0, keepdims=True) + 1
    notes = jnp.where(lane == ENDS, most, notes)
    most = jnp.max(turn_column, axis=0, keepdims=True) + 1
    notes = jnp.where(lane == ENDS + 1, most, notes)
    count = jnp.sum(count, axis=1, keepdims=True).astype(jnp.int32)
    notes = jnp.where(lane == ENDS + 2, count, notes)
    counts = jnp.where(lane == iota((RING, HEAD), 0) + COUNTS, count, 0)
    counts = jnp.sum(counts, axis=0, keepdims=True)
    listed = (lane >= COUNTS) & (lane < COUNTS + RING)
    notes_ref[...] = jnp.where(listed, counts, notes)

    def slots(holder, turn):
        now = jnp.where(turn < SLOT, holder * SLOT + turn, -1)
        later = jnp.where(turn >= SLOT, holder * SLOT + turn - SLOT, -1)
        return now, later

    columns_ref[...] = jnp.concatenate(slots(holder_column, turn_column), axis=1)
    lines_ref[...] = jnp.concatenate(slots(holder, turn), axis=0)


LONG = 20_000_000_000
PIECE = 1024


def pick_kernel(counts_ref, notes_ref, table_ref, out_ref, rows_ref):
    vocab = table_ref.shape[1]
    lane = iota((8, HEAD), 1)
    ids = jnp.zeros((8, ALL), jnp.int32)
    start = 0
    starts = []
    for d in range(RING):
        starts.append(start)
        row = jnp.broadcast_to(notes_ref[d : d + 1, :], (8, HEAD))
        row = jnp.where(lane < ROOM, row + 1, 0)
        row = jnp.concatenate([row, jnp.zeros((8, ALL - HEAD), jnp.int32)], axis=1)
        ids = ids + (pltpu.roll(row, start & (ALL - 1), 1) if d else row)
        start = jnp.minimum(start + counts_ref[d, ENDS + 2], ALL)
    ids = ids[0:1] - 1
    count = ALL
    step = 256
    lines = iota((step, count), 0).astype(F32).astype(BF16)

    def picked(start, rows):
        size = rows.shape[1]
        hots = []
        for at in range(start, start + size, step):
            here = (ids >= at) & (ids < at + step)
            near = jnp.where(here, ids - at, -1).astype(F32).astype(BF16)
            some = lines[: min(step, start + size - at)]
            hots.append(jnp.where(some == near, jnp.ones((), BF16), jnp.zeros((), BF16)))
        return dot(rows, jnp.concatenate(hots, axis=0) if len(hots) > 1 else hots[0])

    total = jnp.zeros((SHARE, count), F32)
    for start in range(0, vocab, PIECE):
        total = total + picked(start, table_ref[:, start : min(start + PIECE, vocab)])
    rows_ref[:ALL, :] = total.T
    rows_ref[ALL:, :] = jnp.zeros((ROOM, SHARE), F32)
    for d in range(RING):
        if d:
            whole_start = pl.multiple_of(starts[d] - (starts[d] & 7), 8)
            some = rows_ref[pl.ds(whole_start, ROOM), :]
            some = pltpu.roll(some, (ROOM - (starts[d] & 7)) & (ROOM - 1), 0)
        else:
            some = rows_ref[:ROOM, :]
        out_ref[d] = some[:TAKE].astype(BF16)


def pack(rows, packed_ref):
    low = rows[:, :HEAD].astype(BF16)
    high = rows[:, HEAD : 2 * HEAD].astype(BF16)
    tail = jnp.concatenate([rows[:, 2 * HEAD :], jnp.zeros((TOKENS, HEAD - TAIL), F32)], axis=1)
    mixed = tail[:ROWS]
    for t in range(1, STEPS):
        mixed = mixed + pltpu.roll(tail[t * ROWS : (t + 1) * ROWS], TAIL * t, 1)
    mixed = mixed.astype(BF16)
    for b in range(RING):
        packed_ref[b, :TOKENS, :] = low
        packed_ref[b, TOKENS : 2 * TOKENS, :] = high
        packed_ref[b, 2 * TOKENS :, :] = mixed


def unpack_kernel(at_ref, got_ref, out_ref, packed_ref):
    hot = (at_ref[...] == iota((TOKENS, RING * TAKE), 1)).astype(F32).astype(BF16)
    rows = dot(hot, got_ref[...])
    out_ref[...] = rows.astype(BF16)
    pack(rows, packed_ref)


def normed_times(all_ref, gain_ref, weights):
    group = lane_group((ROWS, HEAD))
    squares = jnp.zeros((TOKENS, HEAD), F32)
    tail_squares = jnp.zeros((ROWS, HEAD), F32)
    product = jnp.zeros((TOKENS, 2 * HEAD), F32)
    tail_blocks, tail_weights = [], []
    for b in range(RING):
        low = all_ref[b, :TOKENS, :].astype(F32)
        high = all_ref[b, TOKENS : 2 * TOKENS, :].astype(F32)
        tail = all_ref[b, 2 * TOKENS :, :].astype(F32)
        main_weights, more_weights = weights(b)
        squares = squares + (low * low + high * high)
        tail_squares = tail_squares + tail * tail
        both = jnp.concatenate(
            [
                (low * gain_ref[0, b : b + 1, :]).astype(BF16),
                (high * gain_ref[1, b : b + 1, :]).astype(BF16),
            ],
            axis=1,
        )
        product = product + dot(both, main_weights)
        tail_weights.append(more_weights)
        scaled = tail * gain_ref[2, b : b + 1, :]
        place = b % 4
        if place == 0:
            tail_blocks.append([jnp.zeros((ROWS, HEAD), F32) for _ in range(STEPS)])
        for t in range(STEPS):
            shift = (TAIL * (place - t)) % HEAD
            moved = pltpu.roll(scaled, shift, 1) if shift else scaled
            tail_blocks[-1][t] = jnp.where(group == place, moved, tail_blocks[-1][t])
    tails = jnp.concatenate(
        [jnp.concatenate(block, axis=0).astype(BF16) for block in tail_blocks], axis=1
    )
    product = product + dot(tails, jnp.concatenate(tail_weights, axis=0))
    total = jnp.sum(squares, axis=1, keepdims=True) + jnp.concatenate(
        [
            jnp.sum(jnp.where(group == t, tail_squares, 0.0), axis=1, keepdims=True)
            for t in range(STEPS)
        ],
        axis=0,
    )
    return product * lax.rsqrt(total * (1.0 / D) + EPSILON)


def rotary(u, cos_ref, sin_ref):
    return u * cos_ref[...] + pltpu.roll(u, HEAD // 2, 1) * sin_ref[...]


def query_kernel(all_ref, gain_ref, cos_ref, sin_ref, slot_ref, wq_ref, q_ref, send_ref):
    def weights(b):
        start = b * SHARE
        return wq_ref[start : start + 2 * HEAD, :], wq_ref[start + 2 * HEAD : start + SHARE, :]

    query = normed_times(all_ref, gain_ref, weights)
    turned = jnp.concatenate(
        [
            rotary(query[:, :HEAD], cos_ref, sin_ref).astype(BF16),
            rotary(query[:, HEAD:], cos_ref, sin_ref).astype(BF16),
        ],
        axis=1,
    )
    q_ref[...] = turned
    wide = jnp.concatenate([turned[t * ROWS : (t + 1) * ROWS] for t in range(STEPS)], axis=1)
    hot = (iota((RING * SLOT, ROWS), 0) == slot_ref[0:1, :]).astype(F32).astype(BF16)
    send_ref[...] = dot(hot, wide).astype(BF16)


def place_kernel(q_ref, slot_ref, send_ref):
    turned = q_ref[...]
    wide = jnp.concatenate([turned[t * ROWS : (t + 1) * ROWS] for t in range(STEPS)], axis=1)
    hot = (iota((RING * SLOT, ROWS), 0) == slot_ref[1:2, :]).astype(F32).astype(BF16)
    send_ref[...] = dot(hot, wide).astype(BF16)


def prefix_kernel(
    turn, own_ref, notes_ref, keys_ref, values_ref, out_ref, both_keys, both_values, done
):
    fetches = []
    for m, (source, target) in enumerate(((keys_ref, both_keys), (values_ref, both_values))):
        for n in range(2):
            part = target.at[:, n * HEAD : (n + 1) * HEAD]
            fetches.append(pltpu.make_async_copy(source.at[n], part, done.at[2 * m + n]))
            fetches[-1].start()
    lanes = iota((RING, SLOT, HEAD), 2) - (ROOM + turn) == iota((RING, SLOT, HEAD), 1)
    notes = jnp.where(lanes, notes_ref[...][:, None, :], 0).reshape(RING * SLOT, HEAD)
    odd = jnp.sum(notes, axis=1, keepdims=True) == 1
    slots = RING * SLOT
    lanes = iota((slots, HEAD), 1)
    denoms = jnp.zeros((slots, HEAD), F32)
    batch = 4
    for first in range(0, PAIRS, batch):
        some = range(first, first + batch)
        parts = []
        for i in some:
            q = own_ref[:, i * HEAD : (i + 1) * HEAD].astype(F32)
            parts.append(
                jnp.concatenate(
                    [jnp.where(odd, 0.0, q).astype(BF16), jnp.where(odd, q, 0.0).astype(BF16)],
                    axis=1,
                )
            )
        if first == 0:
            fetches[0].wait()
            fetches[1].wait()
        scores = dot(jnp.concatenate(parts, axis=0), both_keys[...], ((1,), (1,)))
        weights = capped_exp(scores).astype(BF16)
        if first == 0:
            fetches[2].wait()
            fetches[3].wait()
        numer = dot(weights, both_values[...])
        denom = jnp.sum(weights.astype(F32), axis=1, keepdims=True)
        for n, i in enumerate(some):
            part = numer[n * slots : (n + 1) * slots]
            out_ref[:, i * HEAD : (i + 1) * HEAD] = jnp.where(
                odd, part[:, HEAD:], part[:, :HEAD]
            ).astype(BF16)
            denoms = jnp.where(lanes == i, denom[n * slots : (n + 1) * slots], denoms)
    out_ref[:, WIDE:] = denoms.astype(BF16)


def local_kernel(
    all_ref, gain_ref, cos_ref, sin_ref, wkv_ref, q_ref, sk_ref, sv_ref, len_ref, out_ref
):
    def weights(b):
        start = b * SHARE
        return [
            jnp.concatenate([wkv_ref[0, rows, :], wkv_ref[1, rows, :]], axis=1)
            for rows in (
                slice(start, start + 2 * HEAD),
                slice(start + 2 * HEAD, start + SHARE),
            )
        ]

    keyval = normed_times(all_ref, gain_ref, weights)
    new_keys = rotary(keyval[:, :HEAD], cos_ref, sin_ref).astype(BF16)
    new_values = keyval[:, HEAD:].astype(BF16)
    suffix = ROWS * SUF
    keys = jnp.concatenate([sk_ref[...], new_keys], axis=0)
    values = jnp.concatenate([sv_ref[...], new_values], axis=0)
    columns = suffix + TOKENS
    column = iota((ROWS, columns), 1)
    row = iota((ROWS, columns), 0)
    first = row * SUF
    in_suffix = (column >= first) & (column < first + len_ref[...])
    lanes = iota((ROWS, HEAD), 1)
    denoms = jnp.zeros((ROWS, HEAD), F32)
    usable = in_suffix
    for t in range(STEPS):
        usable = usable | (column == row + (suffix + t * ROWS))
        for g in range(GROUP):
            i = t * GROUP + g
            q = q_ref[t * ROWS : (t + 1) * ROWS, g * HEAD : (g + 1) * HEAD]
            scores = dot(q, keys, ((1,), (1,)))
            weights = jnp.where(usable, capped_exp(scores), 0.0).astype(BF16)
            out_ref[:, i * HEAD : (i + 1) * HEAD] = dot(weights, values)
            denom = jnp.sum(weights.astype(F32), axis=1, keepdims=True)
            denoms = jnp.where(lanes == i, denom, denoms)
    out_ref[:, WIDE:] = denoms


def select_kernel(slot_ref, back_ref, local_ref, out_ref):
    hot = (slot_ref[:, 1:2] == iota((ROWS, RING * SLOT), 1)).astype(F32).astype(BF16)
    out_ref[...] = dot(hot, back_ref[...]) + local_ref[...]


def output_kernel(slot_ref, back_ref, local_ref, w_ref, out_ref):
    hot = (slot_ref[:, 0:1] == iota((ROWS, RING * SLOT), 1)).astype(F32).astype(BF16)
    total = dot(hot, back_ref[...]) + local_ref[...]
    rows = []
    for t in range(STEPS):
        heads = []
        for g in range(GROUP):
            i = t * GROUP + g
            heads.append(
                (
                    total[:, i * HEAD : (i + 1) * HEAD] / total[:, WIDE + i : WIDE + i + 1]
                ).astype(BF16)
            )
        rows.append(jnp.concatenate(heads, axis=1))
    attended = jnp.concatenate(rows, axis=0)
    lanes = iota((TOKENS, HEAD), 1)
    group = lane_group((ROWS, HEAD))
    quad = 4 * SHARE
    for first in range(0, RING, 4):
        part = dot(attended, w_ref[:, first * SHARE : first * SHARE + quad])
        for i in range(4):
            b = first + i
            tiles = [part[:, (2 * i + n) * HEAD : (2 * i + n + 1) * HEAD] for n in range(3)]
            away = TAIL * i
            if away:
                moved = [pltpu.roll(tile, HEAD - away, 1) for tile in tiles]
                low = jnp.where(lanes < HEAD - away, moved[0], moved[1])
                high = jnp.where(lanes < HEAD - away, moved[1], moved[2])
            else:
                low, high = tiles[0], tiles[1]
            out_ref[b, :TOKENS, :] = low.astype(BF16)
            out_ref[b, TOKENS : 2 * TOKENS, :] = high.astype(BF16)
            mixed = jnp.zeros((ROWS, HEAD), F32)
            for t in range(STEPS):
                tail = tiles[2][t * ROWS : (t + 1) * ROWS]
                shift = (TAIL * (t - i)) % HEAD
                tail = pltpu.roll(tail, shift, 1) if shift else tail
                mixed = jnp.where(group == t, tail, mixed)
            out_ref[b, 2 * TOKENS :, :] = mixed.astype(BF16)


def reduce_kernel(parts_ref, sum_ref, squares_ref):
    total = parts_ref[0].astype(F32)
    for b in range(1, RING):
        total = total + parts_ref[b].astype(F32)
    sum_ref[...] = total
    low, high, tail = total[:TOKENS], total[TOKENS : 2 * TOKENS], total[2 * TOKENS :]
    group = lane_group((ROWS, HEAD))
    squares = jnp.sum(low * low + high * high, axis=1, keepdims=True) + jnp.concatenate(
        [
            jnp.sum(jnp.where(group == t, tail * tail, 0.0), axis=1, keepdims=True)
            for t in range(STEPS)
        ],
        axis=0,
    )
    diagonal = iota((HEAD, HEAD), 0) == iota((HEAD, HEAD), 1)
    one = jnp.sum(jnp.where(diagonal, squares[:HEAD], 0.0), axis=0, keepdims=True)
    rest = TOKENS - HEAD
    two = jnp.sum(jnp.where(diagonal[:rest], squares[HEAD:], 0.0), axis=0, keepdims=True)
    line = jnp.concatenate([one, two], axis=0)
    for b in range(RING):
        squares_ref[b] = line


def scale_kernel(sum_ref, gain_ref, rows_ref, out_ref, wide_ref):
    total = sum_ref[...]
    tails = []
    for t in range(STEPS):
        tail = total[2 * TOKENS :]
        tails.append(pltpu.roll(tail, HEAD - TAIL * t, 1) if t else tail)
    tail = jnp.concatenate(tails, axis=0)[:, :TAIL]
    placed = jnp.concatenate([total[:TOKENS], total[TOKENS : 2 * TOKENS], tail], axis=1)
    out_ref[...] = placed * gain_ref[...]
    wide_ref[...] = rows_ref[...].astype(F32)


def finish_kernel(squares_ref, scaled_ref, wide_ref, out_ref):
    line = squares_ref[0]
    for b in range(1, RING):
        line = line + squares_ref[b]
    line = lax.rsqrt(line * (1.0 / D) + EPSILON)
    diagonal = iota((HEAD, HEAD), 0) == iota((HEAD, HEAD), 1)
    rest = TOKENS - HEAD
    one = jnp.sum(jnp.where(diagonal, line[0:1], 0.0), axis=1, keepdims=True)
    two = jnp.sum(jnp.where(diagonal[:rest], line[1:2], 0.0), axis=1, keepdims=True)
    root = jnp.concatenate([one, two], axis=0)
    out_ref[...] = (wide_ref[...] + scaled_ref[...] * root).astype(BF16)


def exchange(x, axis):
    return lax.all_to_all(x, axis, split_axis=0, concat_axis=0, tiled=True)


def per_device(
    token_ids,
    prompt_of,
    suffix_len,
    table,
    pre_gain,
    w_query,
    w_keyval,
    w_out,
    post_gain,
    prefix_keys,
    prefix_values,
    suffix_keys,
    suffix_values,
):
    vocab = table.shape[0]
    prompt_len = prefix_keys.shape[1]
    shape = jax.ShapeDtypeStruct

    notes, at, slot_columns, slot_lines = call(
        functools.partial(ask_kernel, vocab),
        [
            shape((RING, HEAD), jnp.int32),
            shape((TOKENS, 1), jnp.int32),
            shape((ROWS, 2), jnp.int32),
            shape((2, ROWS), jnp.int32),
        ],
        (token_ids, prompt_of.reshape(1, ROWS)),
        flops=LONG,
    )
    notes = exchange(notes.reshape(RING, 1, HEAD), "prefix").reshape(RING, HEAD)
    ends = jnp.max(notes[:, ENDS : ENDS + 2], axis=0)
    asked = jnp.max(jnp.sum(notes[:, COUNTS : COUNTS + RING], axis=0))
    crowded = (ends[0] > TAKE) | (asked > ALL)

    half = HEAD // 2
    frequency = 10000.0 ** (-(jnp.arange(half, dtype=F32) * 2.0 / HEAD))
    positions = (prompt_len + suffix_len[None, :] + jnp.arange(STEPS)[:, None]).astype(F32)
    angles = positions.reshape(TOKENS, 1) * frequency
    cosines = jnp.cos(angles)
    sines = jnp.sin(angles)
    cosines = jnp.concatenate([cosines, cosines], axis=1)
    sines = jnp.concatenate([-sines, sines], axis=1)
    gains = pre_gain.reshape(RING, SHARE)
    gains = jnp.stack(
        [gains[:, :HEAD], gains[:, HEAD : 2 * HEAD], jnp.tile(gains[:, 2 * HEAD :], (1, 4))]
    )
    notes, cosines, sines, gains = lax.optimization_barrier((notes, cosines, sines, gains))
    picked = call(
        pick_kernel,
        shape((RING, TAKE, SHARE), BF16),
        (notes, notes, table.T),
        flops=LONG,
        scalars=1,
        scratch=(pltpu.VMEM((ALL + ROOM, SHARE), F32),),
    )
    got = exchange(picked, "prefix").reshape(RING * TAKE, SHARE)

    def take_all(_):
        everyone = exchange(jnp.broadcast_to(token_ids, (RING, STEPS, ROWS)), "prefix")
        inside_at = everyone - lax.axis_index("prefix") * vocab
        inside = (inside_at >= 0) & (inside_at < vocab)
        rows = jnp.take(table, jnp.clip(inside_at, 0, vocab - 1), axis=0)
        rows = jnp.where(inside[..., None], rows, jnp.zeros_like(rows))
        rows = exchange(rows, "prefix").astype(F32).sum(axis=0).astype(BF16)
        rows = jnp.pad(rows.reshape(TOKENS, SHARE), ((0, RING * TAKE - TOKENS), (0, 0)))
        return jnp.arange(TOKENS, dtype=jnp.int32).reshape(TOKENS, 1), rows

    at, got = lax.cond(crowded, take_all, lambda found: found, (at, got))
    embedded, packed = call(
        unpack_kernel,
        [shape((TOKENS, SHARE), BF16), shape((RING, PACKED, HEAD), BF16)],
        (at, got),
        flops=LONG,
    )
    everywhere = exchange(packed, "branch")

    queries, sent = call(
        query_kernel,
        [shape((TOKENS, GROUP * HEAD), BF16), shape((RING * SLOT, WIDE), BF16)],
        (everywhere, gains, cosines, sines, slot_lines, w_query),
        flops=LONG,
    )

    queries, lengths, ends = lax.optimization_barrier((queries, suffix_len, ends))

    def ask(sent):
        return exchange(sent.reshape(RING, SLOT, WIDE), "prefix").reshape(RING * SLOT, WIDE)

    def answer(own, turn):
        sums = call(
            functools.partial(prefix_kernel, turn),
            shape((RING * SLOT, BACK), BF16),
            (own, notes, prefix_keys, prefix_values),
            left=(2, 3),
            scratch=(
                pltpu.VMEM((prompt_len, 2 * HEAD), BF16),
                pltpu.VMEM((prompt_len, 2 * HEAD), BF16),
                pltpu.SemaphoreType.DMA((4,)),
            ),
            flops=8 * RING * SLOT * prompt_len * WIDE,
        )
        return exchange(sums.reshape(RING, SLOT, BACK), "prefix").reshape(RING * SLOT, BACK)

    own = ask(sent)
    local = call(
        local_kernel,
        shape((ROWS, BACK), F32),
        (
            everywhere,
            gains,
            cosines,
            sines,
            w_keyval,
            queries,
            suffix_keys.reshape(ROWS * SUF, HEAD),
            suffix_values.reshape(ROWS * SUF, HEAD),
            lengths.reshape(ROWS, 1),
        ),
        flops=LONG,
    )
    own, local = lax.optimization_barrier((own, local))

    def second_round(local):
        sent = call(
            place_kernel,
            shape((RING * SLOT, WIDE), BF16),
            (queries, slot_lines),
        )
        back = answer(ask(sent), SLOT)
        return call(
            select_kernel,
            shape((ROWS, BACK), F32),
            (slot_columns, back, local),
        )

    local = lax.cond(ends[1] > SLOT, second_round, lambda local: local, local)
    own, local = lax.optimization_barrier((own, local))
    back = answer(own, 0)

    shares = call(
        output_kernel,
        shape((RING, PACKED, HEAD), BF16),
        (slot_columns, back, local, w_out),
        flops=2 * TOKENS * GROUP * HEAD * D,
    )
    shares = exchange(shares, "branch")
    total, squares = call(
        reduce_kernel,
        [shape((PACKED, HEAD), F32), shape((RING, 2, HEAD), F32)],
        (shares,),
    )
    squares = exchange(squares, "branch")
    scaled, wide = call(
        scale_kernel,
        [shape((TOKENS, SHARE), F32)] * 2,
        (total, post_gain.reshape(1, SHARE), embedded),
    )
    layer_out = call(
        finish_kernel,
        shape((TOKENS, SHARE), BF16),
        (squares, scaled, wide),
    )
    return layer_out.reshape(STEPS, ROWS, SHARE)


def solution(mesh):
    placed = (
        P(None, "prefix"),
        P("prefix", None),
        P("prefix"),
        P("prefix", "branch"),
        P(),
        P(None, "branch"),
        P(None, None, "branch"),
        P("branch", None),
        P("branch"),
        P("prefix", None, "branch"),
        P("prefix", None, "branch"),
        P("prefix", None, "branch"),
        P("prefix", None, "branch"),
    )
    return jax.shard_map(
        per_device,
        mesh=mesh,
        in_specs=placed,
        out_specs=P(None, "prefix", "branch"),
        check_vma=False,
    )
```

```python
import functools

import jax
import jax.numpy as jnp
from jax import lax
from jax.experimental import pallas as pl
from jax.experimental.pallas import tpu as pltpu
from jax.sharding import PartitionSpec as P

D = 4608
HEADS = 32
KV_HEADS = 16
HEAD = 128
SUF = 8
SOFT_CAP = 50.0
EPSILON = 1e-06
LOG2_E = 1.4426950408889634
SCALE = float(D // HEADS) ** (-0.5)

RING = 16
STEPS = 4
ROWS = 48
TOKENS = STEPS * ROWS
SHARE = D // RING
TAIL = SHARE - 2 * HEAD
PACKED = 2 * TOKENS + ROWS
TAKE = 24
ROOM = 32
ENDS = ROOM + 16
COUNTS = 64
ALL = 256
SLOT = 8
GROUP = HEADS // KV_HEADS
PAIRS = STEPS * GROUP
WIDE = PAIRS * HEAD
BACK = WIDE + HEAD

F32 = jnp.float32
BF16 = jnp.bfloat16
VMEM = pl.BlockSpec(memory_space=pltpu.VMEM)
SMEM = pl.BlockSpec(memory_space=pltpu.SMEM)


def call(kernel, out_shape, args, flops=0, scalars=0, scratch=(), limit=24):
    nbytes = sum(a.size * a.dtype.itemsize for a in args)
    many = isinstance(out_shape, (list, tuple))
    return pl.pallas_call(
        kernel,
        out_shape=out_shape,
        in_specs=[SMEM] * scalars + [VMEM] * (len(args) - scalars),
        out_specs=[VMEM] * len(out_shape) if many else VMEM,
        scratch_shapes=list(scratch),
        compiler_params=pltpu.CompilerParams(vmem_limit_bytes=limit * 1024 * 1024),
        cost_estimate=pl.CostEstimate(flops=flops, bytes_accessed=nbytes, transcendentals=0),
    )(*args)


def dot(a, b, contract=((1,), (0,))):
    return lax.dot_general(a, b, (contract, ((), ())), preferred_element_type=F32)


def iota(shape, axis):
    return lax.broadcasted_iota(jnp.int32, shape, axis)


def capped_exp(scores):
    return jnp.exp2(SOFT_CAP * LOG2_E * jnp.tanh(scores * (SCALE / SOFT_CAP)))


def lane_group(shape):
    return lax.shift_right_logical(iota(shape, 1), 5)


def column_of(row):
    n = row.shape[1]
    diagonal = iota((n, n), 0) == iota((n, n), 1)
    return jnp.sum(jnp.where(diagonal, row, 0), axis=1, keepdims=True)


def ask_kernel(vocab, ids_ref, prompt_ref, notes_ref, at_ref, columns_ref, lines_ref):
    def owner_of(ids):
        total = jnp.zeros(ids.shape, jnp.int32)
        for d in range(1, RING):
            total = total + (ids >= d * vocab).astype(jnp.int32)
        return total

    rows = [ids_ref[t : t + 1, :] for t in range(STEPS)]
    column = jnp.concatenate([column_of(row) for row in rows], axis=0)
    owner = owner_of(column)
    base = owner * vocab
    down = iota((TOKENS, ROWS), 0)
    over = iota((TOKENS, ROWS), 1)
    rank = jnp.zeros((TOKENS, ROWS), jnp.int32)
    new_rows = []
    for t in range(STEPS):
        seen = (column == rows[t]) & (down < over + t * ROWS)
        new = 1 - jnp.max(seen.astype(jnp.int32), axis=0, keepdims=True)
        new_rows.append(new)
        rank = rank + jnp.where((rows[t] >= base) & (rows[t] < column), new, 0)
    rank = jnp.sum(rank, axis=1, keepdims=True)
    fits = rank < TAKE
    at_ref[...] = jnp.where(fits, owner * TAKE + rank, -1)
    value = column - base + 1
    cell = jnp.where(fits, rank, -1) == iota((TOKENS, HEAD), 1)
    coarse = jnp.where(cell, lax.shift_right_logical(value, 6), 0).astype(F32).astype(BF16)
    fine = jnp.where(cell, value & 63, 0).astype(F32).astype(BF16)
    holders = iota((RING, ROWS), 0)
    high = jnp.zeros((RING, HEAD), F32)
    low = jnp.zeros((RING, HEAD), F32)
    count = jnp.zeros((RING, ROWS), F32)
    for t in range(STEPS):
        part = slice(t * ROWS, (t + 1) * ROWS)
        mine = jnp.where(owner_of(rows[t]) == holders, new_rows[t], 0).astype(F32)
        count = count + mine
        mine = mine.astype(BF16)
        high = high + dot(mine, coarse[part])
        low = low + dot(mine, fine[part])
    asked = high.astype(jnp.int32) * 64 + low.astype(jnp.int32) - 1

    prompt = prompt_ref[...]
    prompt_column = column_of(prompt)
    holder = lax.shift_right_logical(prompt, 1)
    holder_column = lax.shift_right_logical(prompt_column, 1)
    down = iota((ROWS, ROWS), 0)
    over = iota((ROWS, ROWS), 1)
    same = holder == holder_column
    turn = jnp.sum((same & (down < over)).astype(jnp.int32), axis=0, keepdims=True)
    turn_column = jnp.sum((same & (over < down)).astype(jnp.int32), axis=1, keepdims=True)
    mine = (holder == holders).astype(F32).astype(BF16)
    odd = jnp.where(turn_column + ROOM == iota((ROWS, HEAD), 1), prompt_column & 1, 0)
    odds = dot(mine, odd.astype(F32).astype(BF16)).astype(jnp.int32)
    lane = iota((RING, HEAD), 1)
    notes = jnp.where(lane < ROOM, asked, odds)
    most = jnp.max(rank, axis=0, keepdims=True) + 1
    notes = jnp.where(lane == ENDS, most, notes)
    most = jnp.max(turn_column, axis=0, keepdims=True) + 1
    notes = jnp.where(lane == ENDS + 1, most, notes)
    count = jnp.sum(count, axis=1, keepdims=True).astype(jnp.int32)
    notes = jnp.where(lane == ENDS + 2, count, notes)
    counts = jnp.where(lane == iota((RING, HEAD), 0) + COUNTS, count, 0)
    counts = jnp.sum(counts, axis=0, keepdims=True)
    listed = (lane >= COUNTS) & (lane < COUNTS + RING)
    notes_ref[...] = jnp.where(listed, counts, notes)

    def slots(holder, turn):
        now = jnp.where(turn < SLOT, holder * SLOT + turn, -1)
        later = jnp.where(turn >= SLOT, holder * SLOT + turn - SLOT, -1)
        return now, later

    columns_ref[...] = jnp.concatenate(slots(holder_column, turn_column), axis=1)
    lines_ref[...] = jnp.concatenate(slots(holder, turn), axis=0)


LONG = 20_000_000_000
PIECE = 1024


def pick_kernel(counts_ref, notes_ref, table_ref, out_ref, rows_ref):
    vocab = table_ref.shape[1]
    lane = iota((8, HEAD), 1)
    ids = jnp.zeros((8, ALL), jnp.int32)
    start = 0
    starts = []
    for d in range(RING):
        starts.append(start)
        row = jnp.broadcast_to(notes_ref[d : d + 1, :], (8, HEAD))
        row = jnp.where(lane < ROOM, row + 1, 0)
        row = jnp.concatenate([row, jnp.zeros((8, ALL - HEAD), jnp.int32)], axis=1)
        ids = ids + (pltpu.roll(row, start & (ALL - 1), 1) if d else row)
        start = jnp.minimum(start + counts_ref[d, ENDS + 2], ALL)
    ids = ids[0:1] - 1
    count = ALL
    step = 256
    lines = iota((step, count), 0).astype(F32).astype(BF16)

    def picked(start, rows):
        size = rows.shape[1]
        hots = []
        for at in range(start, start + size, step):
            here = (ids >= at) & (ids < at + step)
            near = jnp.where(here, ids - at, -1).astype(F32).astype(BF16)
            some = lines[: min(step, start + size - at)]
            hots.append(jnp.where(some == near, jnp.ones((), BF16), jnp.zeros((), BF16)))
        return dot(rows, jnp.concatenate(hots, axis=0) if len(hots) > 1 else hots[0])

    total = jnp.zeros((SHARE, count), F32)
    for start in range(0, vocab, PIECE):
        total = total + picked(start, table_ref[:, start : min(start + PIECE, vocab)])
    rows_ref[:ALL, :] = total.T
    rows_ref[ALL:, :] = jnp.zeros((ROOM, SHARE), F32)
    for d in range(RING):
        if d:
            whole_start = pl.multiple_of(starts[d] - (starts[d] & 7), 8)
            some = rows_ref[pl.ds(whole_start, ROOM), :]
            some = pltpu.roll(some, (ROOM - (starts[d] & 7)) & (ROOM - 1), 0)
        else:
            some = rows_ref[:ROOM, :]
        out_ref[d] = some[:TAKE].astype(BF16)


def pack(rows, packed_ref):
    low = rows[:, :HEAD].astype(BF16)
    high = rows[:, HEAD : 2 * HEAD].astype(BF16)
    tail = jnp.concatenate([rows[:, 2 * HEAD :], jnp.zeros((TOKENS, HEAD - TAIL), F32)], axis=1)
    mixed = tail[:ROWS]
    for t in range(1, STEPS):
        mixed = mixed + pltpu.roll(tail[t * ROWS : (t + 1) * ROWS], TAIL * t, 1)
    mixed = mixed.astype(BF16)
    for b in range(RING):
        packed_ref[b, :TOKENS, :] = low
        packed_ref[b, TOKENS : 2 * TOKENS, :] = high
        packed_ref[b, 2 * TOKENS :, :] = mixed


def unpack_kernel(at_ref, got_ref, out_ref, packed_ref):
    hot = (at_ref[...] == iota((TOKENS, RING * TAKE), 1)).astype(F32).astype(BF16)
    rows = dot(hot, got_ref[...])
    out_ref[...] = rows.astype(BF16)
    pack(rows, packed_ref)


def normed_times(all_ref, gain_ref, weights):
    group = lane_group((ROWS, HEAD))
    squares = jnp.zeros((TOKENS, HEAD), F32)
    tail_squares = jnp.zeros((ROWS, HEAD), F32)
    product = jnp.zeros((TOKENS, 2 * HEAD), F32)
    tail_blocks, tail_weights = [], []
    for b in range(RING):
        low = all_ref[b, :TOKENS, :].astype(F32)
        high = all_ref[b, TOKENS : 2 * TOKENS, :].astype(F32)
        tail = all_ref[b, 2 * TOKENS :, :].astype(F32)
        main_weights, more_weights = weights(b)
        squares = squares + (low * low + high * high)
        tail_squares = tail_squares + tail * tail
        both = jnp.concatenate(
            [
                (low * gain_ref[0, b : b + 1, :]).astype(BF16),
                (high * gain_ref[1, b : b + 1, :]).astype(BF16),
            ],
            axis=1,
        )
        product = product + dot(both, main_weights)
        tail_weights.append(more_weights)
        scaled = tail * gain_ref[2, b : b + 1, :]
        place = b % 4
        if place == 0:
            tail_blocks.append([jnp.zeros((ROWS, HEAD), F32) for _ in range(STEPS)])
        for t in range(STEPS):
            shift = (TAIL * (place - t)) % HEAD
            moved = pltpu.roll(scaled, shift, 1) if shift else scaled
            tail_blocks[-1][t] = jnp.where(group == place, moved, tail_blocks[-1][t])
    tails = jnp.concatenate(
        [jnp.concatenate(block, axis=0).astype(BF16) for block in tail_blocks], axis=1
    )
    product = product + dot(tails, jnp.concatenate(tail_weights, axis=0))
    total = jnp.sum(squares, axis=1, keepdims=True) + jnp.concatenate(
        [
            jnp.sum(jnp.where(group == t, tail_squares, 0.0), axis=1, keepdims=True)
            for t in range(STEPS)
        ],
        axis=0,
    )
    return product * lax.rsqrt(total * (1.0 / D) + EPSILON)


def rotary(u, cos_ref, sin_ref):
    return u * cos_ref[...] + pltpu.roll(u, HEAD // 2, 1) * sin_ref[...]


def query_kernel(all_ref, gain_ref, cos_ref, sin_ref, slot_ref, wq_ref, q_ref, send_ref):
    def weights(b):
        start = b * SHARE
        return wq_ref[start : start + 2 * HEAD, :], wq_ref[start + 2 * HEAD : start + SHARE, :]

    query = normed_times(all_ref, gain_ref, weights)
    turned = jnp.concatenate(
        [
            rotary(query[:, :HEAD], cos_ref, sin_ref).astype(BF16),
            rotary(query[:, HEAD:], cos_ref, sin_ref).astype(BF16),
        ],
        axis=1,
    )
    q_ref[...] = turned
    wide = jnp.concatenate([turned[t * ROWS : (t + 1) * ROWS] for t in range(STEPS)], axis=1)
    hot = (iota((RING * SLOT, ROWS), 0) == slot_ref[0:1, :]).astype(F32).astype(BF16)
    send_ref[...] = dot(hot, wide).astype(BF16)


def place_kernel(q_ref, slot_ref, send_ref):
    turned = q_ref[...]
    wide = jnp.concatenate([turned[t * ROWS : (t + 1) * ROWS] for t in range(STEPS)], axis=1)
    hot = (iota((RING * SLOT, ROWS), 0) == slot_ref[1:2, :]).astype(F32).astype(BF16)
    send_ref[...] = dot(hot, wide).astype(BF16)


def prefix_kernel(turn, own_ref, notes_ref, keys_ref, values_ref, out_ref):
    lanes = iota((RING, SLOT, HEAD), 2) - (ROOM + turn) == iota((RING, SLOT, HEAD), 1)
    notes = jnp.where(lanes, notes_ref[...][:, None, :], 0).reshape(RING * SLOT, HEAD)
    odd = jnp.sum(notes, axis=1, keepdims=True) == 1
    keys = jnp.concatenate([keys_ref[0], keys_ref[1]], axis=1)
    values = jnp.concatenate([values_ref[0], values_ref[1]], axis=1)
    slots = RING * SLOT
    lanes = iota((slots, HEAD), 1)
    denoms = jnp.zeros((slots, HEAD), F32)
    batch = 8
    for first in range(0, PAIRS, batch):
        some = range(first, first + batch)
        parts = []
        for i in some:
            q = own_ref[:, i * HEAD : (i + 1) * HEAD].astype(F32)
            parts.append(
                jnp.concatenate(
                    [jnp.where(odd, 0.0, q).astype(BF16), jnp.where(odd, q, 0.0).astype(BF16)],
                    axis=1,
                )
            )
        scores = dot(jnp.concatenate(parts, axis=0), keys, ((1,), (1,)))
        weights = capped_exp(scores).astype(BF16)
        numer = dot(weights, values)
        denom = jnp.sum(weights.astype(F32), axis=1, keepdims=True)
        for n, i in enumerate(some):
            part = numer[n * slots : (n + 1) * slots]
            out_ref[:, i * HEAD : (i + 1) * HEAD] = jnp.where(
                odd, part[:, HEAD:], part[:, :HEAD]
            ).astype(BF16)
            denoms = jnp.where(lanes == i, denom[n * slots : (n + 1) * slots], denoms)
    out_ref[:, WIDE:] = denoms.astype(BF16)


def local_kernel(
    all_ref, gain_ref, cos_ref, sin_ref, wkv_ref, q_ref, sk_ref, sv_ref, len_ref, out_ref
):
    def weights(b):
        start = b * SHARE
        return [
            jnp.concatenate([wkv_ref[0, rows, :], wkv_ref[1, rows, :]], axis=1)
            for rows in (
                slice(start, start + 2 * HEAD),
                slice(start + 2 * HEAD, start + SHARE),
            )
        ]

    keyval = normed_times(all_ref, gain_ref, weights)
    new_keys = rotary(keyval[:, :HEAD], cos_ref, sin_ref).astype(BF16)
    new_values = keyval[:, HEAD:].astype(BF16)
    suffix = ROWS * SUF
    keys = jnp.concatenate([sk_ref[...], new_keys], axis=0)
    values = jnp.concatenate([sv_ref[...], new_values], axis=0)
    columns = suffix + TOKENS
    column = iota((ROWS, columns), 1)
    row = iota((ROWS, columns), 0)
    first = row * SUF
    in_suffix = (column >= first) & (column < first + len_ref[...])
    lanes = iota((ROWS, HEAD), 1)
    denoms = jnp.zeros((ROWS, HEAD), F32)
    usable = in_suffix
    for t in range(STEPS):
        usable = usable | (column == row + (suffix + t * ROWS))
        for g in range(GROUP):
            i = t * GROUP + g
            q = q_ref[t * ROWS : (t + 1) * ROWS, g * HEAD : (g + 1) * HEAD]
            scores = dot(q, keys, ((1,), (1,)))
            weights = jnp.where(usable, capped_exp(scores), 0.0).astype(BF16)
            out_ref[:, i * HEAD : (i + 1) * HEAD] = dot(weights, values)
            denom = jnp.sum(weights.astype(F32), axis=1, keepdims=True)
            denoms = jnp.where(lanes == i, denom, denoms)
    out_ref[:, WIDE:] = denoms


def select_kernel(slot_ref, back_ref, local_ref, out_ref):
    hot = (slot_ref[:, 1:2] == iota((ROWS, RING * SLOT), 1)).astype(F32).astype(BF16)
    out_ref[...] = dot(hot, back_ref[...]) + local_ref[...]


def output_kernel(slot_ref, back_ref, local_ref, w_ref, out_ref):
    hot = (slot_ref[:, 0:1] == iota((ROWS, RING * SLOT), 1)).astype(F32).astype(BF16)
    total = dot(hot, back_ref[...]) + local_ref[...]
    rows = []
    for t in range(STEPS):
        heads = []
        for g in range(GROUP):
            i = t * GROUP + g
            heads.append(
                (
                    total[:, i * HEAD : (i + 1) * HEAD] / total[:, WIDE + i : WIDE + i + 1]
                ).astype(BF16)
            )
        rows.append(jnp.concatenate(heads, axis=1))
    attended = jnp.concatenate(rows, axis=0)
    lanes = iota((TOKENS, HEAD), 1)
    group = lane_group((ROWS, HEAD))
    quad = 4 * SHARE
    for first in range(0, RING, 4):
        part = dot(attended, w_ref[:, first * SHARE : first * SHARE + quad])
        for i in range(4):
            b = first + i
            tiles = [part[:, (2 * i + n) * HEAD : (2 * i + n + 1) * HEAD] for n in range(3)]
            away = TAIL * i
            if away:
                moved = [pltpu.roll(tile, HEAD - away, 1) for tile in tiles]
                low = jnp.where(lanes < HEAD - away, moved[0], moved[1])
                high = jnp.where(lanes < HEAD - away, moved[1], moved[2])
            else:
                low, high = tiles[0], tiles[1]
            out_ref[b, :TOKENS, :] = low.astype(BF16)
            out_ref[b, TOKENS : 2 * TOKENS, :] = high.astype(BF16)
            mixed = jnp.zeros((ROWS, HEAD), F32)
            for t in range(STEPS):
                tail = tiles[2][t * ROWS : (t + 1) * ROWS]
                shift = (TAIL * (t - i)) % HEAD
                tail = pltpu.roll(tail, shift, 1) if shift else tail
                mixed = jnp.where(group == t, tail, mixed)
            out_ref[b, 2 * TOKENS :, :] = mixed.astype(BF16)


def reduce_kernel(parts_ref, sum_ref, squares_ref):
    total = parts_ref[0].astype(F32)
    for b in range(1, RING):
        total = total + parts_ref[b].astype(F32)
    sum_ref[...] = total
    low, high, tail = total[:TOKENS], total[TOKENS : 2 * TOKENS], total[2 * TOKENS :]
    group = lane_group((ROWS, HEAD))
    squares = jnp.sum(low * low + high * high, axis=1, keepdims=True) + jnp.concatenate(
        [
            jnp.sum(jnp.where(group == t, tail * tail, 0.0), axis=1, keepdims=True)
            for t in range(STEPS)
        ],
        axis=0,
    )
    diagonal = iota((HEAD, HEAD), 0) == iota((HEAD, HEAD), 1)
    one = jnp.sum(jnp.where(diagonal, squares[:HEAD], 0.0), axis=0, keepdims=True)
    rest = TOKENS - HEAD
    two = jnp.sum(jnp.where(diagonal[:rest], squares[HEAD:], 0.0), axis=0, keepdims=True)
    line = jnp.concatenate([one, two], axis=0)
    for b in range(RING):
        squares_ref[b] = line


def scale_kernel(sum_ref, gain_ref, rows_ref, out_ref, wide_ref):
    total = sum_ref[...]
    tails = []
    for t in range(STEPS):
        tail = total[2 * TOKENS :]
        tails.append(pltpu.roll(tail, HEAD - TAIL * t, 1) if t else tail)
    tail = jnp.concatenate(tails, axis=0)[:, :TAIL]
    placed = jnp.concatenate([total[:TOKENS], total[TOKENS : 2 * TOKENS], tail], axis=1)
    out_ref[...] = placed * gain_ref[...]
    wide_ref[...] = rows_ref[...].astype(F32)


def finish_kernel(squares_ref, scaled_ref, wide_ref, out_ref):
    line = squares_ref[0]
    for b in range(1, RING):
        line = line + squares_ref[b]
    line = lax.rsqrt(line * (1.0 / D) + EPSILON)
    diagonal = iota((HEAD, HEAD), 0) == iota((HEAD, HEAD), 1)
    rest = TOKENS - HEAD
    one = jnp.sum(jnp.where(diagonal, line[0:1], 0.0), axis=1, keepdims=True)
    two = jnp.sum(jnp.where(diagonal[:rest], line[1:2], 0.0), axis=1, keepdims=True)
    root = jnp.concatenate([one, two], axis=0)
    out_ref[...] = (wide_ref[...] + scaled_ref[...] * root).astype(BF16)


def exchange(x, axis):
    return lax.all_to_all(x, axis, split_axis=0, concat_axis=0, tiled=True)


def per_device(
    token_ids,
    prompt_of,
    suffix_len,
    table,
    pre_gain,
    w_query,
    w_keyval,
    w_out,
    post_gain,
    prefix_keys,
    prefix_values,
    suffix_keys,
    suffix_values,
):
    vocab = table.shape[0]
    prompt_len = prefix_keys.shape[1]
    shape = jax.ShapeDtypeStruct

    notes, at, slot_columns, slot_lines = call(
        functools.partial(ask_kernel, vocab),
        [
            shape((RING, HEAD), jnp.int32),
            shape((TOKENS, 1), jnp.int32),
            shape((ROWS, 2), jnp.int32),
            shape((2, ROWS), jnp.int32),
        ],
        (token_ids, prompt_of.reshape(1, ROWS)),
        flops=LONG,
    )
    notes = exchange(notes.reshape(RING, 1, HEAD), "prefix").reshape(RING, HEAD)
    ends = jnp.max(notes[:, ENDS : ENDS + 2], axis=0)
    asked = jnp.max(jnp.sum(notes[:, COUNTS : COUNTS + RING], axis=0))
    crowded = (ends[0] > TAKE) | (asked > ALL)

    half = HEAD // 2
    frequency = 10000.0 ** (-(jnp.arange(half, dtype=F32) * 2.0 / HEAD))
    positions = (prompt_len + suffix_len[None, :] + jnp.arange(STEPS)[:, None]).astype(F32)
    angles = positions.reshape(TOKENS, 1) * frequency
    cosines = jnp.cos(angles)
    sines = jnp.sin(angles)
    cosines = jnp.concatenate([cosines, cosines], axis=1)
    sines = jnp.concatenate([-sines, sines], axis=1)
    gains = pre_gain.reshape(RING, SHARE)
    gains = jnp.stack(
        [gains[:, :HEAD], gains[:, HEAD : 2 * HEAD], jnp.tile(gains[:, 2 * HEAD :], (1, 4))]
    )
    notes, cosines, sines, gains = lax.optimization_barrier((notes, cosines, sines, gains))
    picked = call(
        pick_kernel,
        shape((RING, TAKE, SHARE), BF16),
        (notes, notes, table.T),
        flops=LONG,
        scalars=1,
        scratch=(pltpu.VMEM((ALL + ROOM, SHARE), F32),),
    )
    got = exchange(picked, "prefix").reshape(RING * TAKE, SHARE)

    def take_all(_):
        everyone = exchange(jnp.broadcast_to(token_ids, (RING, STEPS, ROWS)), "prefix")
        inside_at = everyone - lax.axis_index("prefix") * vocab
        inside = (inside_at >= 0) & (inside_at < vocab)
        rows = jnp.take(table, jnp.clip(inside_at, 0, vocab - 1), axis=0)
        rows = jnp.where(inside[..., None], rows, jnp.zeros_like(rows))
        rows = exchange(rows, "prefix").astype(F32).sum(axis=0).astype(BF16)
        rows = jnp.pad(rows.reshape(TOKENS, SHARE), ((0, RING * TAKE - TOKENS), (0, 0)))
        return jnp.arange(TOKENS, dtype=jnp.int32).reshape(TOKENS, 1), rows

    at, got = lax.cond(crowded, take_all, lambda found: found, (at, got))
    embedded, packed = call(
        unpack_kernel,
        [shape((TOKENS, SHARE), BF16), shape((RING, PACKED, HEAD), BF16)],
        (at, got),
        flops=LONG,
    )
    everywhere = exchange(packed, "branch")

    queries, sent = call(
        query_kernel,
        [shape((TOKENS, GROUP * HEAD), BF16), shape((RING * SLOT, WIDE), BF16)],
        (everywhere, gains, cosines, sines, slot_lines, w_query),
        flops=LONG,
    )

    queries, lengths, ends = lax.optimization_barrier((queries, suffix_len, ends))

    def ask(sent):
        return exchange(sent.reshape(RING, SLOT, WIDE), "prefix").reshape(RING * SLOT, WIDE)

    def answer(own, turn):
        sums = call(
            functools.partial(prefix_kernel, turn),
            shape((RING * SLOT, BACK), BF16),
            (own, notes, prefix_keys, prefix_values),
            flops=8 * RING * SLOT * prompt_len * WIDE,
        )
        return exchange(sums.reshape(RING, SLOT, BACK), "prefix").reshape(RING * SLOT, BACK)

    own = ask(sent)
    local = call(
        local_kernel,
        shape((ROWS, BACK), F32),
        (
            everywhere,
            gains,
            cosines,
            sines,
            w_keyval,
            queries,
            suffix_keys.reshape(ROWS * SUF, HEAD),
            suffix_values.reshape(ROWS * SUF, HEAD),
            lengths.reshape(ROWS, 1),
        ),
        flops=LONG,
    )
    own, local = lax.optimization_barrier((own, local))

    def second_round(local):
        sent = call(
            place_kernel,
            shape((RING * SLOT, WIDE), BF16),
            (queries, slot_lines),
        )
        back = answer(ask(sent), SLOT)
        return call(
            select_kernel,
            shape((ROWS, BACK), F32),
            (slot_columns, back, local),
        )

    local = lax.cond(ends[1] > SLOT, second_round, lambda local: local, local)
    own, local = lax.optimization_barrier((own, local))
    back = answer(own, 0)

    shares = call(
        output_kernel,
        shape((RING, PACKED, HEAD), BF16),
        (slot_columns, back, local, w_out),
        flops=2 * TOKENS * GROUP * HEAD * D,
    )
    shares = exchange(shares, "branch")
    total, squares = call(
        reduce_kernel,
        [shape((PACKED, HEAD), F32), shape((RING, 2, HEAD), F32)],
        (shares,),
    )
    squares = exchange(squares, "branch")
    scaled, wide = call(
        scale_kernel,
        [shape((TOKENS, SHARE), F32)] * 2,
        (total, post_gain.reshape(1, SHARE), embedded),
    )
    layer_out = call(
        finish_kernel,
        shape((TOKENS, SHARE), BF16),
        (squares, scaled, wide),
    )
    return layer_out.reshape(STEPS, ROWS, SHARE)


def solution(mesh):
    placed = (
        P(None, "prefix"),
        P("prefix", None),
        P("prefix"),
        P("prefix", "branch"),
        P(),
        P(None, "branch"),
        P(None, None, "branch"),
        P("branch", None),
        P("branch"),
        P("prefix", None, "branch"),
        P("prefix", None, "branch"),
        P("prefix", None, "branch"),
        P("prefix", None, "branch"),
    )
    return jax.shard_map(
        per_device,
        mesh=mesh,
        in_specs=placed,
        out_specs=P(None, "prefix", "branch"),
        check_vma=False,
    )
```
